256 devices in a mesh: head: 8 (over x, core), expert: 32 (over z, y).
Axes of the slice: x: 4, y: 4, z: 8, core: 2. Of those that a mesh axis runs over, the one named last changes fastest.
Arguments:
- queries: bfloat16 [512, 128, 576], P('expert', 'head'), may hold values from -64 to 64
- resident_cache: bfloat16 [128, 256, 576], P('expert'), may hold values from -6 to 6
- resident_len: int32 [128], P('expert'), may hold values from 1 to 256, as said below
- new_cache: bfloat16 [384, 64, 576], P('expert'), may hold values from -6 to 6
- new_len: int32 [384], replicated, may hold values from 1 to 64, as said below
- new_owner: int32 [384], replicated, may hold values from 0 to 31, as said below
- value_up: bfloat16 [128, 512, 128], P('head'), may hold values from -0.25 to 0.25
- w_output: bfloat16 [16384, 7168], P('head', 'expert'), may hold values from -0.046875 to 0.046875
- residual: bfloat16 [512, 7168], P(None, 'expert'), may hold values from -6 to 6
- expert_ids: int32 [512, 8], replicated, may hold values from 0 to 31, all different within a row; in each aligned block of 16 rows (0 to 15, 16 to 31, ...) at most 6 rows name the same one
- expert_gates: float32 [512, 8], replicated, may hold values from 0.1 to 1
- norm_gain: bfloat16 [7168], replicated, may hold values from 0.5 to 1.5
- w_gate: bfloat16 [32, 7168, 1024], P('expert', None, 'head'), may hold values from -0.0625 to 0.0625
- w_up: bfloat16 [32, 7168, 1024], P('expert', None, 'head'), may hold values from -0.0625 to 0.0625
- w_down: bfloat16 [32, 1024, 7168], P('expert', 'head'), may hold values from -0.1875 to 0.1875
Outputs:
- layer_out: bfloat16 [512, 7168], P('head', 'expert')
The draws below stay inside these ranges and needn't reach their ends.
Inputs may be any that keep to these rules, and one draw needn't show every extreme that they name: `resident_len`: every decode owner has a resident request of length 256. `new_len`: every prefill device holds a new request of length 64. `new_owner`: one prefill device sends at most 2 of its 12 new requests to one decode owner, and every decode owner receives exactly 12 in all; a prefill device sends either 2 or none to each owner, except to at most one owner, which gets the remainder of 12 divided by 2. `expert_ids`: in each aligned block of 16 rows (the rows of one decode owner) no expert is named by more than 6 rows; the 8 experts of a row differ.
All inputs are finite; a program needn't handle non-finite values.
Results may differ from the reference program's by a relative error of at most 0.012.
Values may be sent and summed in bfloat16 or wider, within the bound.
No kernel may reach another device: no remote copies, remote signals or barrier semaphores. Data moves between devices by JAX's collectives and lax.ppermute only.
A program may use at most 128 MiB of HBM per device.

```python
import math
import jax
import jax.numpy as jnp
import numpy as np
from jax import lax

D = 7168
H = 128
LAT = 512
ROPE = 64
NOPE = 128
VDIM = 128
EFF = 1024
TOPK = 8
REQ_DEV = 4
CTX = 256
NEW_DEV = 12
NEWLEN = 64
EXPERTS = 32
ROWS_DEV = 16
ROWS = 512
REQS = 128
NEWS = 384
MOST = 2
CAP = 6
N_EXPERT = 32


def draw_queries(key, part):
    values = jax.random.normal(key, (ROWS, H, LAT + ROPE), jnp.float32)
    return jnp.clip(values, -64.0, 64.0).astype(jnp.bfloat16)


def draw_resident_len(key, part):
    base = jax.random.randint(key, (N_EXPERT, REQ_DEV), 1, CTX + 1)
    chosen = jax.random.randint(jax.random.fold_in(key, 3), (N_EXPERT, 1), 0, REQ_DEV)
    longest = jnp.arange(REQ_DEV)[None, :] == chosen
    return jnp.where(longest, CTX, base).reshape(REQS).astype(jnp.int32)


def draw_new_len(key, part):
    base = jax.random.randint(key, (N_EXPERT, NEW_DEV), 1, NEWLEN + 1)
    chosen = jax.random.randint(jax.random.fold_in(key, 5), (N_EXPERT, 1), 0, NEW_DEV)
    longest = jnp.arange(NEW_DEV)[None, :] == chosen
    return jnp.where(longest, NEWLEN, base).reshape(NEWS).astype(jnp.int32)


def draw_new_owner(key, part):
    spread = jax.random.permutation(jax.random.fold_in(key, 11), N_EXPERT)
    shifted = jax.random.permutation(jax.random.fold_in(key, 12), N_EXPERT)
    offsets = jax.random.permutation(jax.random.fold_in(key, 13), N_EXPERT)
    labels = jax.vmap(lambda one: jax.random.permutation(one, NEW_DEV))(jax.random.split(jax.random.fold_in(key, 14), N_EXPERT))
    groups = labels // MOST
    target = (shifted[:, None] + offsets[groups]) % N_EXPERT
    return spread[target].reshape(NEWS).astype(jnp.int32)


def level_of(own_key, shape, pieces, least, top_value):
    def one(position, shards_of):
        steps = jax.random.uniform(jax.random.fold_in(jax.random.fold_in(own_key, 6), position), (shards_of,), jnp.float32, least / len(pieces), top_value / len(pieces))
        return jnp.repeat(jnp.exp(steps), shape[position] // shards_of).reshape((-1,) + (1,) * (len(shape) - position - 1))

    level = one(*pieces[0])
    for cut in pieces[1:]:
        level = level * one(*cut)
    return level


def shared_out(own_key, own, number, rows, amount, top, limit, slope):
    order = jax.random.permutation(own_key, amount)
    crowded, usual = shares(amount, rows * top, limit, slope, True), shares(amount, rows * top, limit, slope, False)
    places = jnp.arange(amount)

    def named(lengths, offset_by):
        used = int((lengths > 0).sum())
        fixed = max(1, used // 4)
        moved = fixed + (places - fixed + offset_by * (used - fixed)) % max(1, amount - fixed)
        return jnp.zeros((amount,), jnp.int32).at[order[jnp.where(places < fixed, places, moved)]].set(jnp.asarray(lengths, jnp.int32))

    lengths = jnp.where(number % 4 == 0, named(crowded, number // 4), named(usual, number - number // 4 - 1))
    mixed = jax.random.permutation(jax.random.fold_in(own, 3), amount)
    source_of, receiver = mixed[0:amount // 2 * 2:2], mixed[1:amount // 2 * 2:2]
    margin = jnp.minimum(lengths[source_of] - 1, limit - lengths[receiver]) // 2
    margin = jnp.where((source_of == order[0]) | (receiver == order[0]) | (lengths[receiver] == 0), 0, jnp.maximum(margin, 0))
    moved = jax.random.randint(jax.random.fold_in(own, 4), (amount // 2,), 0, 1 << 20) % (margin + 1)
    lengths = lengths.at[source_of].add(-moved).at[receiver].add(moved)
    members = jnp.searchsorted(jnp.cumsum(lengths), jnp.arange(rows * top), side="right").astype(jnp.int32)
    grid = members.reshape(top, rows).T
    grid = grid[jax.random.permutation(jax.random.fold_in(own, 1), rows)]
    offset_by = jax.random.randint(jax.random.fold_in(own, 2), (rows, 1), 0, top)
    return jnp.take_along_axis(grid, (jnp.arange(top)[None, :] + offset_by) % top, axis=1)


def shares(amount, total, reach, slope, full):
    portions = [(1 << 20) // math.isqrt(grade ** slope) + 1 for grade in range(1, amount + 1)]
    largest = reach if full else min(reach, max(-(-total // amount), total * portions[0] // sum(portions)))
    least = 1 if total - largest >= amount - 1 else 0
    holding, rest = [largest] + [least] * (amount - 1), total - largest - least * (amount - 1)
    while rest > 0:
        candidates = [i for i in range(1, amount) if holding[i] < largest] or [i for i in range(1, amount) if holding[i] < reach]
        whole, left = sum([portions[i] for i in candidates]), rest
        for i in candidates:
            addition = min(reach - holding[i], max(1, left * portions[i] // whole), rest)
            holding[i] = holding[i] + addition
            rest = rest - addition
    return np.array(holding)


def noise(key, dims, width, limit, shards=(), kind=jnp.bfloat16):
    entries = width * jax.random.normal(key, dims, jnp.float32)
    if shards:
        entries = entries * level_of(key, dims, shards, -0.22, 0.18)
    return jnp.clip(entries, -limit, limit).astype(kind)


def setup_inputs(seed: int = 0) -> dict:
    key_list = jax.random.split(jax.random.key(seed), 16)
    queries = draw_queries(jax.random.fold_in(key_list[15], 71), 0)
    resident_cache = noise(key_list[1], (REQS, CTX, LAT + ROPE), 1.0, 6.0, ((0, 32),))
    resident_len = draw_resident_len(jax.random.fold_in(key_list[15], 71), 0)
    new_cache = noise(key_list[3], (NEWS, NEWLEN, LAT + ROPE), 1.0, 6.0, ((0, 32),))
    new_len = draw_new_len(jax.random.fold_in(key_list[15], 71), 0)
    new_owner = draw_new_owner(jax.random.fold_in(key_list[15], 71), 0)
    value_up = noise(key_list[6], (H, LAT, VDIM), LAT ** -0.5, 0.25, ((0, 8),))
    w_output = noise(key_list[7], (H * VDIM, D), (H * VDIM) ** -0.5, 0.046875, ((0, 8), (1, 32)))
    residual = noise(key_list[8], (ROWS, D), 1.0, 6.0, ((1, 32),))
    expert_ids_keys = jax.random.split(jax.random.fold_in(key_list[9], 1), ROWS // ROWS_DEV)
    expert_ids_turns = jax.random.permutation(jax.random.fold_in(key_list[9], 3), ROWS // ROWS_DEV)
    expert_ids = jax.vmap(lambda own, number: shared_out(jax.random.fold_in(key_list[9], 2), own, number, ROWS_DEV, EXPERTS, TOPK, CAP, 2))(expert_ids_keys, expert_ids_turns).reshape((ROWS, TOPK))
    expert_gates = jnp.clip(jnp.exp(jax.random.uniform(key_list[10], (ROWS, TOPK), jnp.float32, math.log(0.1), math.log(1.0))), 0.1, 1.0)
    norm_gain = jnp.clip(1.0 + 0.1 * jax.random.normal(key_list[11], (D,), jnp.float32), 0.5, 1.5).astype(jnp.bfloat16)
    w_gate = noise(key_list[12], (EXPERTS, D, EFF), D ** -0.5, 0.0625, ((0, 32), (2, 8)))
    w_up = noise(key_list[13], (EXPERTS, D, EFF), D ** -0.5, 0.0625, ((0, 32), (2, 8)))
    w_down = noise(key_list[14], (EXPERTS, EFF, D), EFF ** -0.5, 0.1875, ((0, 32), (1, 8)))
    return {"queries": queries, "resident_cache": resident_cache, "resident_len": resident_len, "new_cache": new_cache, "new_len": new_len, "new_owner": new_owner, "value_up": value_up, "w_output": w_output, "residual": residual, "expert_ids": expert_ids, "expert_gates": expert_gates, "norm_gain": norm_gain, "w_gate": w_gate, "w_up": w_up, "w_down": w_down}


def attend(queries, caches, length, value_up):
    inverse_root = (NOPE + ROPE) ** (-0.5)
    scores = jnp.einsum('rhc,rtc->rht', queries.astype(jnp.float32), caches.astype(jnp.float32)) * inverse_root
    inside = jnp.arange(caches.shape[1], dtype=jnp.int32)[None, None, :] < length[:, None, None]
    scores = jnp.where(inside, scores, -jnp.inf)
    highest = lax.optimization_barrier(jnp.max(scores, axis=2, keepdims=True))
    raised = jnp.exp(scores - highest)
    weights = (raised / lax.optimization_barrier(jnp.sum(raised, axis=2, keepdims=True))).astype(jnp.bfloat16)
    latent = jnp.einsum('rht,rtc->rhc', weights.astype(jnp.float32), caches[:, :, :LAT].astype(jnp.float32)).astype(jnp.bfloat16)
    values = jnp.einsum('rhc,hcv->rhv', latent.astype(jnp.float32), value_up.astype(jnp.float32)).astype(jnp.bfloat16)
    return values.reshape(values.shape[0], H * VDIM)

def reference(queries, resident_cache, resident_len, new_cache, new_len, new_owner, value_up, w_output, residual, expert_ids, expert_gates, norm_gain, w_gate, w_up, w_down):
    blocks = queries.reshape(N_EXPERT, ROWS_DEV, H, LAT + ROPE)
    ordering = jnp.argsort(new_owner, stable=True).astype(jnp.int32)
    resident_att = attend(blocks[:, :REQ_DEV].reshape(REQS, H, LAT + ROPE), resident_cache, resident_len, value_up)
    arrived_att = attend(blocks[:, REQ_DEV:].reshape(NEWS, H, LAT + ROPE), new_cache[ordering], new_len[ordering], value_up)
    attention = jnp.concatenate([resident_att.reshape(N_EXPERT, REQ_DEV, H * VDIM), arrived_att.reshape(N_EXPERT, NEW_DEV, H * VDIM)], axis=1).reshape(ROWS, H * VDIM)
    mixed = jnp.dot(attention, w_output, preferred_element_type=jnp.float32)
    hidden = (residual.astype(jnp.float32) + mixed).astype(jnp.bfloat16)
    picks = expert_ids.reshape(N_EXPERT, ROWS_DEV * TOPK)
    onehot = (picks[:, :, None] == jnp.arange(EXPERTS, dtype=jnp.int32)[None, None, :]).astype(jnp.int32)
    ranking = (lax.optimization_barrier(jnp.sum(jnp.cumsum(onehot, axis=1) * onehot, axis=2)) - 1).astype(jnp.int32)
    source = jnp.arange(N_EXPERT, dtype=jnp.int32)[:, None]
    slot_index = (picks * (N_EXPERT * CAP) + source * CAP + ranking).astype(jnp.int32)
    row_index = (source * ROWS_DEV + jnp.arange(ROWS_DEV * TOPK, dtype=jnp.int32)[None, :] // TOPK).astype(jnp.int32)
    slot_rows = jnp.full((EXPERTS * N_EXPERT * CAP,), ROWS, jnp.int32).at[slot_index.reshape(-1)].set(row_index.reshape(-1))
    padded = jnp.concatenate([hidden, jnp.zeros((1, D), jnp.bfloat16)], axis=0)
    inputs_all = padded[slot_rows].reshape(EXPERTS, N_EXPERT * CAP, D)

    def apply_expert(operands):
        inputs, gate_weight, up_weight, down_weight = operands
        values = inputs.astype(jnp.float32)
        inverse = lax.rsqrt(lax.optimization_barrier(jnp.mean(values * values, axis=1, keepdims=True)) + 1e-06)
        normed = (values * inverse * norm_gain.astype(jnp.float32)).astype(jnp.bfloat16)
        gate_act = jnp.dot(normed, gate_weight, preferred_element_type=jnp.float32)
        up_act = jnp.dot(normed, up_weight, preferred_element_type=jnp.float32)
        hidden_act = (jax.nn.silu(gate_act) * up_act).astype(jnp.bfloat16)
        return jnp.dot(hidden_act, down_weight, preferred_element_type=jnp.float32)
    expert_out = lax.map(apply_expert, (inputs_all, w_gate, w_up, w_down))
    picked = expert_out.reshape(EXPERTS * N_EXPERT * CAP, D)[slot_index.reshape(ROWS, TOPK)]
    routed = lax.optimization_barrier(jnp.sum(picked * expert_gates[:, :, None], axis=1))
    return (hidden.astype(jnp.float32) + routed).astype(jnp.bfloat16)
```

```python
import functools

import jax
import jax.numpy as jnp
from jax import lax
from jax.experimental import pallas as pl
from jax.experimental.pallas import tpu as pltpu
from jax.sharding import Mesh
from jax.sharding import PartitionSpec as P

ROPE = 64
NOPE = 128
EXPERT = ("expert_0", "expert_1")
HEAD = ("head_0", "head_1")
MOST = 2
CAP = 6
BF = jnp.bfloat16
F32 = jnp.float32
I32 = jnp.int32
VMEM_BYTES = 48 * 1024 * 1024


def params():
    return pltpu.CompilerParams(vmem_limit_bytes=VMEM_BYTES)


def whole(memory=pltpu.VMEM):
    return pl.BlockSpec(memory_space=memory)


def shifted(x, axis, step):
    n = lax.axis_size(axis)
    return lax.ppermute(x, axis, [(i, (i + step) % n) for i in range(n)])


def ring_gather(x, axis):
    n = lax.axis_size(axis)
    far = n // 2
    cut = x.shape[0] // 2
    found = {0: x}
    right, left = x, x
    for step in range(1, far):
        right, left = shifted(right, axis, 1), shifted(left, axis, -1)
        found[step], found[n - step] = right, left
    found[far] = (shifted(right[:cut], axis, 1), shifted(left[cut:], axis, -1))
    return [found[d] for d in range(n)]


def flat(pieces):
    out = []
    for piece in pieces:
        out.extend(piece if isinstance(piece, tuple) else (piece,))
    return out


def attend(queries, caches_t, length, value_up):
    inverse_root = (NOPE + ROPE) ** (-0.5)
    latent_width = value_up.shape[1]
    scores = jnp.einsum("rhc,rct->rht", queries, caches_t, preferred_element_type=F32) * inverse_root
    inside = lax.broadcasted_iota(I32, scores.shape, 2) < length[:, None, None]
    scores = jnp.where(inside, scores, -jnp.inf)
    highest = jnp.max(scores, axis=2, keepdims=True)
    raised = jnp.exp(scores - highest)
    weights = (raised / jnp.sum(raised, axis=2, keepdims=True)).astype(BF)
    latent = jnp.einsum("rht,rct->rhc", weights, caches_t[:, :latent_width], preferred_element_type=F32).astype(BF)
    values = jnp.einsum("rhc,hcv->rhv", latent, value_up, preferred_element_type=F32).astype(BF)
    return values.reshape(values.shape[0], -1)


def pack_kernel(first, slots, q_ref, out_ref, sems):
    count = sems.shape[0]
    copies = [
        pltpu.make_async_copy(q_ref.at[first + j], out_ref.at[slots[j]], sems.at[j]) for j in range(count)
    ]
    for copy in copies:
        copy.start()
    for copy in copies:
        copy.wait()


def pack_queries(queries, slots, first, slots_all):
    count = slots.shape[0]
    return pl.pallas_call(
        functools.partial(pack_kernel, first),
        out_shape=jax.ShapeDtypeStruct((slots_all,) + queries.shape[1:], queries.dtype),
        in_specs=[whole(pltpu.SMEM), whole(pl.ANY)],
        out_specs=whole(pl.ANY),
        scratch_shapes=[pltpu.SemaphoreType.DMA((count,))],
        compiler_params=params(),
        name="pack_queries",
    )(slots, queries)


def new_attention_kernel(slots, lens, q_ref, cache_ref, up_ref, res_ref, a_ref, b_ref, latents):
    count, span = cache_ref.shape[0], cache_ref.shape[1]
    heads, latent_width, value_width = up_ref.shape
    inverse_root = (NOPE + ROPE) ** (-0.5)
    for i in range(count):
        cache = cache_ref[i]
        scores = (
            lax.dot_general(q_ref[slots[i]], cache, (((1,), (1,)), ((), ())), preferred_element_type=F32)
            * inverse_root
        )
        inside = lax.broadcasted_iota(I32, (heads, span), 1) < lens[i]
        scores = jnp.where(inside, scores, -jnp.inf)
        raised = jnp.exp(scores - jnp.max(scores, axis=1, keepdims=True))
        weights = (raised / jnp.sum(raised, axis=1, keepdims=True)).astype(BF)
        latents[:, i, :] = jnp.dot(weights, cache[:, :latent_width], preferred_element_type=F32)
    half = heads // 2
    for h in range(heads):
        values = jnp.dot(latents[h, :, :].astype(BF), up_ref[h], preferred_element_type=F32)
        rows = jnp.concatenate(
            [values[:count], res_ref[:, h * value_width : (h + 1) * value_width].astype(F32)], axis=0
        ).astype(BF)
        target = a_ref if h < half else b_ref
        at = (h % half) * value_width
        target[:, at : at + value_width] = rows


def new_attention(slots, lens, arrived, cache, value_up, resident):
    count = cache.shape[0]
    heads, latent_width, value_width = value_up.shape
    rows = count + resident.shape[0]
    half = jax.ShapeDtypeStruct((rows, heads * value_width // 2), BF)
    return pl.pallas_call(
        new_attention_kernel,
        out_shape=(half, half),
        in_specs=[whole(pltpu.SMEM)] * 2 + [whole()] * 4,
        out_specs=(whole(), whole()),
        scratch_shapes=[pltpu.VMEM((heads, rows, latent_width), F32)],
        compiler_params=params(),
        name="new_attention",
    )(slots, lens, arrived, cache, value_up, resident)


def plan_kernel(rows_dev, ids_ref, gates_ref, sel_ref, mix_ref):
    rows, choose = ids_ref.shape
    slots_all = sel_ref.shape[1]
    slots = rows // rows_dev * CAP
    experts = slots_all // slots
    expert = lax.broadcasted_iota(I32, (rows, experts), 1)
    member = jnp.zeros((rows, experts), F32)
    gate = jnp.zeros((rows, experts), F32)
    for k in range(choose):
        same = ids_ref[:, k : k + 1] == expert
        member = jnp.where(same, 1.0, member)
        gate = jnp.where(same, gates_ref[:, k : k + 1], gate)
    to_row = lax.broadcasted_iota(I32, (rows, rows), 0)
    from_row = lax.broadcasted_iota(I32, (rows, rows), 1)
    before = (from_row < to_row) & (from_row // rows_dev == to_row // rows_dev)
    rank = jnp.dot(before.astype(F32).astype(BF), member.astype(BF), preferred_element_type=F32)
    block = lax.broadcasted_iota(I32, (rows, experts), 0) // rows_dev
    slot = jnp.where(member > 0, rank + (block * CAP).astype(F32), -1.0)
    spread = (
        lax.broadcasted_iota(I32, (experts, slots_all), 0)
        == lax.broadcasted_iota(I32, (experts, slots_all), 1) // slots
    ).astype(F32)
    slot_wide = jnp.dot(slot.astype(BF), spread.astype(BF), preferred_element_type=F32)
    gate_wide = jnp.dot(gate, spread, preferred_element_type=F32, precision=lax.Precision.HIGHEST)
    wanted = (lax.broadcasted_iota(I32, (rows, slots_all), 1) % slots).astype(F32)
    hit = slot_wide == wanted
    sel_ref[...] = jnp.where(hit, 1.0, 0.0).astype(BF)
    mix_ref[...] = jnp.where(hit, gate_wide, 0.0)


def plan(ids, gates, rows_dev, experts):
    rows = ids.shape[0]
    slots_all = experts * (rows // rows_dev) * CAP
    return pl.pallas_call(
        functools.partial(plan_kernel, rows_dev),
        out_shape=(
            jax.ShapeDtypeStruct((rows, slots_all), BF),
            jax.ShapeDtypeStruct((rows, slots_all), F32),
        ),
        in_specs=[whole()] * 2,
        out_specs=(whole(), whole()),
        compiler_params=params(),
        name="plan",
    )(ids, gates)


def dispatch_kernel(parts_ref, residual_ref, sel_ref, hidden_ref, out_ref):
    total = parts_ref[0].astype(F32)
    for k in range(1, parts_ref.shape[0]):
        total = total + parts_ref[k].astype(F32)
    hidden = (residual_ref[...].astype(F32) + total).astype(BF)
    hidden_ref[...] = hidden
    picked = lax.dot_general(sel_ref[...], hidden, (((0,), (0,)), ((), ())), preferred_element_type=F32)
    out_ref[...] = picked.reshape(out_ref.shape).astype(BF)


def dispatch(parts, residual, sel, experts):
    rows, columns = residual.shape
    return pl.pallas_call(
        dispatch_kernel,
        out_shape=(
            jax.ShapeDtypeStruct((rows, columns), BF),
            jax.ShapeDtypeStruct((experts, sel.shape[1] // experts, columns), BF),
        ),
        in_specs=[whole()] * 3,
        out_specs=(whole(), whole()),
        compiler_params=params(),
        name="dispatch",
    )(parts, residual, sel)


def norm_kernel(x_ref, gain_ref, out_ref):
    x = x_ref[...].astype(F32)
    width = x.shape[0] * x.shape[2]
    squares = jnp.sum(jnp.sum(x * x, axis=0), axis=1, keepdims=True)
    inverse = lax.rsqrt(squares / width + 1e-06)
    out_ref[...] = (x * inverse[None] * gain_ref[...].astype(F32)).astype(BF)


def normed_rows(x, gain):
    return pl.pallas_call(
        norm_kernel,
        out_shape=jax.ShapeDtypeStruct(x.shape, BF),
        in_specs=[whole()] * 2,
        out_specs=whole(),
        compiler_params=params(),
        name="norm",
    )(x, gain)


def experts_kernel(layout, *refs):
    count = sum(layout)
    x_refs, (gate_ref, up_ref, down_ref), outs = refs[:count], refs[count : count + 3], refs[count + 3 :]
    columns, slots = x_refs[0].shape[0], x_refs[0].shape[1]
    width = x_refs[0].shape[2]
    gate = up = None
    for j in range(columns):
        pieces, at = [], 0
        for parts in layout:
            split = columns // parts
            pieces.append(x_refs[at + j // split][j % split].astype(F32))
            at += parts
        x = jnp.concatenate(pieces, axis=0).astype(BF)
        g = jnp.dot(x, gate_ref[j], preferred_element_type=F32)
        u = jnp.dot(x, up_ref[j], preferred_element_type=F32)
        gate, up = (g, u) if gate is None else (gate + g, up + u)
    act = (gate * jax.nn.sigmoid(gate) * up).astype(BF)
    for j in range(columns):
        y = jnp.dot(act, down_ref[:, j * width : (j + 1) * width], preferred_element_type=F32)
        for k, out in enumerate(outs):
            out[j] = y[k * slots : (k + 1) * slots].astype(out.dtype)


def run_experts(layout, pieces, w_gate, w_up, w_down, types):
    shape = pieces[0].shape
    return pl.pallas_call(
        functools.partial(experts_kernel, layout),
        out_shape=tuple(jax.ShapeDtypeStruct(shape, kind) for kind in types),
        in_specs=[whole()] * (len(pieces) + 3),
        out_specs=tuple(whole() for _ in types),
        compiler_params=params(),
        name="experts",
    )(*pieces, w_gate, w_up, w_down)


def combine_kernel(back_ref, mix_ref, hidden_ref, out_ref):
    back = back_ref[...].astype(F32).reshape(-1, back_ref.shape[2])
    routed = jnp.dot(mix_ref[...], back, preferred_element_type=F32, precision=lax.Precision.HIGHEST)
    out_ref[...] = (hidden_ref[...].astype(F32) + routed).astype(BF)


def combine(back, mix, hidden):
    return pl.pallas_call(
        combine_kernel,
        out_shape=jax.ShapeDtypeStruct(hidden.shape, BF),
        in_specs=[whole()] * 3,
        out_specs=whole(),
        compiler_params=params(),
        name="combine",
    )(back, mix, hidden)


def exchange(x, axes):
    return lax.all_to_all(x, axes, split_axis=0, concat_axis=0, tiled=True)


def gather_over_head(x):
    near = ring_gather(x, HEAD[0])
    layout = [len(p) if isinstance(p, tuple) else 1 for p in near]
    near = flat(near)
    far = [shifted(p, HEAD[1], 1) for p in near]
    return layout * 2, near + far


def sum_over_head(kept, sent):
    other = [shifted(s, HEAD[1], 1) for s in (sent[2], sent[1], sent[3], sent[0])]
    other = [other[3], other[1], other[0], other[2]]
    pair = [k + o.astype(F32) for k, o in zip(kept, other)]
    cut = pair[2].shape[0] // 2
    far = pair[2].astype(BF)
    low = shifted(far[:cut], HEAD[0], -1).astype(F32)
    high = shifted(far[cut:], HEAD[0], 1).astype(F32)
    before = jnp.concatenate([pair[1][:cut] + low, pair[1][cut:]], axis=0).astype(BF)
    after = jnp.concatenate([pair[3][:cut], pair[3][cut:] + high], axis=0).astype(BF)
    from_after = shifted(before, HEAD[0], -1).astype(F32)
    from_before = shifted(after, HEAD[0], 1).astype(F32)
    return (pair[0] + from_after + from_before).astype(BF)


def per_device(
    queries,
    resident_cache,
    resident_len,
    new_cache,
    new_len,
    new_owner,
    value_up,
    w_output,
    residual,
    expert_ids,
    expert_gates,
    norm_gain,
    w_gate,
    w_up,
    w_down,
):
    n_expert = lax.axis_size(EXPERT)
    n_head = lax.axis_size(HEAD)
    n_z, n_y = lax.axis_size(EXPERT[0]), lax.axis_size(EXPERT[1])
    z, y = lax.axis_index(EXPERT[0]), lax.axis_index(EXPERT[1])
    me = lax.axis_index(EXPERT)
    head = lax.axis_index(HEAD)
    req_count = resident_cache.shape[0]
    new_count = new_cache.shape[0]
    rows_dev = req_count + new_count
    rows_all = rows_dev * n_expert
    block_rows = rows_all // n_head
    columns = residual.shape[1]
    news = new_owner.shape[0]

    number = jnp.arange(news, dtype=I32)
    equal = (new_owner[:, None] == new_owner[None, :]) & (number[None, :] < number[:, None])
    place = jnp.sum(equal.astype(I32), axis=1)
    nearby = equal & (number[None, :] // new_count == number[:, None] // new_count)
    turn = jnp.sum(nearby.astype(I32), axis=1)
    mine = (new_owner == me)[None, :] & (place[None, :] == jnp.arange(new_count, dtype=I32)[:, None])
    out_slots = jnp.sum(jnp.where(mine, ((number // new_count) * MOST + turn)[None, :], 0), axis=1)
    own = lambda a: lax.dynamic_slice_in_dim(a, me * new_count, new_count)
    in_slots = own(new_owner * MOST + turn)
    in_lens = own(new_len)
    new_rows = (new_owner * rows_dev + req_count + place).reshape(n_expert, new_count)
    old_rows = (jnp.arange(n_expert, dtype=I32) * rows_dev)[:, None] + jnp.arange(req_count, dtype=I32)[None, :]
    rows_of = jnp.concatenate([new_rows, old_rows], axis=1)
    away = jnp.arange(n_expert, dtype=I32)
    maker = ((z - away // n_y) % n_z) * n_y + (y - away % n_y) % n_y
    rows_here = jnp.sum(
        jnp.where(maker[:, None, None] == jnp.arange(n_expert, dtype=I32)[None, :, None], rows_of[None], 0), axis=1
    )

    packed = pack_queries(queries, out_slots, req_count, n_expert * MOST)
    arrived = exchange(packed.reshape((n_expert, MOST) + queries.shape[1:]), EXPERT)
    arrived = arrived.reshape((n_expert * MOST,) + queries.shape[1:])
    resident = attend(queries[:req_count], jnp.swapaxes(resident_cache, 1, 2), resident_len, value_up)
    first, second = new_attention(in_slots, in_lens, arrived, new_cache, value_up, resident)

    by_y = jnp.concatenate(flat(ring_gather(first, EXPERT[1])), axis=0)
    by_z = jnp.concatenate(flat(ring_gather(second, EXPERT[0])), axis=0)
    first_all = jnp.concatenate(flat(ring_gather(by_y, EXPERT[0])), axis=0)
    second_all = jnp.concatenate(
        flat(ring_gather(by_z, EXPERT[1])), axis=0
    )
    half = first.shape[1]
    in_order = (rows_here.reshape(1, rows_all) == jnp.arange(rows_all, dtype=I32)[:, None]).astype(BF)
    swapped = jnp.swapaxes(rows_here.reshape(n_z, n_y, rows_dev), 0, 1).reshape(1, rows_all)
    in_other = (swapped == jnp.arange(rows_all, dtype=I32)[:, None]).astype(BF)
    mixed_a = jnp.dot(first_all, w_output[:half], preferred_element_type=F32).astype(BF)
    mixed_b = jnp.dot(second_all, w_output[half:], preferred_element_type=F32).astype(BF)
    mixed = (
        jnp.dot(in_order, mixed_a, preferred_element_type=F32)
        + jnp.dot(in_other, mixed_b, preferred_element_type=F32)
    ).astype(BF)
    parts = exchange(mixed.reshape(n_head, block_rows, columns), HEAD)

    block = lambda a: lax.dynamic_slice_in_dim(a, head * block_rows, block_rows)
    sel, mix = plan(block(expert_ids), block(expert_gates), rows_dev, n_expert)
    hidden, outgoing = dispatch(parts, block(residual), sel, n_expert)
    received = exchange(outgoing, EXPERT)
    normed = normed_rows(received, norm_gain.reshape(n_expert, 1, columns))
    layout, pieces = gather_over_head(normed)
    x_count = lax.axis_size(HEAD[0])
    made = run_experts(
        tuple(layout),
        pieces,
        w_gate.reshape(n_expert, columns, -1),
        w_up.reshape(n_expert, columns, -1),
        w_down.reshape(w_down.shape[1:]),
        [F32] * x_count + [BF] * x_count,
    )
    summed = sum_over_head(made[:x_count], made[x_count:])
    back = exchange(summed, EXPERT)
    return combine(back, mix, hidden)


def solution(mesh):
    finer = Mesh(mesh.devices.reshape(4, 2, 8, 4), ("head_0", "head_1", "expert_0", "expert_1"))
    in_specs = (
        P(EXPERT, HEAD, None),
        P(EXPERT, None, None),
        P(EXPERT),
        P(EXPERT, None, None),
        P(),
        P(),
        P(HEAD, None, None),
        P(HEAD, EXPERT),
        P(None, EXPERT),
        P(),
        P(),
        P(),
        P(EXPERT, None, HEAD),
        P(EXPERT, None, HEAD),
        P(EXPERT, HEAD, None),
    )
    out_specs = P(HEAD, EXPERT)
    return jax.shard_map(
        per_device, mesh=finer, in_specs=in_specs, out_specs=out_specs, check_vma=False
    )
```

```python
import functools

import jax
import jax.numpy as jnp
from jax import lax
from jax.experimental import pallas as pl
from jax.experimental.pallas import tpu as pltpu
from jax.sharding import Mesh
from jax.sharding import PartitionSpec as P

ROPE = 64
NOPE = 128
EXPERT = ("expert_0", "expert_1")
HEAD = ("head_0", "head_1")
MOST = 2
CAP = 6
BF = jnp.bfloat16
F32 = jnp.float32
I32 = jnp.int32
VMEM_BYTES = 48 * 1024 * 1024


def params():
    return pltpu.CompilerParams(vmem_limit_bytes=VMEM_BYTES)


def whole(memory=pltpu.VMEM):
    return pl.BlockSpec(memory_space=memory)


def shifted(x, axis, step):
    n = lax.axis_size(axis)
    return lax.ppermute(x, axis, [(i, (i + step) % n) for i in range(n)])


def ring_gather(x, axis):
    n = lax.axis_size(axis)
    far = n // 2
    cut = x.shape[0] // 2
    found = {0: x}
    right, left = x, x
    for step in range(1, far):
        right, left = shifted(right, axis, 1), shifted(left, axis, -1)
        found[step], found[n - step] = right, left
    found[far] = (shifted(right[:cut], axis, 1), shifted(left[cut:], axis, -1))
    return [found[d] for d in range(n)]


def flat(pieces):
    out = []
    for piece in pieces:
        out.extend(piece if isinstance(piece, tuple) else (piece,))
    return out


def attend(queries, caches_t, length, value_up):
    inverse_root = (NOPE + ROPE) ** (-0.5)
    latent_width = value_up.shape[1]
    scores = jnp.einsum("rhc,rct->rht", queries, caches_t, preferred_element_type=F32) * inverse_root
    inside = lax.broadcasted_iota(I32, scores.shape, 2) < length[:, None, None]
    scores = jnp.where(inside, scores, -jnp.inf)
    highest = jnp.max(scores, axis=2, keepdims=True)
    raised = jnp.exp(scores - highest)
    weights = (raised / jnp.sum(raised, axis=2, keepdims=True)).astype(BF)
    latent = jnp.einsum("rht,rct->rhc", weights, caches_t[:, :latent_width], preferred_element_type=F32).astype(BF)
    values = jnp.einsum("rhc,hcv->rhv", latent, value_up, preferred_element_type=F32).astype(BF)
    return values.reshape(values.shape[0], -1)


def pack_kernel(owners, turns, at, cache_ref, out_ref, sems):
    span = out_ref.shape[1]
    first = pl.multiple_of(at[0] * span, span)

    def copy(i):
        return pltpu.make_async_copy(
            cache_ref.at[i, pl.ds(first, span)], out_ref.at[owners[i]], sems.at[i]
        )

    for i in range(cache_ref.shape[0]):

        @pl.when(turns[i] == at[1])
        def _():
            copy(i).start()

    for i in range(cache_ref.shape[0]):

        @pl.when(turns[i] == at[1])
        def _():
            copy(i).wait()


def pack_cache(owners, turns, at, cache, span, n_expert):
    return pl.pallas_call(
        pack_kernel,
        out_shape=jax.ShapeDtypeStruct((n_expert, span, cache.shape[2]), cache.dtype),
        in_specs=[whole(pltpu.SMEM)] * 3 + [whole(pl.ANY)],
        out_specs=whole(pl.ANY),
        scratch_shapes=[pltpu.SemaphoreType.DMA((cache.shape[0],))],
        compiler_params=params(),
        name="pack_cache",
    )(owners, turns, at, cache)


def select_kernel(sources, arrived_ref, out_ref, sems):
    copies = [
        pltpu.make_async_copy(arrived_ref.at[sources[k]], out_ref.at[k], sems.at[k])
        for k in range(out_ref.shape[0])
    ]
    for copy in copies:
        copy.start()
    for copy in copies:
        copy.wait()


def select_arrived(sources, arrived):
    count = sources.shape[0]
    return pl.pallas_call(
        select_kernel,
        out_shape=jax.ShapeDtypeStruct((count,) + arrived.shape[1:], arrived.dtype),
        in_specs=[whole(pltpu.SMEM), whole(pl.ANY)],
        out_specs=whole(pl.ANY),
        scratch_shapes=[pltpu.SemaphoreType.DMA((count,))],
        compiler_params=params(),
        name="select_arrived",
    )(sources, arrived)


def new_attention_kernel(lens, at, q_ref, up_ref, res_ref, *refs):
    pieces, out_ref, latents = refs[:-2], refs[-2], refs[-1]
    ring = len(pieces) // 2
    pairs, span = pieces[0].shape[0], pieces[0].shape[1]
    old = res_ref.shape[0]
    count = pairs * MOST
    heads, latent_width, value_width = up_ref.shape
    inverse_root = (NOPE + ROPE) ** (-0.5)
    place, core = at[0], at[1]
    column = lax.broadcasted_iota(I32, (heads, ring * span), 1)
    position = ((place + ring - column // span) % ring) * span + column % span
    for i in range(count):
        k, turn = i // MOST, i % MOST
        ours = core == turn
        cache = jnp.concatenate(
            [jnp.where(ours, pieces[d][k], pieces[ring + d][k]) for d in range(ring)], axis=0
        )
        scores = (
            lax.dot_general(q_ref[old + i], cache, (((1,), (1,)), ((), ())), preferred_element_type=F32)
            * inverse_root
        )
        scores = jnp.where(position < lens[i], scores, -jnp.inf)
        raised = jnp.exp(scores - jnp.max(scores, axis=1, keepdims=True))
        weights = (raised / jnp.sum(raised, axis=1, keepdims=True)).astype(BF)
        latents[:, i, :] = jnp.dot(weights, cache[:, :latent_width], preferred_element_type=F32)
    for h in range(heads):
        values = jnp.dot(latents[h, :, :].astype(BF), up_ref[h], preferred_element_type=F32)
        rows = jnp.concatenate(
            [res_ref[:, h * value_width : (h + 1) * value_width].astype(F32), values[:count]], axis=0
        ).astype(BF)
        out_ref[:, h * value_width : (h + 1) * value_width] = rows


def new_attention(lens, at, queries, value_up, resident, pieces):
    heads, latent_width, value_width = value_up.shape
    rows = queries.shape[0]
    return pl.pallas_call(
        new_attention_kernel,
        out_shape=jax.ShapeDtypeStruct((rows, heads * value_width), BF),
        in_specs=[whole(pltpu.SMEM)] * 2 + [whole()] * (3 + len(pieces)),
        out_specs=whole(),
        scratch_shapes=[pltpu.VMEM((heads, rows, latent_width), F32)],
        compiler_params=params(),
        name="new_attention",
    )(lens, at, queries, value_up, resident, *pieces)


def plan_kernel(rows_dev, ids_ref, gates_ref, sel_ref, mix_ref):
    rows, choose = ids_ref.shape
    slots_all = sel_ref.shape[1]
    slots = rows // rows_dev * CAP
    experts = slots_all // slots
    expert = lax.broadcasted_iota(I32, (rows, experts), 1)
    member = jnp.zeros((rows, experts), F32)
    gate = jnp.zeros((rows, experts), F32)
    for k in range(choose):
        same = ids_ref[:, k : k + 1] == expert
        member = jnp.where(same, 1.0, member)
        gate = jnp.where(same, gates_ref[:, k : k + 1], gate)
    to_row = lax.broadcasted_iota(I32, (rows, rows), 0)
    from_row = lax.broadcasted_iota(I32, (rows, rows), 1)
    before = (from_row < to_row) & (from_row // rows_dev == to_row // rows_dev)
    rank = jnp.dot(before.astype(F32).astype(BF), member.astype(BF), preferred_element_type=F32)
    block = lax.broadcasted_iota(I32, (rows, experts), 0) // rows_dev
    slot = jnp.where(member > 0, rank + (block * CAP).astype(F32), -1.0)
    spread = (
        lax.broadcasted_iota(I32, (experts, slots_all), 0)
        == lax.broadcasted_iota(I32, (experts, slots_all), 1) // slots
    ).astype(F32)
    slot_wide = jnp.dot(slot.astype(BF), spread.astype(BF), preferred_element_type=F32)
    gate_wide = jnp.dot(gate, spread, preferred_element_type=F32, precision=lax.Precision.HIGHEST)
    wanted = (lax.broadcasted_iota(I32, (rows, slots_all), 1) % slots).astype(F32)
    hit = slot_wide == wanted
    sel_ref[...] = jnp.where(hit, 1.0, 0.0).astype(BF)
    mix_ref[...] = jnp.where(hit, gate_wide, 0.0)


def plan(ids, gates, rows_dev, experts):
    rows = ids.shape[0]
    slots_all = experts * (rows // rows_dev) * CAP
    return pl.pallas_call(
        functools.partial(plan_kernel, rows_dev),
        out_shape=(
            jax.ShapeDtypeStruct((rows, slots_all), BF),
            jax.ShapeDtypeStruct((rows, slots_all), F32),
        ),
        in_specs=[whole()] * 2,
        out_specs=(whole(), whole()),
        compiler_params=params(),
        name="plan",
    )(ids, gates)


def dispatch_kernel(parts_ref, residual_ref, sel_ref, hidden_ref, out_ref):
    total = parts_ref[0].astype(F32)
    for k in range(1, parts_ref.shape[0]):
        total = total + parts_ref[k].astype(F32)
    hidden = (residual_ref[...].astype(F32) + total).astype(BF)
    hidden_ref[...] = hidden
    picked = lax.dot_general(sel_ref[...], hidden, (((0,), (0,)), ((), ())), preferred_element_type=F32)
    out_ref[...] = picked.reshape(out_ref.shape).astype(BF)


def dispatch(parts, residual, sel, experts):
    rows, columns = residual.shape
    return pl.pallas_call(
        dispatch_kernel,
        out_shape=(
            jax.ShapeDtypeStruct((rows, columns), BF),
            jax.ShapeDtypeStruct((experts, sel.shape[1] // experts, columns), BF),
        ),
        in_specs=[whole()] * 3,
        out_specs=(whole(), whole()),
        compiler_params=params(),
        name="dispatch",
    )(parts, residual, sel)


def norm_kernel(x_ref, gain_ref, out_ref):
    x = x_ref[...].astype(F32)
    width = x.shape[0] * x.shape[2]
    squares = jnp.sum(jnp.sum(x * x, axis=0), axis=1, keepdims=True)
    inverse = lax.rsqrt(squares / width + 1e-06)
    out_ref[...] = (x * inverse[None] * gain_ref[...].astype(F32)).astype(BF)


def normed_rows(x, gain):
    return pl.pallas_call(
        norm_kernel,
        out_shape=jax.ShapeDtypeStruct(x.shape, BF),
        in_specs=[whole()] * 2,
        out_specs=whole(),
        compiler_params=params(),
        name="norm",
    )(x, gain)


def experts_kernel(layout, *refs):
    count = sum(layout)
    x_refs, (gate_ref, up_ref, down_ref), outs = refs[:count], refs[count : count + 3], refs[count + 3 :]
    columns, slots = x_refs[0].shape[0], x_refs[0].shape[1]
    width = x_refs[0].shape[2]
    gate = up = None
    for j in range(columns):
        pieces, at = [], 0
        for parts in layout:
            split = columns // parts
            pieces.append(x_refs[at + j // split][j % split].astype(F32))
            at += parts
        x = jnp.concatenate(pieces, axis=0).astype(BF)
        g = jnp.dot(x, gate_ref[j], preferred_element_type=F32)
        u = jnp.dot(x, up_ref[j], preferred_element_type=F32)
        gate, up = (g, u) if gate is None else (gate + g, up + u)
    act = (gate * jax.nn.sigmoid(gate) * up).astype(BF)
    for j in range(columns):
        y = jnp.dot(act, down_ref[:, j * width : (j + 1) * width], preferred_element_type=F32)
        for k, out in enumerate(outs):
            out[j] = y[k * slots : (k + 1) * slots].astype(out.dtype)


def run_experts(layout, pieces, w_gate, w_up, w_down, types):
    shape = pieces[0].shape
    return pl.pallas_call(
        functools.partial(experts_kernel, layout),
        out_shape=tuple(jax.ShapeDtypeStruct(shape, kind) for kind in types),
        in_specs=[whole()] * (len(pieces) + 3),
        out_specs=tuple(whole() for _ in types),
        compiler_params=params(),
        name="experts",
    )(*pieces, w_gate, w_up, w_down)


def combine_kernel(back_ref, mix_ref, hidden_ref, out_ref):
    back = back_ref[...].astype(F32).reshape(-1, back_ref.shape[2])
    routed = jnp.dot(mix_ref[...], back, preferred_element_type=F32, precision=lax.Precision.HIGHEST)
    out_ref[...] = (hidden_ref[...].astype(F32) + routed).astype(BF)


def combine(back, mix, hidden):
    return pl.pallas_call(
        combine_kernel,
        out_shape=jax.ShapeDtypeStruct(hidden.shape, BF),
        in_specs=[whole()] * 3,
        out_specs=whole(),
        compiler_params=params(),
        name="combine",
    )(back, mix, hidden)


def exchange(x, axes):
    return lax.all_to_all(x, axes, split_axis=0, concat_axis=0, tiled=True)


def gather_over_head(x):
    near = ring_gather(x, HEAD[0])
    layout = [len(p) if isinstance(p, tuple) else 1 for p in near]
    near = flat(near)
    far = [shifted(p, HEAD[1], 1) for p in near]
    return layout * 2, near + far


def sum_over_head(kept, sent):
    other = [shifted(s, HEAD[1], 1) for s in (sent[2], sent[1], sent[3], sent[0])]
    other = [other[3], other[1], other[0], other[2]]
    pair = [k + o.astype(F32) for k, o in zip(kept, other)]
    cut = pair[2].shape[0] // 2
    far = pair[2].astype(BF)
    low = shifted(far[:cut], HEAD[0], -1).astype(F32)
    high = shifted(far[cut:], HEAD[0], 1).astype(F32)
    before = jnp.concatenate([pair[1][:cut] + low, pair[1][cut:]], axis=0).astype(BF)
    after = jnp.concatenate([pair[3][:cut], pair[3][cut:] + high], axis=0).astype(BF)
    from_after = shifted(before, HEAD[0], -1).astype(F32)
    from_before = shifted(after, HEAD[0], 1).astype(F32)
    return (pair[0] + from_after + from_before).astype(BF)


def per_device(
    queries,
    resident_cache,
    resident_len,
    new_cache,
    new_len,
    new_owner,
    value_up,
    w_output,
    residual,
    expert_ids,
    expert_gates,
    norm_gain,
    w_gate,
    w_up,
    w_down,
):
    n_expert = lax.axis_size(EXPERT)
    n_head = lax.axis_size(HEAD)
    me = lax.axis_index(EXPERT)
    head = lax.axis_index(HEAD)
    req_count = resident_cache.shape[0]
    new_count = new_cache.shape[0]
    rows_dev = req_count + new_count
    rows_all = rows_dev * n_expert
    block_rows = rows_all // n_head
    columns = residual.shape[1]
    news = new_owner.shape[0]

    x, core = lax.axis_index(HEAD[0]), lax.axis_index(HEAD[1])
    ring = lax.axis_size(HEAD[0])
    number = jnp.arange(news, dtype=I32)
    equal = (new_owner[:, None] == new_owner[None, :]) & (number[None, :] < number[:, None])
    place = jnp.sum(equal.astype(I32), axis=1)
    owners = lax.dynamic_slice_in_dim(new_owner, me * new_count, new_count)
    mine = jnp.arange(new_count, dtype=I32)
    turns = jnp.sum(((owners[:, None] == owners[None, :]) & (mine[None, :] < mine[:, None])).astype(I32), axis=1)
    taken = (new_owner == me)[None, :] & (place[None, :] == mine[:, None])
    sources = jnp.sum(jnp.where(taken, (number // new_count)[None, :], 0), axis=1)[::MOST]
    lens = jnp.sum(jnp.where(taken, new_len[None, :], 0), axis=1)
    at = jnp.stack([x, core]).astype(I32)

    packed = pack_cache(owners, turns, at, new_cache, new_cache.shape[1] // ring, n_expert)
    ours = select_arrived(sources, exchange(packed, EXPERT))
    near = [ours] + [shifted(ours, HEAD[0], d) for d in range(1, ring)]
    pieces = near + [shifted(p, HEAD[1], 1) for p in near]
    resident = attend(queries[:req_count], jnp.swapaxes(resident_cache, 1, 2), resident_len, value_up)
    attention = new_attention(lens, at, queries, value_up, resident, pieces)

    everywhere = exchange(jnp.broadcast_to(attention[None], (n_expert,) + attention.shape), EXPERT)
    mixed = jnp.dot(everywhere.reshape(rows_all, -1), w_output, preferred_element_type=F32).astype(BF)
    parts = exchange(mixed.reshape(n_head, block_rows, columns), HEAD)

    block = lambda a: lax.dynamic_slice_in_dim(a, head * block_rows, block_rows)
    sel, mix = plan(block(expert_ids), block(expert_gates), rows_dev, n_expert)
    hidden, outgoing = dispatch(parts, block(residual), sel, n_expert)
    received = exchange(outgoing, EXPERT)
    normed = normed_rows(received, norm_gain.reshape(n_expert, 1, columns))
    layout, pieces = gather_over_head(normed)
    x_count = lax.axis_size(HEAD[0])
    made = run_experts(
        tuple(layout),
        pieces,
        w_gate.reshape(n_expert, columns, -1),
        w_up.reshape(n_expert, columns, -1),
        w_down.reshape(w_down.shape[1:]),
        [F32] * x_count + [BF] * x_count,
    )
    summed = sum_over_head(made[:x_count], made[x_count:])
    back = exchange(summed, EXPERT)
    return combine(back, mix, hidden)


def solution(mesh):
    finer = Mesh(mesh.devices.reshape(4, 2, 8, 4), ("head_0", "head_1", "expert_0", "expert_1"))
    in_specs = (
        P(EXPERT, HEAD, None),
        P(EXPERT, None, None),
        P(EXPERT),
        P(EXPERT, None, None),
        P(),
        P(),
        P(HEAD, None, None),
        P(HEAD, EXPERT),
        P(None, EXPERT),
        P(),
        P(),
        P(),
        P(EXPERT, None, HEAD),
        P(EXPERT, None, HEAD),
        P(EXPERT, HEAD, None),
    )
    out_specs = P(HEAD, EXPERT)
    return jax.shard_map(
        per_device, mesh=finer, in_specs=in_specs, out_specs=out_specs, check_vma=False
    )
```

```python
import functools

import jax
import jax.numpy as jnp
from jax import lax
from jax.experimental import pallas as pl
from jax.experimental.pallas import tpu as pltpu
from jax.sharding import Mesh
from jax.sharding import PartitionSpec as P

ROPE = 64
NOPE = 128
EXPERT = ("expert_0", "expert_1")
HEAD = ("head_0", "head_1")
MOST = 2
CAP = 6
BF = jnp.bfloat16
F32 = jnp.float32
I32 = jnp.int32
VMEM_BYTES = 48 * 1024 * 1024


def params():
    return pltpu.CompilerParams(vmem_limit_bytes=VMEM_BYTES)


def whole(memory=pltpu.VMEM):
    return pl.BlockSpec(memory_space=memory)


def shifted(x, axis, step):
    n = lax.axis_size(axis)
    return lax.ppermute(x, axis, [(i, (i + step) % n) for i in range(n)])


def ring_gather(x, axis, dim):
    n = lax.axis_size(axis)
    far = n // 2
    cut = x.shape[dim] // 2
    found = {0: x}
    right, left = x, x
    for step in range(1, far):
        right, left = shifted(right, axis, 1), shifted(left, axis, -1)
        found[step], found[n - step] = right, left
    low = lax.slice_in_dim(right, 0, cut, axis=dim)
    high = lax.slice_in_dim(left, cut, x.shape[dim], axis=dim)
    found[far] = (shifted(low, axis, 1), shifted(high, axis, -1))
    return [found[d] for d in range(n)]


def flat(pieces):
    out = []
    for piece in pieces:
        out.extend(piece if isinstance(piece, tuple) else (piece,))
    return out


def attend(queries, caches_t, length, value_up):
    inverse_root = (NOPE + ROPE) ** (-0.5)
    latent_width = value_up.shape[1]
    scores = jnp.einsum("rhc,rct->rht", queries, caches_t, preferred_element_type=F32) * inverse_root
    inside = lax.broadcasted_iota(I32, scores.shape, 2) < length[:, None, None]
    scores = jnp.where(inside, scores, -jnp.inf)
    highest = jnp.max(scores, axis=2, keepdims=True)
    raised = jnp.exp(scores - highest)
    weights = (raised / jnp.sum(raised, axis=2, keepdims=True)).astype(BF)
    latent = jnp.einsum("rht,rct->rhc", weights, caches_t[:, :latent_width], preferred_element_type=F32).astype(BF)
    values = jnp.einsum("rhc,hcv->rhv", latent, value_up, preferred_element_type=F32).astype(BF)
    return values.reshape(values.shape[0], -1)


def pack_kernel(owners, turns, at, cache_ref, out_ref, sems):
    span = out_ref.shape[1]
    first = pl.multiple_of(at[0] * span, span)

    def copy(i):
        return pltpu.make_async_copy(
            cache_ref.at[i, pl.ds(first, span)], out_ref.at[owners[i]], sems.at[i]
        )

    for i in range(cache_ref.shape[0]):

        @pl.when(turns[i] == at[1])
        def _():
            copy(i).start()

    for i in range(cache_ref.shape[0]):

        @pl.when(turns[i] == at[1])
        def _():
            copy(i).wait()


def pack_cache(owners, turns, at, cache, span, n_expert):
    return pl.pallas_call(
        pack_kernel,
        out_shape=jax.ShapeDtypeStruct((n_expert, span, cache.shape[2]), cache.dtype),
        in_specs=[whole(pltpu.SMEM)] * 3 + [whole(pl.ANY)],
        out_specs=whole(pl.ANY),
        scratch_shapes=[pltpu.SemaphoreType.DMA((cache.shape[0],))],
        compiler_params=params(),
        name="pack_cache",
    )(owners, turns, at, cache)


def select_kernel(sources, arrived_ref, out_ref, sems):
    copies = [
        pltpu.make_async_copy(arrived_ref.at[sources[k]], out_ref.at[k], sems.at[k])
        for k in range(out_ref.shape[0])
    ]
    for copy in copies:
        copy.start()
    for copy in copies:
        copy.wait()


def select_arrived(sources, arrived):
    count = sources.shape[0]
    return pl.pallas_call(
        select_kernel,
        out_shape=jax.ShapeDtypeStruct((count,) + arrived.shape[1:], arrived.dtype),
        in_specs=[whole(pltpu.SMEM), whole(pl.ANY)],
        out_specs=whole(pl.ANY),
        scratch_shapes=[pltpu.SemaphoreType.DMA((count,))],
        compiler_params=params(),
        name="select_arrived",
    )(sources, arrived)


def new_attention_kernel(lens, at, q_ref, up_ref, res_ref, *refs):
    pieces, out_ref, latents = refs[:-2], refs[-2], refs[-1]
    ring = len(pieces) // 2
    pairs, span = pieces[0].shape[0], pieces[0].shape[1]
    old = res_ref.shape[0]
    count = pairs * MOST
    heads, latent_width, value_width = up_ref.shape
    inverse_root = (NOPE + ROPE) ** (-0.5)
    place, core = at[0], at[1]
    column = lax.broadcasted_iota(I32, (heads, ring * span), 1)
    position = ((place + ring - column // span) % ring) * span + column % span
    for i in range(count):
        k, turn = i // MOST, i % MOST
        ours = core == turn
        cache = jnp.concatenate(
            [jnp.where(ours, pieces[d][k], pieces[ring + d][k]) for d in range(ring)], axis=0
        )
        scores = (
            lax.dot_general(q_ref[old + i], cache, (((1,), (1,)), ((), ())), preferred_element_type=F32)
            * inverse_root
        )
        scores = jnp.where(position < lens[i], scores, -jnp.inf)
        raised = jnp.exp(scores - jnp.max(scores, axis=1, keepdims=True))
        weights = (raised / jnp.sum(raised, axis=1, keepdims=True)).astype(BF)
        latents[:, i, :] = jnp.dot(weights, cache[:, :latent_width], preferred_element_type=F32)
    for h in range(heads):
        values = jnp.dot(latents[h, :, :].astype(BF), up_ref[h], preferred_element_type=F32)
        rows = jnp.concatenate(
            [res_ref[:, h * value_width : (h + 1) * value_width].astype(F32), values[:count]], axis=0
        ).astype(BF)
        out_ref[:, h * value_width : (h + 1) * value_width] = rows


def new_attention(lens, at, queries, value_up, resident, pieces):
    heads, latent_width, value_width = value_up.shape
    rows = queries.shape[0]
    return pl.pallas_call(
        new_attention_kernel,
        out_shape=jax.ShapeDtypeStruct((rows, heads * value_width), BF),
        in_specs=[whole(pltpu.SMEM)] * 2 + [whole()] * (3 + len(pieces)),
        out_specs=whole(),
        scratch_shapes=[pltpu.VMEM((heads, rows, latent_width), F32)],
        compiler_params=params(),
        name="new_attention",
    )(lens, at, queries, value_up, resident, *pieces)


def stack_kernel(*refs):
    rows = refs[0].shape[0]
    for k, ref in enumerate(refs[:-1]):
        refs[-1][k * rows : (k + 1) * rows, :] = ref[...]


def stacked(pieces):
    rows, width = pieces[0].shape
    return pl.pallas_call(
        stack_kernel,
        out_shape=jax.ShapeDtypeStruct((rows * len(pieces), width), pieces[0].dtype),
        in_specs=[whole()] * len(pieces),
        out_specs=whole(),
        compiler_params=params(),
        name="stack",
    )(*pieces)


def project_kernel(makers, w_ref, *refs):
    pieces, out_ref = refs[:-1], refs[-1]
    rows = out_ref.shape[1]
    attention = jnp.concatenate([piece[...] for piece in pieces], axis=0)
    mixed = lax.dot_general(attention, w_ref[...], (((1,), (1,)), ((), ())), preferred_element_type=F32).astype(BF)
    for k in range(out_ref.shape[0]):
        out_ref[makers[k]] = mixed[k * rows : (k + 1) * rows]


def project(makers, w_output_t, pieces, rows):
    return pl.pallas_call(
        project_kernel,
        out_shape=jax.ShapeDtypeStruct((makers.shape[0], rows, w_output_t.shape[0]), BF),
        in_specs=[whole(pltpu.SMEM)] + [whole()] * (1 + len(pieces)),
        out_specs=whole(),
        compiler_params=params(),
        name="project",
    )(makers, w_output_t, *pieces)


def plan_kernel(rows_dev, ids_ref, gates_ref, sel_ref, mix_ref):
    rows, choose = ids_ref.shape
    slots_all = sel_ref.shape[1]
    slots = rows // rows_dev * CAP
    experts = slots_all // slots
    expert = lax.broadcasted_iota(I32, (rows, experts), 1)
    member = jnp.zeros((rows, experts), F32)
    gate = jnp.zeros((rows, experts), F32)
    for k in range(choose):
        same = ids_ref[:, k : k + 1] == expert
        member = jnp.where(same, 1.0, member)
        gate = jnp.where(same, gates_ref[:, k : k + 1], gate)
    to_row = lax.broadcasted_iota(I32, (rows, rows), 0)
    from_row = lax.broadcasted_iota(I32, (rows, rows), 1)
    before = (from_row < to_row) & (from_row // rows_dev == to_row // rows_dev)
    rank = jnp.dot(before.astype(F32).astype(BF), member.astype(BF), preferred_element_type=F32)
    block = lax.broadcasted_iota(I32, (rows, experts), 0) // rows_dev
    slot = jnp.where(member > 0, rank + (block * CAP).astype(F32), -1.0)
    spread = (
        lax.broadcasted_iota(I32, (experts, slots_all), 0)
        == lax.broadcasted_iota(I32, (experts, slots_all), 1) // slots
    ).astype(F32)
    slot_wide = jnp.dot(slot.astype(BF), spread.astype(BF), preferred_element_type=F32)
    gate_wide = jnp.dot(gate, spread, preferred_element_type=F32, precision=lax.Precision.HIGHEST)
    wanted = (lax.broadcasted_iota(I32, (rows, slots_all), 1) % slots).astype(F32)
    hit = slot_wide == wanted
    sel_ref[...] = jnp.where(hit, 1.0, 0.0).astype(BF)
    mix_ref[...] = jnp.where(hit, gate_wide, 0.0)


def plan(ids, gates, rows_dev, experts):
    rows = ids.shape[0]
    slots_all = experts * (rows // rows_dev) * CAP
    return pl.pallas_call(
        functools.partial(plan_kernel, rows_dev),
        out_shape=(
            jax.ShapeDtypeStruct((rows, slots_all), BF),
            jax.ShapeDtypeStruct((rows, slots_all), F32),
        ),
        in_specs=[whole()] * 2,
        out_specs=(whole(), whole()),
        compiler_params=params(),
        name="plan",
    )(ids, gates)


def dispatch_kernel(parts_ref, residual_ref, sel_ref, hidden_ref, out_ref):
    total = parts_ref[0].astype(F32)
    for k in range(1, parts_ref.shape[0]):
        total = total + parts_ref[k].astype(F32)
    hidden = (residual_ref[...].astype(F32) + total).astype(BF)
    hidden_ref[...] = hidden
    picked = lax.dot_general(sel_ref[...], hidden, (((0,), (0,)), ((), ())), preferred_element_type=F32)
    out_ref[...] = picked.reshape(out_ref.shape).astype(BF)


def dispatch(parts, residual, sel, experts):
    rows, columns = residual.shape
    return pl.pallas_call(
        dispatch_kernel,
        out_shape=(
            jax.ShapeDtypeStruct((rows, columns), BF),
            jax.ShapeDtypeStruct((experts, sel.shape[1] // experts, columns), BF),
        ),
        in_specs=[whole()] * 3,
        out_specs=(whole(), whole()),
        compiler_params=params(),
        name="dispatch",
    )(parts, residual, sel)


def norm_kernel(x_ref, gain_ref, out_ref):
    count = x_ref.shape[0]
    squares = 0.0
    for j in range(count):
        x = x_ref[j].astype(F32)
        squares = squares + x * x
    mean = jnp.sum(squares, axis=1, keepdims=True) / out_ref.shape[1]
    inverse = lax.rsqrt(mean + 1e-06)
    x = jnp.concatenate([x_ref[j].astype(F32) for j in range(count)], axis=1)
    out_ref[...] = (x * inverse * gain_ref[...].astype(F32)).astype(BF)


def normed_rows(x, gain):
    return pl.pallas_call(
        norm_kernel,
        out_shape=jax.ShapeDtypeStruct((x.shape[1], x.shape[0] * x.shape[2]), BF),
        in_specs=[whole()] * 2,
        out_specs=whole(),
        compiler_params=params(),
        name="norm",
    )(x, gain)


def experts_kernel(layout, *refs):
    count = sum(layout)
    x_refs, (gate_ref, up_ref, down_ref), outs = refs[:count], refs[count : count + 3], refs[count + 3 :]
    slots = x_refs[0].shape[0]
    blocks, at = [], 0
    for parts in layout:
        blocks.append(jnp.concatenate([x_refs[at + p][...] for p in range(parts)], axis=1))
        at += parts
    x = jnp.concatenate(blocks, axis=0)
    gate = jnp.dot(x, gate_ref[...], preferred_element_type=F32)
    up = jnp.dot(x, up_ref[...], preferred_element_type=F32)
    act = (gate * jax.nn.sigmoid(gate) * up).astype(BF)
    y = jnp.dot(act, down_ref[...], preferred_element_type=F32)
    for k, out in enumerate(outs):
        out[...] = y[k * slots : (k + 1) * slots].astype(BF)


def run_experts(layout, pieces, w_gate, w_up, w_down):
    out = jax.ShapeDtypeStruct(pieces[0].shape, BF)
    return pl.pallas_call(
        functools.partial(experts_kernel, layout),
        out_shape=(out,) * len(layout),
        in_specs=[whole()] * (len(pieces) + 3),
        out_specs=(whole(),) * len(layout),
        compiler_params=params(),
        name="experts",
    )(*pieces, w_gate, w_up, w_down)


def total_kernel(kept_ref, after_ref, before_ref, out_ref):
    width = out_ref.shape[2]
    total = kept_ref[...] + after_ref[...].astype(F32) + before_ref[...].astype(F32)
    for j in range(out_ref.shape[0]):
        out_ref[j] = total[:, j * width : (j + 1) * width].astype(BF)


def total_by_columns(kept, after, before, parts):
    return pl.pallas_call(
        total_kernel,
        out_shape=jax.ShapeDtypeStruct((parts, kept.shape[0], kept.shape[1] // parts), BF),
        in_specs=[whole()] * 3,
        out_specs=whole(),
        compiler_params=params(),
        name="total",
    )(kept, after, before)


def combine_kernel(back_ref, mix_ref, hidden_ref, out_ref):
    back = back_ref[...].astype(F32).reshape(-1, back_ref.shape[2])
    routed = jnp.dot(mix_ref[...], back, preferred_element_type=F32, precision=lax.Precision.HIGHEST)
    out_ref[...] = (hidden_ref[...].astype(F32) + routed).astype(BF)


def combine(back, mix, hidden):
    return pl.pallas_call(
        combine_kernel,
        out_shape=jax.ShapeDtypeStruct(hidden.shape, BF),
        in_specs=[whole()] * 3,
        out_specs=whole(),
        compiler_params=params(),
        name="combine",
    )(back, mix, hidden)


def exchange(x, axes):
    return lax.all_to_all(x, axes, split_axis=0, concat_axis=0, tiled=True)


def gather_over_head(x):
    near = ring_gather(x, HEAD[0], 1)
    layout = [len(p) if isinstance(p, tuple) else 1 for p in near]
    near = flat(near)
    far = [shifted(p, HEAD[1], 1) for p in near]
    return tuple(layout * 2), near + far


def sum_over_head(kept, sent, parts):
    other = {d: shifted(sent[d], HEAD[1], 1) for d in (2, 1, 3, 0)}
    pair = [kept[d].astype(F32) + other[d].astype(F32) for d in range(4)]
    cut = pair[2].shape[1] // 2
    far = pair[2].astype(BF)
    low = shifted(far[:, :cut], HEAD[0], -1).astype(F32)
    high = shifted(far[:, cut:], HEAD[0], 1).astype(F32)
    before = jnp.concatenate([pair[1][:, :cut] + low, pair[1][:, cut:]], axis=1).astype(BF)
    after = jnp.concatenate([pair[3][:, :cut], pair[3][:, cut:] + high], axis=1).astype(BF)
    return total_by_columns(pair[0], shifted(before, HEAD[0], -1), shifted(after, HEAD[0], 1), parts)


def per_device(
    queries,
    resident_cache,
    resident_len,
    new_cache,
    new_len,
    new_owner,
    value_up,
    w_output,
    residual,
    expert_ids,
    expert_gates,
    norm_gain,
    w_gate,
    w_up,
    w_down,
):
    n_expert = lax.axis_size(EXPERT)
    n_head = lax.axis_size(HEAD)
    n_z, n_y = lax.axis_size(EXPERT[0]), lax.axis_size(EXPERT[1])
    z, y = lax.axis_index(EXPERT[0]), lax.axis_index(EXPERT[1])
    me = lax.axis_index(EXPERT)
    head = lax.axis_index(HEAD)
    req_count = resident_cache.shape[0]
    new_count = new_cache.shape[0]
    rows_dev = req_count + new_count
    rows_all = rows_dev * n_expert
    block_rows = rows_all // n_head
    columns = residual.shape[1]
    news = new_owner.shape[0]

    x, core = lax.axis_index(HEAD[0]), lax.axis_index(HEAD[1])
    ring = lax.axis_size(HEAD[0])
    number = jnp.arange(news, dtype=I32)
    equal = (new_owner[:, None] == new_owner[None, :]) & (number[None, :] < number[:, None])
    place = jnp.sum(equal.astype(I32), axis=1)
    owners = lax.dynamic_slice_in_dim(new_owner, me * new_count, new_count)
    mine = jnp.arange(new_count, dtype=I32)
    turns = jnp.sum(((owners[:, None] == owners[None, :]) & (mine[None, :] < mine[:, None])).astype(I32), axis=1)
    taken = (new_owner == me)[None, :] & (place[None, :] == mine[:, None])
    sources = jnp.sum(jnp.where(taken, (number // new_count)[None, :], 0), axis=1)[::MOST]
    lens = jnp.sum(jnp.where(taken, new_len[None, :], 0), axis=1)
    at = jnp.stack([x, core]).astype(I32)

    packed = pack_cache(owners, turns, at, new_cache, new_cache.shape[1] // ring, n_expert)
    ours = select_arrived(sources, exchange(packed, EXPERT))
    near = [ours] + [shifted(ours, HEAD[0], d) for d in range(1, ring)]
    pieces = near + [shifted(p, HEAD[1], 1) for p in near]
    resident = attend(queries[:req_count], jnp.swapaxes(resident_cache, 1, 2), resident_len, value_up)
    attention = new_attention(lens, at, queries, value_up, resident, pieces)

    along_y = [attention] + [shifted(attention, EXPERT[1], d) for d in range(1, n_y)]
    rows_here = flat(ring_gather(stacked(along_y), EXPERT[0], 0))
    away = jnp.arange(n_expert, dtype=I32)
    makers = ((z + n_z - (away // n_y)) % n_z) * n_y + (y + n_y - away % n_y) % n_y
    mixed = project(makers, w_output.T, rows_here, rows_dev)
    parts = exchange(mixed.reshape(n_head, block_rows, columns), HEAD)

    block = lambda a: lax.dynamic_slice_in_dim(a, head * block_rows, block_rows)
    sel, mix = plan(block(expert_ids), block(expert_gates), rows_dev, n_expert)
    hidden, outgoing = dispatch(parts, block(residual), sel, n_expert)
    received = exchange(outgoing, EXPERT)
    normed = normed_rows(received, norm_gain.reshape(1, -1))
    layout, pieces = gather_over_head(normed)
    made = run_experts(layout, pieces, *(w.reshape(w.shape[1:]) for w in (w_gate, w_up, w_down)))
    summed = sum_over_head(made[:ring], made[ring:], n_expert)
    back = exchange(summed, EXPERT)
    return combine(back, mix, hidden)


def solution(mesh):
    finer = Mesh(mesh.devices.reshape(4, 2, 8, 4), ("head_0", "head_1", "expert_0", "expert_1"))
    in_specs = (
        P(EXPERT, HEAD, None),
        P(EXPERT, None, None),
        P(EXPERT),
        P(EXPERT, None, None),
        P(),
        P(),
        P(HEAD, None, None),
        P(HEAD, EXPERT),
        P(None, EXPERT),
        P(),
        P(),
        P(),
        P(EXPERT, None, HEAD),
        P(EXPERT, None, HEAD),
        P(EXPERT, HEAD, None),
    )
    out_specs = P(HEAD, EXPERT)
    return jax.shard_map(
        per_device, mesh=finer, in_specs=in_specs, out_specs=out_specs, check_vma=False
    )
```

```python
import functools

import jax
import jax.numpy as jnp
from jax import lax
from jax.experimental import pallas as pl
from jax.experimental.pallas import tpu as pltpu
from jax.sharding import Mesh
from jax.sharding import PartitionSpec as P

ROPE = 64
NOPE = 128
EXPERT = ("expert_0", "expert_1")
HEAD = ("head_0", "head_1")
MOST = 2
CAP = 6
BF = jnp.bfloat16
F32 = jnp.float32
I32 = jnp.int32
VMEM_BYTES = 48 * 1024 * 1024


def params():
    return pltpu.CompilerParams(vmem_limit_bytes=VMEM_BYTES)


def whole(memory=pltpu.VMEM):
    return pl.BlockSpec(memory_space=memory)


def shifted(x, axis, step):
    n = lax.axis_size(axis)
    return lax.ppermute(x, axis, [(i, (i + step) % n) for i in range(n)])


def ring_gather(x, axis, dim):
    n = lax.axis_size(axis)
    far = n // 2
    cut = x.shape[dim] // 2
    found = {0: x}
    right, left = x, x
    for step in range(1, far):
        right, left = shifted(right, axis, 1), shifted(left, axis, -1)
        found[step], found[n - step] = right, left
    low = lax.slice_in_dim(right, 0, cut, axis=dim)
    high = lax.slice_in_dim(left, cut, x.shape[dim], axis=dim)
    found[far] = (shifted(low, axis, 1), shifted(high, axis, -1))
    return [found[d] for d in range(n)]


def flat(pieces):
    out = []
    for piece in pieces:
        out.extend(piece if isinstance(piece, tuple) else (piece,))
    return out


def attend(queries, caches_t, length, value_up):
    inverse_root = (NOPE + ROPE) ** (-0.5)
    latent_width = value_up.shape[1]
    scores = jnp.einsum("rhc,rct->rht", queries, caches_t, preferred_element_type=F32) * inverse_root
    inside = lax.broadcasted_iota(I32, scores.shape, 2) < length[:, None, None]
    scores = jnp.where(inside, scores, -jnp.inf)
    highest = jnp.max(scores, axis=2, keepdims=True)
    raised = jnp.exp(scores - highest)
    weights = (raised / jnp.sum(raised, axis=2, keepdims=True)).astype(BF)
    latent = jnp.einsum("rht,rct->rhc", weights, caches_t[:, :latent_width], preferred_element_type=F32).astype(BF)
    return jnp.einsum("rhc,hcv->hrv", latent, value_up, preferred_element_type=F32).astype(BF)


def pack_kernel(owners, turns, at, cache_ref, out_ref, sems):
    span = out_ref.shape[1]
    first = pl.multiple_of(at[0] * span, span)

    def copy(i):
        return pltpu.make_async_copy(
            cache_ref.at[i, pl.ds(first, span)], out_ref.at[owners[i]], sems.at[i]
        )

    for i in range(cache_ref.shape[0]):

        @pl.when(turns[i] == at[1])
        def _():
            copy(i).start()

    for i in range(cache_ref.shape[0]):

        @pl.when(turns[i] == at[1])
        def _():
            copy(i).wait()


def pack_cache(owners, turns, at, cache, span, n_expert):
    return pl.pallas_call(
        pack_kernel,
        out_shape=jax.ShapeDtypeStruct((n_expert, span, cache.shape[2]), cache.dtype),
        in_specs=[whole(pltpu.SMEM)] * 3 + [whole(pl.ANY)],
        out_specs=whole(pl.ANY),
        scratch_shapes=[pltpu.SemaphoreType.DMA((cache.shape[0],))],
        compiler_params=params(),
        name="pack_cache",
    )(owners, turns, at, cache)


def select_kernel(sources, arrived_ref, out_ref, sems):
    copies = [
        pltpu.make_async_copy(arrived_ref.at[sources[k]], out_ref.at[k], sems.at[k])
        for k in range(out_ref.shape[0])
    ]
    for copy in copies:
        copy.start()
    for copy in copies:
        copy.wait()


def select_arrived(sources, arrived):
    count = sources.shape[0]
    return pl.pallas_call(
        select_kernel,
        out_shape=jax.ShapeDtypeStruct((count,) + arrived.shape[1:], arrived.dtype),
        in_specs=[whole(pltpu.SMEM), whole(pl.ANY)],
        out_specs=whole(pl.ANY),
        scratch_shapes=[pltpu.SemaphoreType.DMA((count,))],
        compiler_params=params(),
        name="select_arrived",
    )(sources, arrived)


def new_attention_kernel(groups, lens, at, q_ref, up_ref, res_ref, *refs):
    pieces, out_refs, latents = refs[: -groups - 1], refs[-groups - 1 : -1], refs[-1]
    ring = len(pieces) // 2
    pairs, span = pieces[0].shape[0], pieces[0].shape[1]
    old = res_ref.shape[1]
    count = pairs * MOST
    heads, latent_width, value_width = up_ref.shape
    inverse_root = (NOPE + ROPE) ** (-0.5)
    place, core, row = at[0], at[1], at[2]
    column = lax.broadcasted_iota(I32, (heads, ring * span), 1)
    position = ((place + ring - column // span) % ring) * span + column % span
    for i in range(count):
        k, turn = i // MOST, i % MOST
        ours = core == turn
        cache = jnp.concatenate(
            [jnp.where(ours, pieces[d][k], pieces[ring + d][k]) for d in range(ring)], axis=0
        )
        scores = (
            lax.dot_general(q_ref[old + i], cache, (((1,), (1,)), ((), ())), preferred_element_type=F32)
            * inverse_root
        )
        scores = jnp.where(position < lens[i], scores, -jnp.inf)
        raised = jnp.exp(scores - jnp.max(scores, axis=1, keepdims=True))
        weights = (raised / jnp.sum(raised, axis=1, keepdims=True)).astype(BF)
        latents[:, i, :] = jnp.dot(weights, cache[:, :latent_width], preferred_element_type=F32)
    each = heads // groups
    for d, out_ref in enumerate(out_refs):
        for k in range(each):
            h = lax.rem(row + d, groups) * each + k
            values = jnp.dot(latents[h].astype(BF), up_ref[h], preferred_element_type=F32)
            rows = jnp.concatenate([res_ref[h].astype(F32), values[:count]], axis=0).astype(BF)
            out_ref[:, k * value_width : (k + 1) * value_width] = rows


def new_attention(lens, at, queries, value_up, resident, pieces, groups):
    heads, latent_width, value_width = value_up.shape
    rows = queries.shape[0]
    out = jax.ShapeDtypeStruct((rows, heads // groups * value_width), BF)
    return pl.pallas_call(
        functools.partial(new_attention_kernel, groups),
        out_shape=(out,) * groups,
        in_specs=[whole(pltpu.SMEM)] * 2 + [whole()] * (3 + len(pieces)),
        out_specs=(whole(),) * groups,
        scratch_shapes=[pltpu.VMEM((heads, rows, latent_width), F32)],
        compiler_params=params(),
        name="new_attention",
    )(lens, at, queries, value_up, resident, *pieces)


def stack_kernel(*refs):
    rows = refs[0].shape[0]
    for k, ref in enumerate(refs[:-1]):
        refs[-1][k * rows : (k + 1) * rows, :] = ref[...]


def stacked(pieces):
    rows, width = pieces[0].shape
    return pl.pallas_call(
        stack_kernel,
        out_shape=jax.ShapeDtypeStruct((rows * len(pieces), width), pieces[0].dtype),
        in_specs=[whole()] * len(pieces),
        out_specs=whole(),
        compiler_params=params(),
        name="stack",
    )(*pieces)


def project_kernel(places, count, *refs):
    pieces, weights, outs = refs[:count], refs[count:-2], refs[-2:]
    n_y, subs = outs[0].shape[0], outs[0].shape[2]
    rows = outs[0].shape[3]
    attention = jnp.concatenate([piece[...] for piece in pieces], axis=0)
    blocks = attention.shape[0] // rows
    mixed = [
        lax.dot_general(attention, w[...], (((1,), (1,)), ((), ())), preferred_element_type=F32).astype(BF)
        for w in weights
    ]

    def store(even, odd):
        for k in range(blocks):
            out = odd if (k // subs) % 2 else even
            for d in range(n_y):
                out[d, places[0, k], places[1, k]] = mixed[d][k * rows : (k + 1) * rows]

    @pl.when(places[0, blocks] == 0)
    def _():
        store(outs[0], outs[1])

    @pl.when(places[0, blocks] != 0)
    def _():
        store(outs[1], outs[0])


def project(places, pieces, weights, shape):
    out = jax.ShapeDtypeStruct(shape, BF)
    kernel = lambda p, *refs: project_kernel(p, len(pieces), *refs)
    return pl.pallas_call(
        kernel,
        out_shape=(out, out),
        in_specs=[whole(pltpu.SMEM)] + [whole()] * (len(pieces) + len(weights)),
        out_specs=(whole(), whole()),
        compiler_params=params(),
        name="project",
    )(places, *pieces, *weights)


def pair_kernel(a_ref, b_ref, *outs):
    for d, out in enumerate(outs):
        out[...] = (a_ref[d].astype(F32) + b_ref[d].astype(F32)).astype(out.dtype)


def pair_sum(a, b):
    out = jax.ShapeDtypeStruct(a.shape[1:], BF)
    return pl.pallas_call(
        pair_kernel,
        out_shape=(out,) * a.shape[0],
        in_specs=[whole()] * 2,
        out_specs=(whole(),) * a.shape[0],
        compiler_params=params(),
        name="pair_sum",
    )(a, b)


def several_kernel(count, *refs):
    for k, out in enumerate(refs[count:]):
        total = refs[0][k].astype(F32)
        for ref in refs[1:count]:
            total = total + ref[k].astype(F32)
        out[...] = total.astype(BF)


def several_sum(arrays):
    out = jax.ShapeDtypeStruct(arrays[0].shape[1:], BF)
    parts = arrays[0].shape[0]
    return pl.pallas_call(
        functools.partial(several_kernel, len(arrays)),
        out_shape=(out,) * parts,
        in_specs=[whole()] * len(arrays),
        out_specs=(whole(),) * parts,
        compiler_params=params(),
        name="several_sum",
    )(*arrays)


def plan_kernel(rows_dev, ids_ref, gates_ref, sel_ref, mix_ref):
    rows, choose = ids_ref.shape
    slots_all = sel_ref.shape[1]
    slots = rows // rows_dev * CAP
    experts = slots_all // slots
    expert = lax.broadcasted_iota(I32, (rows, experts), 1)
    member = jnp.zeros((rows, experts), F32)
    gate = jnp.zeros((rows, experts), F32)
    for k in range(choose):
        same = ids_ref[:, k : k + 1] == expert
        member = jnp.where(same, 1.0, member)
        gate = jnp.where(same, gates_ref[:, k : k + 1], gate)
    to_row = lax.broadcasted_iota(I32, (rows, rows), 0)
    from_row = lax.broadcasted_iota(I32, (rows, rows), 1)
    before = (from_row < to_row) & (from_row // rows_dev == to_row // rows_dev)
    rank = jnp.dot(before.astype(F32).astype(BF), member.astype(BF), preferred_element_type=F32)
    block = lax.broadcasted_iota(I32, (rows, experts), 0) // rows_dev
    slot = jnp.where(member > 0, rank + (block * CAP).astype(F32), -1.0)
    spread = (
        lax.broadcasted_iota(I32, (experts, slots_all), 0)
        == lax.broadcasted_iota(I32, (experts, slots_all), 1) // slots
    ).astype(F32)
    slot_wide = jnp.dot(slot.astype(BF), spread.astype(BF), preferred_element_type=F32)
    gate_wide = jnp.dot(gate, spread, preferred_element_type=F32, precision=lax.Precision.HIGHEST)
    wanted = (lax.broadcasted_iota(I32, (rows, slots_all), 1) % slots).astype(F32)
    hit = slot_wide == wanted
    sel_ref[...] = jnp.where(hit, 1.0, 0.0).astype(BF)
    mix_ref[...] = jnp.where(hit, gate_wide, 0.0)


def plan(ids, gates, rows_dev, experts):
    rows = ids.shape[0]
    slots_all = experts * (rows // rows_dev) * CAP
    return pl.pallas_call(
        functools.partial(plan_kernel, rows_dev),
        out_shape=(
            jax.ShapeDtypeStruct((rows, slots_all), BF),
            jax.ShapeDtypeStruct((rows, slots_all), F32),
        ),
        in_specs=[whole()] * 2,
        out_specs=(whole(), whole()),
        compiler_params=params(),
        name="plan",
    )(ids, gates)


def dispatch_kernel(count, *refs):
    parts, (residual_ref, sel_ref, hidden_ref, out_ref) = refs[:count], refs[count:]
    total = parts[0][...].astype(F32)
    for part in parts[1:]:
        total = total + part[...].astype(F32)
    hidden = (residual_ref[...].astype(F32) + total).astype(BF)
    hidden_ref[...] = hidden
    picked = lax.dot_general(sel_ref[...], hidden, (((0,), (0,)), ((), ())), preferred_element_type=F32)
    out_ref[...] = picked.reshape(out_ref.shape).astype(BF)


def dispatch(parts, residual, sel, experts):
    rows, columns = residual.shape
    return pl.pallas_call(
        functools.partial(dispatch_kernel, len(parts)),
        out_shape=(
            jax.ShapeDtypeStruct((rows, columns), BF),
            jax.ShapeDtypeStruct((experts, sel.shape[1] // experts, columns), BF),
        ),
        in_specs=[whole()] * (len(parts) + 2),
        out_specs=(whole(), whole()),
        compiler_params=params(),
        name="dispatch",
    )(*parts, residual, sel)


def norm_kernel(x_ref, gain_ref, out_ref):
    count = x_ref.shape[0]
    squares = 0.0
    for j in range(count):
        x = x_ref[j].astype(F32)
        squares = squares + x * x
    mean = jnp.sum(squares, axis=1, keepdims=True) / out_ref.shape[1]
    inverse = lax.rsqrt(mean + 1e-06)
    x = jnp.concatenate([x_ref[j].astype(F32) for j in range(count)], axis=1)
    out_ref[...] = (x * inverse * gain_ref[...].astype(F32)).astype(BF)


def normed_rows(x, gain):
    return pl.pallas_call(
        norm_kernel,
        out_shape=jax.ShapeDtypeStruct((x.shape[1], x.shape[0] * x.shape[2]), BF),
        in_specs=[whole()] * 2,
        out_specs=whole(),
        compiler_params=params(),
        name="norm",
    )(x, gain)


def units_kernel(layout, *refs):
    count = sum(layout)
    x_refs, (gate_ref, up_ref, act_ref) = refs[:count], refs[count:]
    blocks, at = [], 0
    for parts in layout:
        blocks.append(jnp.concatenate([x_refs[at + p][...] for p in range(parts)], axis=1))
        at += parts
    x = jnp.concatenate(blocks, axis=0)
    gate = jnp.dot(x, gate_ref[...], preferred_element_type=F32)
    up = jnp.dot(x, up_ref[...], preferred_element_type=F32)
    act_ref[...] = (gate * jax.nn.sigmoid(gate) * up).astype(BF)


def run_units(layout, pieces, w_gate, w_up):
    slots = pieces[0].shape[0] * len(layout)
    return pl.pallas_call(
        functools.partial(units_kernel, layout),
        out_shape=jax.ShapeDtypeStruct((slots, w_gate.shape[1]), BF),
        in_specs=[whole()] * (len(pieces) + 2),
        out_specs=whole(),
        compiler_params=params(),
        name="units",
    )(*pieces, w_gate, w_up)


def down_kernel(*refs):
    ring = len(refs) // 2 - 1
    acts, downs, outs = refs[:ring], refs[ring : 2 * ring], refs[2 * ring :]
    slots = acts[0].shape[0] // (2 * ring)
    turned = []
    for d in range(ring):
        act = acts[d][...].astype(F32)
        order = [core * ring + (t + ring - d) % ring for core in range(2) for t in range(ring)]
        turned.append(jnp.concatenate([act[k * slots : (k + 1) * slots] for k in order], axis=0).astype(BF))
    units = jnp.concatenate(turned, axis=1)
    down = jnp.concatenate([w[...] for w in downs], axis=0)
    y = jnp.dot(units, down, preferred_element_type=F32).astype(BF)
    half = ring * slots
    for k, out in enumerate(outs):
        for t in range(ring):
            at = k * half + t * slots
            out[t] = y[at : at + slots]


def run_down(acts, downs):
    ring = len(acts)
    out = jax.ShapeDtypeStruct((ring, acts[0].shape[0] // (2 * ring), downs[0].shape[1]), BF)
    return pl.pallas_call(
        down_kernel,
        out_shape=(out, out),
        in_specs=[whole()] * (2 * ring),
        out_specs=(whole(), whole()),
        compiler_params=params(),
        name="down",
    )(*acts, *downs)


def columns_kernel(at, *refs):
    pieces, out_ref = refs[:-1], refs[-1]
    ring = len(pieces)
    each, width = out_ref.shape[0] // ring, out_ref.shape[2]
    for t, piece in enumerate(pieces):
        first = lax.rem(at[0] + t, ring) * each
        values = piece[...].astype(F32)
        for j in range(each):
            out_ref[first + j] = values[:, j * width : (j + 1) * width].astype(BF)


def by_columns(at, pieces, parts):
    slots, width = pieces[0].shape
    return pl.pallas_call(
        columns_kernel,
        out_shape=jax.ShapeDtypeStruct((parts, slots, width * len(pieces) // parts), BF),
        in_specs=[whole(pltpu.SMEM)] + [whole()] * len(pieces),
        out_specs=whole(),
        compiler_params=params(),
        name="by_columns",
    )(at, *pieces)


def combine_kernel(back_ref, mix_ref, hidden_ref, out_ref):
    back = back_ref[...].astype(F32).reshape(-1, back_ref.shape[2])
    routed = jnp.dot(mix_ref[...], back, preferred_element_type=F32, precision=lax.Precision.HIGHEST)
    out_ref[...] = (hidden_ref[...].astype(F32) + routed).astype(BF)


def combine(back, mix, hidden):
    return pl.pallas_call(
        combine_kernel,
        out_shape=jax.ShapeDtypeStruct(hidden.shape, BF),
        in_specs=[whole()] * 3,
        out_specs=whole(),
        compiler_params=params(),
        name="combine",
    )(back, mix, hidden)


def exchange(x, axes):
    return lax.all_to_all(x, axes, split_axis=0, concat_axis=0, tiled=True)


def gather_over_head(x):
    near = ring_gather(x, HEAD[0], 1)
    layout = [len(p) if isinstance(p, tuple) else 1 for p in near]
    near = flat(near)
    far = [shifted(p, HEAD[1], 1) for p in near]
    return tuple(layout * 2), near + far


def per_device(
    queries,
    resident_cache,
    resident_len,
    new_cache,
    new_len,
    new_owner,
    value_up,
    w_output,
    residual,
    expert_ids,
    expert_gates,
    norm_gain,
    w_gate,
    w_up,
    w_down,
):
    n_expert = lax.axis_size(EXPERT)
    n_head = lax.axis_size(HEAD)
    n_z, n_y = lax.axis_size(EXPERT[0]), lax.axis_size(EXPERT[1])
    z, y = lax.axis_index(EXPERT[0]), lax.axis_index(EXPERT[1])
    me = lax.axis_index(EXPERT)
    head = lax.axis_index(HEAD)
    req_count = resident_cache.shape[0]
    new_count = new_cache.shape[0]
    rows_dev = req_count + new_count
    rows_all = rows_dev * n_expert
    block_rows = rows_all // n_head
    columns = residual.shape[1]
    news = new_owner.shape[0]

    x, core = lax.axis_index(HEAD[0]), lax.axis_index(HEAD[1])
    ring = lax.axis_size(HEAD[0])
    number = jnp.arange(news, dtype=I32)
    equal = (new_owner[:, None] == new_owner[None, :]) & (number[None, :] < number[:, None])
    place = jnp.sum(equal.astype(I32), axis=1)
    owners = lax.dynamic_slice_in_dim(new_owner, me * new_count, new_count)
    mine = jnp.arange(new_count, dtype=I32)
    turns = jnp.sum(((owners[:, None] == owners[None, :]) & (mine[None, :] < mine[:, None])).astype(I32), axis=1)
    taken = (new_owner == me)[None, :] & (place[None, :] == mine[:, None])
    sources = jnp.sum(jnp.where(taken, (number // new_count)[None, :], 0), axis=1)[::MOST]
    lens = jnp.sum(jnp.where(taken, new_len[None, :], 0), axis=1)
    at = jnp.stack([x, core, y]).astype(I32)

    packed = pack_cache(owners, turns, at, new_cache, new_cache.shape[1] // ring, n_expert)
    w_t = w_output.T
    width = w_t.shape[1] // n_y
    group = lambda d: lax.dynamic_slice_in_dim(w_t, ((y + d) % n_y) * width, width, 1)
    weights = [group(0)] + [shifted(group(d), EXPERT[1], d) for d in range(1, n_y)]

    w_d = w_down.reshape(w_down.shape[1:])
    part = w_d.shape[1] // ring
    some = lambda d: lax.dynamic_slice_in_dim(w_d, ((x + d) % ring) * part, part, 1)
    downs = [some(0)] + [shifted(some(d), HEAD[0], d) for d in range(1, ring)]

    ours = select_arrived(sources, exchange(packed, EXPERT))
    near = [ours] + [shifted(ours, HEAD[0], d) for d in range(1, ring)]
    pieces = near + [shifted(p, HEAD[1], 1) for p in near]
    resident = attend(queries[:req_count], jnp.swapaxes(resident_cache, 1, 2), resident_len, value_up)
    attention = new_attention(lens, at, queries, value_up, resident, pieces, n_y)

    along_y = list(attention[:1]) + [shifted(attention[d], EXPERT[1], d) for d in range(1, n_y)]
    rows_here = flat(ring_gather(stacked(along_y), EXPERT[0], 0))
    away = jnp.arange(n_expert, dtype=I32)
    maker_z = (z + n_z - away // n_y) % n_z
    places = jnp.stack([(maker_z // 2 + ring - x) % ring, (y + n_y - away % n_y) % n_y])
    places = jnp.concatenate([places, jnp.full((2, 1), (z + core) % 2, I32)], axis=1)
    shape = (n_y, ring, n_y, rows_dev, columns)
    own, other = project(places, rows_here, weights, shape)
    by_column = pair_sum(own, shifted(other, HEAD[1], 1))
    by_column = list(by_column[:1]) + [shifted(by_column[d], EXPERT[1], -d) for d in range(1, n_y)]
    by_block = several_sum([p.reshape(ring, block_rows, columns) for p in by_column])
    parts = list(by_block[:1]) + [shifted(by_block[t], HEAD[0], t) for t in range(1, ring)]

    block = lambda a: lax.dynamic_slice_in_dim(a, head * block_rows, block_rows)
    sel, mix = plan(block(expert_ids), block(expert_gates), rows_dev, n_expert)
    hidden, outgoing = dispatch(parts, block(residual), sel, n_expert)
    received = exchange(outgoing, EXPERT)
    normed = normed_rows(received, norm_gain.reshape(1, -1))
    layout, pieces = gather_over_head(normed)
    act = run_units(layout, pieces, w_gate.reshape(w_gate.shape[1:]), w_up.reshape(w_up.shape[1:]))
    acts = [act] + [shifted(act, HEAD[0], d) for d in range(1, ring)]
    kept, sent = run_down(acts, downs)
    made = pair_sum(kept, shifted(sent, HEAD[1], 1))
    made = list(made[:1]) + [shifted(made[t], HEAD[0], -t) for t in range(1, ring)]
    back = exchange(by_columns(at, made, n_expert), EXPERT)
    return combine(back, mix, hidden)


def solution(mesh):
    finer = Mesh(mesh.devices.reshape(4, 2, 8, 4), ("head_0", "head_1", "expert_0", "expert_1"))
    in_specs = (
        P(EXPERT, HEAD, None),
        P(EXPERT, None, None),
        P(EXPERT),
        P(EXPERT, None, None),
        P(),
        P(),
        P(HEAD, None, None),
        P(HEAD, EXPERT),
        P(None, EXPERT),
        P(),
        P(),
        P(),
        P(EXPERT, None, HEAD),
        P(EXPERT, None, HEAD),
        P(EXPERT, HEAD, None),
    )
    out_specs = P(HEAD, EXPERT)
    return jax.shard_map(
        per_device, mesh=finer, in_specs=in_specs, out_specs=out_specs, check_vma=False
    )
```

```python
import functools

import jax
import jax.numpy as jnp
from jax import lax
from jax.experimental import pallas as pl
from jax.experimental.pallas import tpu as pltpu
from jax.sharding import Mesh
from jax.sharding import PartitionSpec as P

ROPE = 64
NOPE = 128
EXPERT = ("expert_0", "expert_1")
HEAD = ("head_0", "head_1")
MOST = 2
CAP = 6
BF = jnp.bfloat16
F32 = jnp.float32
I32 = jnp.int32
VMEM_BYTES = 48 * 1024 * 1024


def params(limit=VMEM_BYTES):
    return pltpu.CompilerParams(vmem_limit_bytes=limit)


def whole(memory=pltpu.VMEM):
    return pl.BlockSpec(memory_space=memory)


def shifted(x, axis, step):
    n = lax.axis_size(axis)
    return lax.ppermute(x, axis, [(i, (i + step) % n) for i in range(n)])


def ring_gather(x, axis, dim):
    n = lax.axis_size(axis)
    far = n // 2
    cut = x.shape[dim] // 2
    found = {0: x}
    right, left = x, x
    for step in range(1, far):
        right, left = shifted(right, axis, 1), shifted(left, axis, -1)
        found[step], found[n - step] = right, left
    low = lax.slice_in_dim(right, 0, cut, axis=dim)
    high = lax.slice_in_dim(left, cut, x.shape[dim], axis=dim)
    found[far] = (shifted(low, axis, 1), shifted(high, axis, -1))
    return [found[d] for d in range(n)]


def flat(pieces):
    out = []
    for piece in pieces:
        out.extend(piece if isinstance(piece, tuple) else (piece,))
    return out


def attend(queries, caches_t, length, value_up):
    inverse_root = (NOPE + ROPE) ** (-0.5)
    latent_width = value_up.shape[1]
    scores = jnp.einsum("rhc,rct->rht", queries, caches_t, preferred_element_type=F32) * inverse_root
    inside = lax.broadcasted_iota(I32, scores.shape, 2) < length[:, None, None]
    scores = jnp.where(inside, scores, -jnp.inf)
    highest = jnp.max(scores, axis=2, keepdims=True)
    raised = jnp.exp(scores - highest)
    weights = (raised / jnp.sum(raised, axis=2, keepdims=True)).astype(BF)
    latent = jnp.einsum("rht,rct->rhc", weights, caches_t[:, :latent_width], preferred_element_type=F32).astype(BF)
    values = jnp.einsum("rhc,hcv->rhv", latent, value_up, preferred_element_type=F32).astype(BF)
    return values.reshape(values.shape[0], -1)


def pack_kernel(owners, turns, at, cache_ref, out_ref, sems):
    span = out_ref.shape[1]
    first = pl.multiple_of(at[0] * span, span)

    def copy(i):
        return pltpu.make_async_copy(
            cache_ref.at[i, pl.ds(first, span)], out_ref.at[owners[i]], sems.at[i]
        )

    for i in range(cache_ref.shape[0]):

        @pl.when(turns[i] == at[1])
        def _():
            copy(i).start()

    for i in range(cache_ref.shape[0]):

        @pl.when(turns[i] == at[1])
        def _():
            copy(i).wait()


def pack_cache(owners, turns, at, cache, span, n_expert):
    return pl.pallas_call(
        pack_kernel,
        out_shape=jax.ShapeDtypeStruct((n_expert, span, cache.shape[2]), cache.dtype),
        in_specs=[whole(pltpu.SMEM)] * 3 + [whole(pltpu.HBM)],
        out_specs=whole(pl.ANY),
        scratch_shapes=[pltpu.SemaphoreType.DMA((cache.shape[0],))],
        compiler_params=params(60 * 1024 * 1024),
        name="pack_cache",
    )(owners, turns, at, cache)


def select_kernel(sources, arrived_ref, out_ref, sems):
    copies = [
        pltpu.make_async_copy(arrived_ref.at[sources[k]], out_ref.at[k], sems.at[k])
        for k in range(out_ref.shape[0])
    ]
    for copy in copies:
        copy.start()
    for copy in copies:
        copy.wait()


def select_arrived(sources, arrived):
    count = sources.shape[0]
    return pl.pallas_call(
        select_kernel,
        out_shape=jax.ShapeDtypeStruct((count,) + arrived.shape[1:], arrived.dtype),
        in_specs=[whole(pltpu.SMEM), whole(pl.ANY)],
        out_specs=whole(pl.ANY),
        scratch_shapes=[pltpu.SemaphoreType.DMA((count,))],
        compiler_params=params(),
        name="select_arrived",
    )(sources, arrived)


def new_attention_kernel(lens, at, q_ref, up_ref, res_ref, near_ref, far_ref, out_ref, latents):
    ring, pairs, span = near_ref.shape[:3]
    old = res_ref.shape[0]
    count = pairs * MOST
    heads, latent_width, value_width = up_ref.shape
    inverse_root = (NOPE + ROPE) ** (-0.5)
    place, core = at[0], at[1]
    column = lax.broadcasted_iota(I32, (heads, ring * span), 1)
    position = ((place + ring - column // span) % ring) * span + column % span
    for i in range(count):
        k, turn = i // MOST, i % MOST
        ours = core == turn
        cache = jnp.concatenate(
            [jnp.where(ours, near_ref[d, k], far_ref[d, k]) for d in range(ring)], axis=0
        )
        scores = (
            lax.dot_general(q_ref[old + i], cache, (((1,), (1,)), ((), ())), preferred_element_type=F32)
            * inverse_root
        )
        scores = jnp.where(position < lens[i], scores, -jnp.inf)
        raised = jnp.exp(scores - jnp.max(scores, axis=1, keepdims=True))
        weights = (raised / jnp.sum(raised, axis=1, keepdims=True)).astype(BF)
        latents[:, i, :] = jnp.dot(weights, cache[:, :latent_width], preferred_element_type=F32)
    for h in range(heads):
        values = jnp.dot(latents[h, :, :].astype(BF), up_ref[h], preferred_element_type=F32)
        rows = jnp.concatenate(
            [res_ref[:, h * value_width : (h + 1) * value_width].astype(F32), values[:count]], axis=0
        ).astype(BF)
        out_ref[:, h * value_width : (h + 1) * value_width] = rows


def new_attention(lens, at, queries, value_up, resident, near, far):
    heads, latent_width, value_width = value_up.shape
    rows = queries.shape[0]
    return pl.pallas_call(
        new_attention_kernel,
        out_shape=jax.ShapeDtypeStruct((rows, heads * value_width), BF),
        in_specs=[whole(pltpu.SMEM)] * 2 + [whole()] * 5,
        out_specs=whole(),
        scratch_shapes=[pltpu.VMEM((heads, rows, latent_width), F32)],
        compiler_params=params(),
        name="new_attention",
    )(lens, at, queries, value_up, resident, near, far)


def stack_kernel(*refs):
    rows = refs[0].shape[0]
    for k, ref in enumerate(refs[:-1]):
        refs[-1][k * rows : (k + 1) * rows, :] = ref[...]


def stacked(pieces):
    rows, width = pieces[0].shape
    return pl.pallas_call(
        stack_kernel,
        out_shape=jax.ShapeDtypeStruct((rows * len(pieces), width), pieces[0].dtype),
        in_specs=[whole()] * len(pieces),
        out_specs=whole(),
        compiler_params=params(),
        name="stack",
    )(*pieces)


def layers_kernel(*refs):
    for k, ref in enumerate(refs[:-1]):
        refs[-1][k] = ref[...]


def layers(pieces):
    return pl.pallas_call(
        layers_kernel,
        out_shape=jax.ShapeDtypeStruct((len(pieces),) + pieces[0].shape, pieces[0].dtype),
        in_specs=[whole()] * len(pieces),
        out_specs=whole(),
        compiler_params=params(),
        name="layers",
    )(*pieces)


def project_kernel(makers, w_ref, *refs):
    pieces, out_ref = refs[:-1], refs[-1]
    rows = out_ref.shape[1]
    attention = jnp.concatenate([piece[...] for piece in pieces], axis=0)
    mixed = lax.dot_general(attention, w_ref[...], (((1,), (1,)), ((), ())), preferred_element_type=F32).astype(BF)
    for k in range(out_ref.shape[0]):
        out_ref[makers[k]] = mixed[k * rows : (k + 1) * rows]


def project(makers, w_output_t, pieces, rows):
    return pl.pallas_call(
        project_kernel,
        out_shape=jax.ShapeDtypeStruct((makers.shape[0], rows, w_output_t.shape[0]), BF),
        in_specs=[whole(pltpu.SMEM)] + [whole()] * (1 + len(pieces)),
        out_specs=whole(),
        compiler_params=params(),
        name="project",
    )(makers, w_output_t, *pieces)


def pair_kernel(a_ref, b_ref, *outs):
    for d, out in enumerate(outs):
        out[...] = (a_ref[d].astype(F32) + b_ref[d].astype(F32)).astype(out.dtype)


def pair_sum(a, b):
    out = jax.ShapeDtypeStruct(a.shape[1:], BF)
    return pl.pallas_call(
        pair_kernel,
        out_shape=(out,) * a.shape[0],
        in_specs=[whole()] * 2,
        out_specs=(whole(),) * a.shape[0],
        compiler_params=params(),
        name="pair_sum",
    )(a, b)


def plan_kernel(rows_dev, ids_ref, gates_ref, sel_ref, mix_ref):
    rows, choose = ids_ref.shape
    slots_all = sel_ref.shape[1]
    slots = rows // rows_dev * CAP
    experts = slots_all // slots
    expert = lax.broadcasted_iota(I32, (rows, experts), 1)
    member = jnp.zeros((rows, experts), F32)
    gate = jnp.zeros((rows, experts), F32)
    for k in range(choose):
        same = ids_ref[:, k : k + 1] == expert
        member = jnp.where(same, 1.0, member)
        gate = jnp.where(same, gates_ref[:, k : k + 1], gate)
    to_row = lax.broadcasted_iota(I32, (rows, rows), 0)
    from_row = lax.broadcasted_iota(I32, (rows, rows), 1)
    before = (from_row < to_row) & (from_row // rows_dev == to_row // rows_dev)
    rank = jnp.dot(before.astype(F32).astype(BF), member.astype(BF), preferred_element_type=F32)
    block = lax.broadcasted_iota(I32, (rows, experts), 0) // rows_dev
    slot = jnp.where(member > 0, rank + (block * CAP).astype(F32), -1.0)
    spread = (
        lax.broadcasted_iota(I32, (experts, slots_all), 0)
        == lax.broadcasted_iota(I32, (experts, slots_all), 1) // slots
    ).astype(F32)
    slot_wide = jnp.dot(slot.astype(BF), spread.astype(BF), preferred_element_type=F32)
    gate_wide = jnp.dot(gate, spread, preferred_element_type=F32, precision=lax.Precision.HIGHEST)
    wanted = (lax.broadcasted_iota(I32, (rows, slots_all), 1) % slots).astype(F32)
    hit = slot_wide == wanted
    sel_ref[...] = jnp.where(hit, 1.0, 0.0).astype(BF)
    mix_ref[...] = jnp.where(hit, gate_wide, 0.0)


def plan(ids, gates, rows_dev, experts):
    rows = ids.shape[0]
    slots_all = experts * (rows // rows_dev) * CAP
    return pl.pallas_call(
        functools.partial(plan_kernel, rows_dev),
        out_shape=(
            jax.ShapeDtypeStruct((rows, slots_all), BF),
            jax.ShapeDtypeStruct((rows, slots_all), F32),
        ),
        in_specs=[whole()] * 2,
        out_specs=(whole(), whole()),
        compiler_params=params(),
        name="plan",
    )(ids, gates)


def dispatch_kernel(parts_ref, residual_ref, sel_ref, hidden_ref, out_ref):
    total = parts_ref[0].astype(F32)
    for k in range(1, parts_ref.shape[0]):
        total = total + parts_ref[k].astype(F32)
    hidden = (residual_ref[...].astype(F32) + total).astype(BF)
    hidden_ref[...] = hidden
    picked = lax.dot_general(sel_ref[...], hidden, (((0,), (0,)), ((), ())), preferred_element_type=F32)
    out_ref[...] = picked.reshape(out_ref.shape).astype(BF)


def dispatch(parts, residual, sel, experts):
    rows, columns = residual.shape
    return pl.pallas_call(
        dispatch_kernel,
        out_shape=(
            jax.ShapeDtypeStruct((rows, columns), BF),
            jax.ShapeDtypeStruct((experts, sel.shape[1] // experts, columns), BF),
        ),
        in_specs=[whole()] * 3,
        out_specs=(whole(), whole()),
        compiler_params=params(),
        name="dispatch",
    )(parts, residual, sel)


def norm_kernel(x_ref, gain_ref, out_ref):
    count = x_ref.shape[0]
    squares = 0.0
    for j in range(count):
        x = x_ref[j].astype(F32)
        squares = squares + x * x
    mean = jnp.sum(squares, axis=1, keepdims=True) / out_ref.shape[1]
    inverse = lax.rsqrt(mean + 1e-06)
    x = jnp.concatenate([x_ref[j].astype(F32) for j in range(count)], axis=1)
    out_ref[...] = (x * inverse * gain_ref[...].astype(F32)).astype(BF)


def normed_rows(x, gain):
    return pl.pallas_call(
        norm_kernel,
        out_shape=jax.ShapeDtypeStruct((x.shape[1], x.shape[0] * x.shape[2]), BF),
        in_specs=[whole()] * 2,
        out_specs=whole(),
        compiler_params=params(),
        name="norm",
    )(x, gain)


def units_kernel(layout, *refs):
    count = sum(layout)
    x_refs, (gate_ref, up_ref, act_ref) = refs[:count], refs[count:]
    blocks, at = [], 0
    for parts in layout:
        blocks.append(jnp.concatenate([x_refs[at + p][...] for p in range(parts)], axis=1))
        at += parts
    x = jnp.concatenate(blocks, axis=0)
    gate = jnp.dot(x, gate_ref[...], preferred_element_type=F32)
    up = jnp.dot(x, up_ref[...], preferred_element_type=F32)
    act_ref[...] = (gate * jax.nn.sigmoid(gate) * up).astype(BF)


def run_units(layout, pieces, w_gate, w_up):
    slots = pieces[0].shape[0] * len(layout)
    return pl.pallas_call(
        functools.partial(units_kernel, layout),
        out_shape=jax.ShapeDtypeStruct((slots, w_gate.shape[1]), BF),
        in_specs=[whole()] * (len(pieces) + 2),
        out_specs=whole(),
        compiler_params=params(),
        name="units",
    )(*pieces, w_gate, w_up)


def down_kernel(*refs):
    ring = len(refs) // 2 - 1
    acts, downs, outs = refs[:ring], refs[ring : 2 * ring], refs[2 * ring :]
    slots = acts[0].shape[0] // (2 * ring)
    turned = []
    for d in range(ring):
        act = acts[d][...].astype(F32)
        order = [core * ring + (t + ring - d) % ring for core in range(2) for t in range(ring)]
        turned.append(jnp.concatenate([act[k * slots : (k + 1) * slots] for k in order], axis=0).astype(BF))
    units = jnp.concatenate(turned, axis=1)
    down = jnp.concatenate([w[...] for w in downs], axis=0)
    y = jnp.dot(units, down, preferred_element_type=F32).astype(BF)
    half = ring * slots
    for k, out in enumerate(outs):
        for t in range(ring):
            at = k * half + t * slots
            out[t] = y[at : at + slots]


def run_down(acts, downs):
    ring = len(acts)
    out = jax.ShapeDtypeStruct((ring, acts[0].shape[0] // (2 * ring), downs[0].shape[1]), BF)
    return pl.pallas_call(
        down_kernel,
        out_shape=(out, out),
        in_specs=[whole()] * (2 * ring),
        out_specs=(whole(), whole()),
        compiler_params=params(),
        name="down",
    )(*acts, *downs)


def columns_kernel(at, *refs):
    pieces, out_ref = refs[:-1], refs[-1]
    ring = len(pieces)
    each, width = out_ref.shape[0] // ring, out_ref.shape[2]
    for t, piece in enumerate(pieces):
        first = lax.rem(at[0] + t, ring) * each
        values = piece[...].astype(F32)
        for j in range(each):
            out_ref[first + j] = values[:, j * width : (j + 1) * width].astype(BF)


def by_columns(at, pieces, parts):
    slots, width = pieces[0].shape
    return pl.pallas_call(
        columns_kernel,
        out_shape=jax.ShapeDtypeStruct((parts, slots, width * len(pieces) // parts), BF),
        in_specs=[whole(pltpu.SMEM)] + [whole()] * len(pieces),
        out_specs=whole(),
        compiler_params=params(),
        name="by_columns",
    )(at, *pieces)


def combine_kernel(back_ref, mix_ref, hidden_ref, out_ref):
    back = back_ref[...].astype(F32).reshape(-1, back_ref.shape[2])
    routed = jnp.dot(mix_ref[...], back, preferred_element_type=F32, precision=lax.Precision.HIGHEST)
    out_ref[...] = (hidden_ref[...].astype(F32) + routed).astype(BF)


def combine(back, mix, hidden):
    return pl.pallas_call(
        combine_kernel,
        out_shape=jax.ShapeDtypeStruct(hidden.shape, BF),
        in_specs=[whole()] * 3,
        out_specs=whole(),
        compiler_params=params(),
        name="combine",
    )(back, mix, hidden)


def exchange(x, axes):
    return lax.all_to_all(x, axes, split_axis=0, concat_axis=0, tiled=True)


def gather_over_head(x):
    near = ring_gather(x, HEAD[0], 1)
    layout = [len(p) if isinstance(p, tuple) else 1 for p in near]
    near = flat(near)
    far = [shifted(p, HEAD[1], 1) for p in near]
    return tuple(layout * 2), near + far


def per_device(
    queries,
    resident_cache,
    resident_len,
    new_cache,
    new_len,
    new_owner,
    value_up,
    w_output,
    residual,
    expert_ids,
    expert_gates,
    norm_gain,
    w_gate,
    w_up,
    w_down,
):
    n_expert = lax.axis_size(EXPERT)
    n_head = lax.axis_size(HEAD)
    n_z, n_y = lax.axis_size(EXPERT[0]), lax.axis_size(EXPERT[1])
    z, y = lax.axis_index(EXPERT[0]), lax.axis_index(EXPERT[1])
    me = lax.axis_index(EXPERT)
    head = lax.axis_index(HEAD)
    req_count = resident_cache.shape[0]
    new_count = new_cache.shape[0]
    rows_dev = req_count + new_count
    rows_all = rows_dev * n_expert
    block_rows = rows_all // n_head
    columns = residual.shape[1]
    news = new_owner.shape[0]

    x, core = lax.axis_index(HEAD[0]), lax.axis_index(HEAD[1])
    ring = lax.axis_size(HEAD[0])
    number = jnp.arange(news, dtype=I32)
    equal = (new_owner[:, None] == new_owner[None, :]) & (number[None, :] < number[:, None])
    place = jnp.sum(equal.astype(I32), axis=1)
    owners = lax.dynamic_slice_in_dim(new_owner, me * new_count, new_count)
    mine = jnp.arange(new_count, dtype=I32)
    turns = jnp.sum(((owners[:, None] == owners[None, :]) & (mine[None, :] < mine[:, None])).astype(I32), axis=1)
    taken = (new_owner == me)[None, :] & (place[None, :] == mine[:, None])
    sources = jnp.sum(jnp.where(taken, (number // new_count)[None, :], 0), axis=1)[::MOST]
    lens = jnp.sum(jnp.where(taken, new_len[None, :], 0), axis=1)
    at = jnp.stack([x, core]).astype(I32)

    packed = pack_cache(owners, turns, at, new_cache, new_cache.shape[1] // ring, n_expert)
    packed, w_d = lax.optimization_barrier((packed, w_down.reshape(w_down.shape[1:])))
    part = w_d.shape[1] // ring
    some = lambda d: lax.dynamic_slice_in_dim(w_d, ((x + d) % ring) * part, part, 1)
    downs = [some(0)] + [shifted(some(d), HEAD[0], d) for d in range(1, ring)]
    resident = attend(queries[:req_count], jnp.swapaxes(resident_cache, 1, 2), resident_len, value_up)
    arrived, resident, *downs = lax.optimization_barrier((exchange(packed, EXPERT), resident, *downs))

    ours = select_arrived(sources, arrived)
    near = layers([ours] + [shifted(ours, HEAD[0], d) for d in range(1, ring)])
    attention = new_attention(lens, at, queries, value_up, resident, near, shifted(near, HEAD[1], 1))

    along_y = [attention] + [shifted(attention, EXPERT[1], d) for d in range(1, n_y)]
    rows_here = flat(ring_gather(stacked(along_y), EXPERT[0], 0))
    away = jnp.arange(n_expert, dtype=I32)
    makers = ((z + n_z - (away // n_y)) % n_z) * n_y + (y + n_y - away % n_y) % n_y
    mixed = project(makers, w_output.T, rows_here, rows_dev)
    parts = exchange(mixed.reshape(n_head, block_rows, columns), HEAD)

    block = lambda a: lax.dynamic_slice_in_dim(a, head * block_rows, block_rows)
    sel, mix = plan(block(expert_ids), block(expert_gates), rows_dev, n_expert)
    hidden, outgoing = dispatch(parts, block(residual), sel, n_expert)
    received = exchange(outgoing, EXPERT)
    normed = normed_rows(received, norm_gain.reshape(1, -1))
    layout, pieces = gather_over_head(normed)
    act = run_units(layout, pieces, w_gate.reshape(w_gate.shape[1:]), w_up.reshape(w_up.shape[1:]))
    acts = [act] + [shifted(act, HEAD[0], d) for d in range(1, ring)]
    kept, sent = run_down(acts, downs)
    made = pair_sum(kept, shifted(sent, HEAD[1], 1))
    made = list(made[:1]) + [shifted(made[t], HEAD[0], -t) for t in range(1, ring)]
    back = exchange(by_columns(at, made, n_expert), EXPERT)
    return combine(back, mix, hidden)


def solution(mesh):
    finer = Mesh(mesh.devices.reshape(4, 2, 8, 4), ("head_0", "head_1", "expert_0", "expert_1"))
    in_specs = (
        P(EXPERT, HEAD, None),
        P(EXPERT, None, None),
        P(EXPERT),
        P(EXPERT, None, None),
        P(),
        P(),
        P(HEAD, None, None),
        P(HEAD, EXPERT),
        P(None, EXPERT),
        P(),
        P(),
        P(),
        P(EXPERT, None, HEAD),
        P(EXPERT, None, HEAD),
        P(EXPERT, HEAD, None),
    )
    out_specs = P(HEAD, EXPERT)
    return jax.shard_map(
        per_device, mesh=finer, in_specs=in_specs, out_specs=out_specs, check_vma=False
    )
```

```python
import functools

import jax
import jax.numpy as jnp
from jax import lax
from jax.experimental import pallas as pl
from jax.experimental.pallas import tpu as pltpu
from jax.sharding import Mesh
from jax.sharding import PartitionSpec as P

ROPE = 64
NOPE = 128
EXPERT = ("expert_0", "expert_1", "expert_2")
COLUMN = EXPERT[1:]
HEAD = ("head_0", "head_1")
MOST = 2
CAP = 6
BF = jnp.bfloat16
F32 = jnp.float32
I32 = jnp.int32
VMEM_BYTES = 24 * 1024 * 1024


def params():
    return pltpu.CompilerParams(vmem_limit_bytes=VMEM_BYTES)


def whole(memory=pltpu.VMEM):
    return pl.BlockSpec(memory_space=memory)


def shifted(x, axis, step):
    n = lax.axis_size(axis)
    return lax.ppermute(x, axis, [(i, (i + step) % n) for i in range(n)])


def across(x, axis, mask):
    return lax.ppermute(x, axis, [(i, i ^ mask) for i in range(lax.axis_size(axis))])


def ring_gather(x, axis, dim):
    n = lax.axis_size(axis)
    far = n // 2
    cut = x.shape[dim] // 2
    found = {0: x}
    right, left = x, x
    for step in range(1, far):
        right, left = shifted(right, axis, 1), shifted(left, axis, -1)
        found[step], found[n - step] = right, left
    low = lax.slice_in_dim(right, 0, cut, axis=dim)
    high = lax.slice_in_dim(left, cut, x.shape[dim], axis=dim)
    found[far] = (shifted(low, axis, 1), shifted(high, axis, -1))
    return [found[d] for d in range(n)]


def flat(pieces):
    out = []
    for piece in pieces:
        out.extend(piece if isinstance(piece, tuple) else (piece,))
    return out


def attend(queries, caches_t, length, value_up):
    inverse_root = (NOPE + ROPE) ** (-0.5)
    latent_width = value_up.shape[1]
    scores = jnp.einsum("rhc,rct->rht", queries, caches_t, preferred_element_type=F32) * inverse_root
    inside = lax.broadcasted_iota(I32, scores.shape, 2) < length[:, None, None]
    scores = jnp.where(inside, scores, -jnp.inf)
    highest = jnp.max(scores, axis=2, keepdims=True)
    raised = jnp.exp(scores - highest)
    weights = (raised / jnp.sum(raised, axis=2, keepdims=True)).astype(BF)
    latent = jnp.einsum("rht,rct->rhc", weights, caches_t[:, :latent_width], preferred_element_type=F32).astype(BF)
    return jnp.einsum("rhc,hcv->hrv", latent, value_up, preferred_element_type=F32).astype(BF)


def pack_kernel(owners, cache_ref, out_ref, sems):
    count, span = cache_ref.shape[0], out_ref.shape[1]
    place, core = lax.axis_index(HEAD[0]), lax.axis_index(HEAD[1])
    base = lax.axis_index(EXPERT) * count
    first = pl.multiple_of(place * span, span)
    owner = [owners[base + i] for i in range(count)]
    turn = []
    for i in range(count):
        earlier = jnp.int32(0)
        for j in range(i):
            earlier = earlier + (owner[j] == owner[i]).astype(I32)
        turn.append(earlier)

    def copy(i):
        return pltpu.make_async_copy(
            cache_ref.at[i, pl.ds(first, span)], out_ref.at[owner[i]], sems.at[i]
        )

    for i in range(count):

        @pl.when(turn[i] == core)
        def _():
            copy(i).start()

    for i in range(count):

        @pl.when(turn[i] == core)
        def _():
            copy(i).wait()


def pack_cache(owners, cache, span, n_expert):
    return pl.pallas_call(
        pack_kernel,
        out_shape=jax.ShapeDtypeStruct((n_expert, span, cache.shape[2]), cache.dtype),
        in_specs=[whole(pltpu.SMEM), whole(pl.ANY)],
        out_specs=whole(pl.ANY),
        scratch_shapes=[pltpu.SemaphoreType.DMA((cache.shape[0],))],
        compiler_params=params(),
        name="pack_cache",
    )(owners, cache)


def select_kernel(sources, arrived_ref, out_ref, sems):
    copies = [
        pltpu.make_async_copy(arrived_ref.at[sources[k]], out_ref.at[k], sems.at[k])
        for k in range(out_ref.shape[0])
    ]
    for copy in copies:
        copy.start()
    for copy in copies:
        copy.wait()


def select_arrived(sources, arrived):
    count = sources.shape[0]
    return pl.pallas_call(
        select_kernel,
        out_shape=jax.ShapeDtypeStruct((count,) + arrived.shape[1:], arrived.dtype),
        in_specs=[whole(pltpu.SMEM), whole(pl.ANY)],
        out_specs=whole(pl.ANY),
        scratch_shapes=[pltpu.SemaphoreType.DMA((count,))],
        compiler_params=params(),
        name="select_arrived",
    )(sources, arrived)


def new_attention_kernel(groups, lens, at, q_ref, up_ref, res_ref, *refs):
    pieces, out_refs, latents = refs[: -groups - 1], refs[-groups - 1 : -1], refs[-1]
    ring = len(pieces) // 2
    pairs, span = pieces[0].shape[0], pieces[0].shape[1]
    old = res_ref.shape[1]
    count = pairs * MOST
    heads, latent_width, value_width = up_ref.shape
    inverse_root = (NOPE + ROPE) ** (-0.5)
    place, core, row = at[0], at[1], at[2]
    column = lax.broadcasted_iota(I32, (heads, ring * span), 1)
    position = ((place + ring - column // span) % ring) * span + column % span
    for i in range(count):
        k, turn = i // MOST, i % MOST
        ours = core == turn
        cache = jnp.concatenate(
            [jnp.where(ours, pieces[d][k], pieces[ring + d][k]) for d in range(ring)], axis=0
        )
        scores = (
            lax.dot_general(q_ref[old + i], cache, (((1,), (1,)), ((), ())), preferred_element_type=F32)
            * inverse_root
        )
        scores = jnp.where(position < lens[i], scores, -jnp.inf)
        raised = jnp.exp(scores - jnp.max(scores, axis=1, keepdims=True))
        weights = (raised / jnp.sum(raised, axis=1, keepdims=True)).astype(BF)
        latents[:, i, :] = jnp.dot(weights, cache[:, :latent_width], preferred_element_type=F32)
    each = heads // groups
    for d, out_ref in enumerate(out_refs):
        for k in range(each):
            h = lax.rem(row + d, groups) * each + k
            values = jnp.dot(latents[h].astype(BF), up_ref[h], preferred_element_type=F32)
            rows = jnp.concatenate([res_ref[h].astype(F32), values[:count]], axis=0).astype(BF)
            out_ref[:, k * value_width : (k + 1) * value_width] = rows


def new_attention(lens, at, queries, value_up, resident, pieces, groups):
    heads, latent_width, value_width = value_up.shape
    rows = queries.shape[0]
    out = jax.ShapeDtypeStruct((rows, heads // groups * value_width), BF)
    return pl.pallas_call(
        functools.partial(new_attention_kernel, groups),
        out_shape=(out,) * groups,
        in_specs=[whole(pltpu.SMEM)] * 2 + [whole()] * (3 + len(pieces)),
        out_specs=(whole(),) * groups,
        scratch_shapes=[pltpu.VMEM((heads, rows, latent_width), F32)],
        compiler_params=params(),
        name="new_attention",
    )(lens, at, queries, value_up, resident, *pieces)


def stack_kernel(*refs):
    rows = refs[0].shape[0]
    for k, ref in enumerate(refs[:-1]):
        refs[-1][k * rows : (k + 1) * rows, :] = ref[...]


def stacked(pieces):
    rows, width = pieces[0].shape
    return pl.pallas_call(
        stack_kernel,
        out_shape=jax.ShapeDtypeStruct((rows * len(pieces), width), pieces[0].dtype),
        in_specs=[whole()] * len(pieces),
        out_specs=whole(),
        compiler_params=params(),
        name="stack",
    )(*pieces)


def project_kernel(count, places, *refs):
    pieces, weights, out_ref = refs[:count], refs[count:-1], refs[-1]
    rows = out_ref.shape[2]
    attention = jnp.concatenate([piece[...] for piece in pieces], axis=0)
    for q, w in enumerate(weights):
        mixed = lax.dot_general(attention, w[...], (((1,), (1,)), ((), ())), preferred_element_type=F32).astype(BF)
        for k in range(attention.shape[0] // rows):
            out_ref[places[q, k], places[2, k]] = mixed[k * rows : (k + 1) * rows]


def project(places, pieces, weights, shape):
    return pl.pallas_call(
        functools.partial(project_kernel, len(pieces)),
        out_shape=jax.ShapeDtypeStruct(shape, BF),
        in_specs=[whole(pltpu.SMEM)] + [whole()] * (len(pieces) + len(weights)),
        out_specs=whole(),
        compiler_params=params(),
        name="project",
    )(places, *pieces, *weights)


def pair_kernel(a_ref, b_ref, *outs):
    for d, out in enumerate(outs):
        out[...] = (a_ref[d].astype(F32) + b_ref[d].astype(F32)).astype(out.dtype)


def pair_sum(a, b):
    out = jax.ShapeDtypeStruct(a.shape[1:], BF)
    return pl.pallas_call(
        pair_kernel,
        out_shape=(out,) * a.shape[0],
        in_specs=[whole()] * 2,
        out_specs=(whole(),) * a.shape[0],
        compiler_params=params(),
        name="pair_sum",
    )(a, b)


def plan_kernel(rows_dev, ids_ref, gates_ref, sel_ref, mix_ref):
    rows, choose = ids_ref.shape
    slots_all = sel_ref.shape[1]
    slots = rows // rows_dev * CAP
    experts = slots_all // slots
    expert = lax.broadcasted_iota(I32, (rows, experts), 1)
    member = jnp.zeros((rows, experts), F32)
    gate = jnp.zeros((rows, experts), F32)
    for k in range(choose):
        same = ids_ref[:, k : k + 1] == expert
        member = jnp.where(same, 1.0, member)
        gate = jnp.where(same, gates_ref[:, k : k + 1], gate)
    to_row = lax.broadcasted_iota(I32, (rows, rows), 0)
    from_row = lax.broadcasted_iota(I32, (rows, rows), 1)
    before = (from_row < to_row) & (from_row // rows_dev == to_row // rows_dev)
    rank = jnp.dot(before.astype(F32).astype(BF), member.astype(BF), preferred_element_type=F32)
    block = lax.broadcasted_iota(I32, (rows, experts), 0) // rows_dev
    slot = jnp.where(member > 0, rank + (block * CAP).astype(F32), -1.0)
    spread = (
        lax.broadcasted_iota(I32, (experts, slots_all), 0)
        == lax.broadcasted_iota(I32, (experts, slots_all), 1) // slots
    ).astype(F32)
    slot_wide = jnp.dot(slot.astype(BF), spread.astype(BF), preferred_element_type=F32)
    gate_wide = jnp.dot(gate, spread, preferred_element_type=F32, precision=lax.Precision.HIGHEST)
    wanted = (lax.broadcasted_iota(I32, (rows, slots_all), 1) % slots).astype(F32)
    hit = slot_wide == wanted
    sel_ref[...] = jnp.where(hit, 1.0, 0.0).astype(BF)
    mix_ref[...] = jnp.where(hit, gate_wide, 0.0)


def plan(ids, gates, rows_dev, experts):
    rows = ids.shape[0]
    slots_all = experts * (rows // rows_dev) * CAP
    return pl.pallas_call(
        functools.partial(plan_kernel, rows_dev),
        out_shape=(
            jax.ShapeDtypeStruct((rows, slots_all), BF),
            jax.ShapeDtypeStruct((rows, slots_all), F32),
        ),
        in_specs=[whole()] * 2,
        out_specs=(whole(), whole()),
        compiler_params=params(),
        name="plan",
    )(ids, gates)


def dispatch_kernel(parts_ref, residual_ref, sel_ref, hidden_ref, out_ref):
    total = parts_ref[0].astype(F32)
    for k in range(1, parts_ref.shape[0]):
        total = total + parts_ref[k].astype(F32)
    hidden = (residual_ref[...].astype(F32) + total).astype(BF)
    hidden_ref[...] = hidden
    picked = lax.dot_general(sel_ref[...], hidden, (((0,), (0,)), ((), ())), preferred_element_type=F32)
    out_ref[...] = picked.reshape(out_ref.shape).astype(BF)


def dispatch(parts, residual, sel, experts):
    rows, columns = residual.shape
    return pl.pallas_call(
        dispatch_kernel,
        out_shape=(
            jax.ShapeDtypeStruct((rows, columns), BF),
            jax.ShapeDtypeStruct((experts, sel.shape[1] // experts, columns), BF),
        ),
        in_specs=[whole()] * 3,
        out_specs=(whole(), whole()),
        compiler_params=params(),
        name="dispatch",
    )(parts, residual, sel)


def norm_kernel(x_ref, gain_ref, out_ref):
    count = x_ref.shape[0]
    squares = 0.0
    for j in range(count):
        x = x_ref[j].astype(F32)
        squares = squares + x * x
    mean = jnp.sum(squares, axis=1, keepdims=True) / out_ref.shape[1]
    inverse = lax.rsqrt(mean + 1e-06)
    x = jnp.concatenate([x_ref[j].astype(F32) for j in range(count)], axis=1)
    out_ref[...] = (x * inverse * gain_ref[...].astype(F32)).astype(BF)


def normed_rows(x, gain):
    return pl.pallas_call(
        norm_kernel,
        out_shape=jax.ShapeDtypeStruct((x.shape[1], x.shape[0] * x.shape[2]), BF),
        in_specs=[whole()] * 2,
        out_specs=whole(),
        compiler_params=params(),
        name="norm",
    )(x, gain)


def units_kernel(layout, *refs):
    count = sum(layout)
    x_refs, (gate_ref, up_ref, act_ref) = refs[:count], refs[count:]
    blocks, at = [], 0
    for parts in layout:
        blocks.append(jnp.concatenate([x_refs[at + p][...] for p in range(parts)], axis=1))
        at += parts
    x = jnp.concatenate(blocks, axis=0)
    gate = jnp.dot(x, gate_ref[...], preferred_element_type=F32)
    up = jnp.dot(x, up_ref[...], preferred_element_type=F32)
    act_ref[...] = (gate * jax.nn.sigmoid(gate) * up).astype(BF)


def run_units(layout, pieces, w_gate, w_up):
    slots = pieces[0].shape[0] * len(layout)
    return pl.pallas_call(
        functools.partial(units_kernel, layout),
        out_shape=jax.ShapeDtypeStruct((slots, w_gate.shape[1]), BF),
        in_specs=[whole()] * (len(pieces) + 2),
        out_specs=whole(),
        compiler_params=params(),
        name="units",
    )(*pieces, w_gate, w_up)


def down_kernel(*refs):
    ring = len(refs) // 2 - 1
    acts, downs, outs = refs[:ring], refs[ring : 2 * ring], refs[2 * ring :]
    slots = acts[0].shape[0] // (2 * ring)
    turned = []
    for d in range(ring):
        act = acts[d][...].astype(F32)
        order = [core * ring + (t + ring - d) % ring for core in range(2) for t in range(ring)]
        turned.append(jnp.concatenate([act[k * slots : (k + 1) * slots] for k in order], axis=0).astype(BF))
    units = jnp.concatenate(turned, axis=1)
    down = jnp.concatenate([w[...] for w in downs], axis=0)
    y = jnp.dot(units, down, preferred_element_type=F32).astype(BF)
    half = ring * slots
    for k, out in enumerate(outs):
        for t in range(ring):
            at = k * half + t * slots
            out[t] = y[at : at + slots]


def run_down(acts, downs):
    ring = len(acts)
    out = jax.ShapeDtypeStruct((ring, acts[0].shape[0] // (2 * ring), downs[0].shape[1]), BF)
    return pl.pallas_call(
        down_kernel,
        out_shape=(out, out),
        in_specs=[whole()] * (2 * ring),
        out_specs=(whole(), whole()),
        compiler_params=params(),
        name="down",
    )(*acts, *downs)


def columns_kernel(at, *refs):
    pieces, out_ref = refs[:-1], refs[-1]
    ring = len(pieces)
    each, width = out_ref.shape[0] // ring, out_ref.shape[2]
    for t, piece in enumerate(pieces):
        first = lax.rem(at[0] + t, ring) * each
        values = piece[...].astype(F32)
        for j in range(each):
            out_ref[first + j] = values[:, j * width : (j + 1) * width].astype(BF)


def by_columns(at, pieces, parts):
    slots, width = pieces[0].shape
    return pl.pallas_call(
        columns_kernel,
        out_shape=jax.ShapeDtypeStruct((parts, slots, width * len(pieces) // parts), BF),
        in_specs=[whole(pltpu.SMEM)] + [whole()] * len(pieces),
        out_specs=whole(),
        compiler_params=params(),
        name="by_columns",
    )(at, *pieces)


def combine_kernel(back_ref, mix_ref, hidden_ref, out_ref):
    back = back_ref[...].astype(F32).reshape(-1, back_ref.shape[2])
    routed = jnp.dot(mix_ref[...], back, preferred_element_type=F32, precision=lax.Precision.HIGHEST)
    out_ref[...] = (hidden_ref[...].astype(F32) + routed).astype(BF)


def combine(back, mix, hidden):
    return pl.pallas_call(
        combine_kernel,
        out_shape=jax.ShapeDtypeStruct(hidden.shape, BF),
        in_specs=[whole()] * 3,
        out_specs=whole(),
        compiler_params=params(),
        name="combine",
    )(back, mix, hidden)


def exchange(x, axes):
    return lax.all_to_all(x, axes, split_axis=0, concat_axis=0, tiled=True)


def gather_over_head(x):
    near = ring_gather(x, HEAD[0], 1)
    layout = [len(p) if isinstance(p, tuple) else 1 for p in near]
    near = flat(near)
    far = [shifted(p, HEAD[1], 1) for p in near]
    return tuple(layout * 2), near + far


def per_device(
    queries,
    resident_cache,
    resident_len,
    new_cache,
    new_len,
    new_owner,
    value_up,
    w_output,
    residual,
    expert_ids,
    expert_gates,
    norm_gain,
    w_gate,
    w_up,
    w_down,
):
    n_expert = lax.axis_size(EXPERT)
    n_head = lax.axis_size(HEAD)
    n_z, n_y = lax.axis_size(EXPERT[0]), lax.axis_size(COLUMN)
    z, y = lax.axis_index(EXPERT[0]), lax.axis_index(COLUMN)
    me = lax.axis_index(EXPERT)
    head = lax.axis_index(HEAD)
    req_count = resident_cache.shape[0]
    new_count = new_cache.shape[0]
    rows_dev = req_count + new_count
    rows_all = rows_dev * n_expert
    block_rows = rows_all // n_head
    columns = residual.shape[1]
    news = new_owner.shape[0]

    x, core = lax.axis_index(HEAD[0]), lax.axis_index(HEAD[1])
    ring = lax.axis_size(HEAD[0])
    number = jnp.arange(news, dtype=I32)
    equal = (new_owner[:, None] == new_owner[None, :]) & (number[None, :] < number[:, None])
    place = jnp.sum(equal.astype(I32), axis=1)
    mine = jnp.arange(new_count, dtype=I32)
    taken = (new_owner == me)[None, :] & (place[None, :] == mine[:, None])
    sources = jnp.sum(jnp.where(taken, (number // new_count)[None, :], 0), axis=1)[::MOST]
    lens = jnp.sum(jnp.where(taken, new_len[None, :], 0), axis=1)
    at = jnp.stack([x, core, y % 2]).astype(I32)

    packed = pack_cache(new_owner, new_cache, new_cache.shape[1] // ring, n_expert)
    resident = attend(queries[:req_count], jnp.swapaxes(resident_cache, 1, 2), resident_len, value_up)
    arrived, resident = lax.optimization_barrier((exchange(packed, EXPERT), resident))
    ours = select_arrived(sources, arrived)
    near = [ours] + [shifted(ours, HEAD[0], d) for d in range(1, ring)]
    pieces = near + [shifted(p, HEAD[1], 1) for p in near]
    attention = new_attention(lens, at, queries, value_up, resident, pieces, 2)

    w_t = w_output.T
    width = w_t.shape[1] // 2
    group = lambda d: lax.dynamic_slice_in_dim(w_t, ((y + d) % 2) * width, width, 1)
    weights = [group(0), across(group(1), COLUMN, 1)]
    along_y = list(attention[:1]) + [across(attention[d % 2], COLUMN, d) for d in range(1, n_y)]
    rows_here = flat(ring_gather(stacked(along_y), EXPERT[0], 0))
    w_d = w_down.reshape(w_down.shape[1:])
    part = w_d.shape[1] // ring
    some = lambda d: lax.dynamic_slice_in_dim(w_d, ((x + d) % ring) * part, part, 1)
    downs = [some(0)] + [shifted(some(d), HEAD[0], d) for d in range(1, ring)]
    downs, rows_here = lax.optimization_barrier((downs, rows_here))
    away = jnp.arange(n_expert, dtype=I32)
    maker_z = (z + n_z - away // n_y) % n_z
    maker_y = y ^ (away % n_y)
    per_head = n_expert // n_head
    maker_head = (maker_z * n_y + maker_y) // per_head
    places = jnp.stack([maker_head * 2 + y % 2, maker_head * 2 + (y + 1) % 2, (maker_z * n_y + maker_y) % per_head])
    mixed = project(places, rows_here, weights, (2 * n_head, per_head, rows_dev, columns))
    parts = exchange(mixed.reshape(2 * n_head, block_rows, columns), HEAD + COLUMN[1:])

    block = lambda a: lax.dynamic_slice_in_dim(a, head * block_rows, block_rows)
    sel, mix = plan(block(expert_ids), block(expert_gates), rows_dev, n_expert)
    hidden, outgoing = dispatch(parts, block(residual), sel, n_expert)
    received = exchange(outgoing, EXPERT)
    normed = normed_rows(received, norm_gain.reshape(1, -1))
    layout, pieces = gather_over_head(normed)
    act = run_units(layout, pieces, w_gate.reshape(w_gate.shape[1:]), w_up.reshape(w_up.shape[1:]))
    acts = [act] + [shifted(act, HEAD[0], d) for d in range(1, ring)]
    kept, sent = run_down(acts, downs)
    made = pair_sum(kept, shifted(sent, HEAD[1], 1))
    made = list(made[:1]) + [shifted(made[t], HEAD[0], -t) for t in range(1, ring)]
    back = exchange(by_columns(at, made, n_expert), EXPERT)
    return combine(back, mix, hidden)


def solution(mesh):
    finer = Mesh(mesh.devices.reshape(4, 2, 8, 2, 2), HEAD + EXPERT)
    in_specs = (
        P(EXPERT, HEAD, None),
        P(EXPERT, None, None),
        P(EXPERT),
        P(EXPERT, None, None),
        P(),
        P(),
        P(HEAD, None, None),
        P(HEAD, EXPERT),
        P(None, EXPERT),
        P(),
        P(),
        P(),
        P(EXPERT, None, HEAD),
        P(EXPERT, None, HEAD),
        P(EXPERT, HEAD, None),
    )
    out_specs = P(HEAD, EXPERT)
    return jax.shard_map(
        per_device, mesh=finer, in_specs=in_specs, out_specs=out_specs, check_vma=False
    )
```

```python
import functools

import jax
import jax.numpy as jnp
from jax import lax
from jax.experimental import pallas as pl
from jax.experimental.pallas import tpu as pltpu
from jax.sharding import Mesh
from jax.sharding import PartitionSpec as P

ROPE = 64
NOPE = 128
EXPERT = ("expert_0", "expert_1", "expert_2")
COLUMN = EXPERT[1:]
HEAD = ("head_0", "head_1")
MOST = 2
CAP = 6
BF = jnp.bfloat16
F32 = jnp.float32
I32 = jnp.int32
VMEM_BYTES = 24 * 1024 * 1024


def params():
    return pltpu.CompilerParams(vmem_limit_bytes=VMEM_BYTES)


def whole(memory=pltpu.VMEM):
    return pl.BlockSpec(memory_space=memory)


def shifted(x, axis, step):
    n = lax.axis_size(axis)
    return lax.ppermute(x, axis, [(i, (i + step) % n) for i in range(n)])


def across(x, axis, mask):
    return lax.ppermute(x, axis, [(i, i ^ mask) for i in range(lax.axis_size(axis))])


def ring_gather(x, axis, dim):
    n = lax.axis_size(axis)
    far = n // 2
    cut = x.shape[dim] // 2
    found = {0: x}
    right, left = x, x
    for step in range(1, far):
        right, left = shifted(right, axis, 1), shifted(left, axis, -1)
        found[step], found[n - step] = right, left
    low = lax.slice_in_dim(right, 0, cut, axis=dim)
    high = lax.slice_in_dim(left, cut, x.shape[dim], axis=dim)
    found[far] = (shifted(low, axis, 1), shifted(high, axis, -1))
    return [found[d] for d in range(n)]


def flat(pieces):
    out = []
    for piece in pieces:
        out.extend(piece if isinstance(piece, tuple) else (piece,))
    return out


def attend(queries, caches_t, length, value_up):
    inverse_root = (NOPE + ROPE) ** (-0.5)
    latent_width = value_up.shape[1]
    scores = jnp.einsum("rhc,rct->rht", queries, caches_t, preferred_element_type=F32) * inverse_root
    inside = lax.broadcasted_iota(I32, scores.shape, 2) < length[:, None, None]
    scores = jnp.where(inside, scores, -jnp.inf)
    highest = jnp.max(scores, axis=2, keepdims=True)
    raised = jnp.exp(scores - highest)
    weights = (raised / jnp.sum(raised, axis=2, keepdims=True)).astype(BF)
    latent = jnp.einsum("rht,rct->rhc", weights, caches_t[:, :latent_width], preferred_element_type=F32).astype(BF)
    return jnp.einsum("rhc,hcv->hrv", latent, value_up, preferred_element_type=F32).astype(BF)


def pack_kernel(owners, cache_ref, out_ref, sems):
    count, span = cache_ref.shape[0], out_ref.shape[1]
    place, core = lax.axis_index(HEAD[0]), lax.axis_index(HEAD[1])
    base = lax.axis_index(EXPERT) * count
    first = pl.multiple_of(place * span, span)
    owner = [owners[base + i] for i in range(count)]
    turn = []
    for i in range(count):
        earlier = jnp.int32(0)
        for j in range(i):
            earlier = earlier + (owner[j] == owner[i]).astype(I32)
        turn.append(earlier)

    def copy(i):
        return pltpu.make_async_copy(
            cache_ref.at[i, pl.ds(first, span)], out_ref.at[owner[i]], sems.at[i]
        )

    for i in range(count):

        @pl.when(turn[i] == core)
        def _():
            copy(i).start()

    for i in range(count):

        @pl.when(turn[i] == core)
        def _():
            copy(i).wait()


def pack_cache(owners, cache, span, n_expert):
    return pl.pallas_call(
        pack_kernel,
        out_shape=jax.ShapeDtypeStruct((n_expert, span, cache.shape[2]), cache.dtype),
        in_specs=[whole(pltpu.SMEM), whole(pl.ANY)],
        out_specs=whole(pl.ANY),
        scratch_shapes=[pltpu.SemaphoreType.DMA((cache.shape[0],))],
        compiler_params=params(),
        name="pack_cache",
    )(owners, cache)


def select_kernel(sources, arrived_ref, out_ref, sems):
    copies = [
        pltpu.make_async_copy(arrived_ref.at[sources[k]], out_ref.at[k], sems.at[k])
        for k in range(out_ref.shape[0])
    ]
    for copy in copies:
        copy.start()
    for copy in copies:
        copy.wait()


def select_arrived(sources, arrived):
    count = sources.shape[0]
    return pl.pallas_call(
        select_kernel,
        out_shape=jax.ShapeDtypeStruct((count,) + arrived.shape[1:], arrived.dtype),
        in_specs=[whole(pltpu.SMEM), whole(pl.ANY)],
        out_specs=whole(pl.ANY),
        scratch_shapes=[pltpu.SemaphoreType.DMA((count,))],
        compiler_params=params(),
        name="select_arrived",
    )(sources, arrived)


def new_attention_kernel(groups, lens, at, q_ref, up_ref, res_ref, near_ref, far_ref, *refs):
    out_refs, latents = refs[:-1], refs[-1]
    ring, pairs, span = near_ref.shape[:3]
    old = res_ref.shape[1]
    count = pairs * MOST
    heads, latent_width, value_width = up_ref.shape
    inverse_root = (NOPE + ROPE) ** (-0.5)
    place, core, row = at[0], at[1], at[2]
    column = lax.broadcasted_iota(I32, (heads, ring * span), 1)
    position = ((place + ring - column // span) % ring) * span + column % span
    for i in range(count):
        k, turn = i // MOST, i % MOST
        ours = core == turn
        cache = jnp.concatenate(
            [jnp.where(ours, near_ref[d, k], far_ref[d, k]) for d in range(ring)], axis=0
        )
        scores = (
            lax.dot_general(q_ref[old + i], cache, (((1,), (1,)), ((), ())), preferred_element_type=F32)
            * inverse_root
        )
        scores = jnp.where(position < lens[i], scores, -jnp.inf)
        raised = jnp.exp(scores - jnp.max(scores, axis=1, keepdims=True))
        weights = (raised / jnp.sum(raised, axis=1, keepdims=True)).astype(BF)
        latents[:, i, :] = jnp.dot(weights, cache[:, :latent_width], preferred_element_type=F32)
    each = heads // groups
    for d, out_ref in enumerate(out_refs):
        for k in range(each):
            h = lax.rem(row + d, groups) * each + k
            values = jnp.dot(latents[h].astype(BF), up_ref[h], preferred_element_type=F32)
            rows = jnp.concatenate([res_ref[h].astype(F32), values[:count]], axis=0).astype(BF)
            out_ref[:, k * value_width : (k + 1) * value_width] = rows


def new_attention(lens, at, queries, value_up, resident, near, far, groups):
    heads, latent_width, value_width = value_up.shape
    rows = queries.shape[0]
    out = jax.ShapeDtypeStruct((rows, heads // groups * value_width), BF)
    return pl.pallas_call(
        functools.partial(new_attention_kernel, groups),
        out_shape=(out,) * groups,
        in_specs=[whole(pltpu.SMEM)] * 2 + [whole()] * 5,
        out_specs=(whole(),) * groups,
        scratch_shapes=[pltpu.VMEM((heads, rows, latent_width), F32)],
        compiler_params=params(),
        name="new_attention",
    )(lens, at, queries, value_up, resident, near, far)


def stack_kernel(*refs):
    rows = refs[0].shape[0]
    for k, ref in enumerate(refs[:-1]):
        refs[-1][k * rows : (k + 1) * rows, :] = ref[...]


def stacked(pieces):
    rows, width = pieces[0].shape
    return pl.pallas_call(
        stack_kernel,
        out_shape=jax.ShapeDtypeStruct((rows * len(pieces), width), pieces[0].dtype),
        in_specs=[whole()] * len(pieces),
        out_specs=whole(),
        compiler_params=params(),
        name="stack",
    )(*pieces)


def layers_kernel(*refs):
    for k, ref in enumerate(refs[:-1]):
        refs[-1][k] = ref[...]


def layers(pieces):
    return pl.pallas_call(
        layers_kernel,
        out_shape=jax.ShapeDtypeStruct((len(pieces),) + pieces[0].shape, pieces[0].dtype),
        in_specs=[whole()] * len(pieces),
        out_specs=whole(),
        compiler_params=params(),
        name="layers",
    )(*pieces)


def project_kernel(count, places, *refs):
    pieces, weights, out_ref = refs[:count], refs[count:-1], refs[-1]
    rows = out_ref.shape[2]
    attention = jnp.concatenate([piece[...] for piece in pieces], axis=0)
    for q, w in enumerate(weights):
        mixed = lax.dot_general(attention, w[...], (((1,), (1,)), ((), ())), preferred_element_type=F32).astype(BF)
        for k in range(attention.shape[0] // rows):
            out_ref[places[q, k], places[2, k]] = mixed[k * rows : (k + 1) * rows]


def project(places, pieces, weights, shape):
    return pl.pallas_call(
        functools.partial(project_kernel, len(pieces)),
        out_shape=jax.ShapeDtypeStruct(shape, BF),
        in_specs=[whole(pltpu.SMEM)] + [whole()] * (len(pieces) + len(weights)),
        out_specs=whole(),
        compiler_params=params(),
        name="project",
    )(places, *pieces, *weights)


def pair_kernel(a_ref, b_ref, *outs):
    for d, out in enumerate(outs):
        out[...] = (a_ref[d].astype(F32) + b_ref[d].astype(F32)).astype(out.dtype)


def pair_sum(a, b):
    out = jax.ShapeDtypeStruct(a.shape[1:], BF)
    return pl.pallas_call(
        pair_kernel,
        out_shape=(out,) * a.shape[0],
        in_specs=[whole()] * 2,
        out_specs=(whole(),) * a.shape[0],
        compiler_params=params(),
        name="pair_sum",
    )(a, b)


def plan_kernel(rows_dev, ids_ref, gates_ref, sel_ref, mix_ref):
    rows, choose = ids_ref.shape
    slots_all = sel_ref.shape[1]
    slots = rows // rows_dev * CAP
    experts = slots_all // slots
    expert = lax.broadcasted_iota(I32, (rows, experts), 1)
    member = jnp.zeros((rows, experts), F32)
    gate = jnp.zeros((rows, experts), F32)
    for k in range(choose):
        same = ids_ref[:, k : k + 1] == expert
        member = jnp.where(same, 1.0, member)
        gate = jnp.where(same, gates_ref[:, k : k + 1], gate)
    to_row = lax.broadcasted_iota(I32, (rows, rows), 0)
    from_row = lax.broadcasted_iota(I32, (rows, rows), 1)
    before = (from_row < to_row) & (from_row // rows_dev == to_row // rows_dev)
    rank = jnp.dot(before.astype(F32).astype(BF), member.astype(BF), preferred_element_type=F32)
    block = lax.broadcasted_iota(I32, (rows, experts), 0) // rows_dev
    slot = jnp.where(member > 0, rank + (block * CAP).astype(F32), -1.0)
    spread = (
        lax.broadcasted_iota(I32, (experts, slots_all), 0)
        == lax.broadcasted_iota(I32, (experts, slots_all), 1) // slots
    ).astype(F32)
    slot_wide = jnp.dot(slot.astype(BF), spread.astype(BF), preferred_element_type=F32)
    gate_wide = jnp.dot(gate, spread, preferred_element_type=F32, precision=lax.Precision.HIGHEST)
    wanted = (lax.broadcasted_iota(I32, (rows, slots_all), 1) % slots).astype(F32)
    hit = slot_wide == wanted
    sel_ref[...] = jnp.where(hit, 1.0, 0.0).astype(BF)
    mix_ref[...] = jnp.where(hit, gate_wide, 0.0)


def plan(ids, gates, rows_dev, experts):
    rows = ids.shape[0]
    slots_all = experts * (rows // rows_dev) * CAP
    return pl.pallas_call(
        functools.partial(plan_kernel, rows_dev),
        out_shape=(
            jax.ShapeDtypeStruct((rows, slots_all), BF),
            jax.ShapeDtypeStruct((rows, slots_all), F32),
        ),
        in_specs=[whole()] * 2,
        out_specs=(whole(), whole()),
        compiler_params=params(),
        name="plan",
    )(ids, gates)


def dispatch_kernel(parts_ref, residual_ref, sel_ref, hidden_ref, out_ref):
    total = parts_ref[0].astype(F32)
    for k in range(1, parts_ref.shape[0]):
        total = total + parts_ref[k].astype(F32)
    hidden = (residual_ref[...].astype(F32) + total).astype(BF)
    hidden_ref[...] = hidden
    picked = lax.dot_general(sel_ref[...], hidden, (((0,), (0,)), ((), ())), preferred_element_type=F32)
    out_ref[...] = picked.reshape(out_ref.shape).astype(BF)


def dispatch(parts, residual, sel, experts):
    rows, columns = residual.shape
    return pl.pallas_call(
        dispatch_kernel,
        out_shape=(
            jax.ShapeDtypeStruct((rows, columns), BF),
            jax.ShapeDtypeStruct((experts, sel.shape[1] // experts, columns), BF),
        ),
        in_specs=[whole()] * 3,
        out_specs=(whole(), whole()),
        compiler_params=params(),
        name="dispatch",
    )(parts, residual, sel)


def norm_kernel(x_ref, gain_ref, out_ref):
    count = x_ref.shape[0]
    squares = 0.0
    for j in range(count):
        x = x_ref[j].astype(F32)
        squares = squares + x * x
    mean = jnp.sum(squares, axis=1, keepdims=True) / out_ref.shape[1]
    inverse = lax.rsqrt(mean + 1e-06)
    x = jnp.concatenate([x_ref[j].astype(F32) for j in range(count)], axis=1)
    out_ref[...] = (x * inverse * gain_ref[...].astype(F32)).astype(BF)


def normed_rows(x, gain):
    return pl.pallas_call(
        norm_kernel,
        out_shape=jax.ShapeDtypeStruct((x.shape[1], x.shape[0] * x.shape[2]), BF),
        in_specs=[whole()] * 2,
        out_specs=whole(),
        compiler_params=params(),
        name="norm",
    )(x, gain)


def units_kernel(layout, *refs):
    count = sum(layout)
    x_refs, (gate_ref, up_ref, act_ref) = refs[:count], refs[count:]
    blocks, at = [], 0
    for parts in layout:
        blocks.append(jnp.concatenate([x_refs[at + p][...] for p in range(parts)], axis=1))
        at += parts
    x = jnp.concatenate(blocks, axis=0)
    gate = jnp.dot(x, gate_ref[...], preferred_element_type=F32)
    up = jnp.dot(x, up_ref[...], preferred_element_type=F32)
    act_ref[...] = (gate * jax.nn.sigmoid(gate) * up).astype(BF)


def run_units(layout, pieces, w_gate, w_up):
    slots = pieces[0].shape[0] * len(layout)
    return pl.pallas_call(
        functools.partial(units_kernel, layout),
        out_shape=jax.ShapeDtypeStruct((slots, w_gate.shape[1]), BF),
        in_specs=[whole()] * (len(pieces) + 2),
        out_specs=whole(),
        compiler_params=params(),
        name="units",
    )(*pieces, w_gate, w_up)


def down_kernel(*refs):
    ring = len(refs) // 2 - 1
    acts, downs, outs = refs[:ring], refs[ring : 2 * ring], refs[2 * ring :]
    slots = acts[0].shape[0] // (2 * ring)
    turned = []
    for d in range(ring):
        act = acts[d][...].astype(F32)
        order = [core * ring + (t + ring - d) % ring for core in range(2) for t in range(ring)]
        turned.append(jnp.concatenate([act[k * slots : (k + 1) * slots] for k in order], axis=0).astype(BF))
    units = jnp.concatenate(turned, axis=1)
    down = jnp.concatenate([w[...] for w in downs], axis=0)
    y = jnp.dot(units, down, preferred_element_type=F32).astype(BF)
    half = ring * slots
    for k, out in enumerate(outs):
        for t in range(ring):
            at = k * half + t * slots
            out[t] = y[at : at + slots]


def run_down(acts, downs):
    ring = len(acts)
    out = jax.ShapeDtypeStruct((ring, acts[0].shape[0] // (2 * ring), downs[0].shape[1]), BF)
    return pl.pallas_call(
        down_kernel,
        out_shape=(out, out),
        in_specs=[whole()] * (2 * ring),
        out_specs=(whole(), whole()),
        compiler_params=params(),
        name="down",
    )(*acts, *downs)


def columns_kernel(at, *refs):
    pieces, out_ref = refs[:-1], refs[-1]
    ring = len(pieces)
    each, width = out_ref.shape[0] // ring, out_ref.shape[2]
    for t, piece in enumerate(pieces):
        first = lax.rem(at[0] + t, ring) * each
        values = piece[...].astype(F32)
        for j in range(each):
            out_ref[first + j] = values[:, j * width : (j + 1) * width].astype(BF)


def by_columns(at, pieces, parts):
    slots, width = pieces[0].shape
    return pl.pallas_call(
        columns_kernel,
        out_shape=jax.ShapeDtypeStruct((parts, slots, width * len(pieces) // parts), BF),
        in_specs=[whole(pltpu.SMEM)] + [whole()] * len(pieces),
        out_specs=whole(),
        compiler_params=params(),
        name="by_columns",
    )(at, *pieces)


def combine_kernel(back_ref, mix_ref, hidden_ref, out_ref):
    back = back_ref[...].astype(F32).reshape(-1, back_ref.shape[2])
    routed = jnp.dot(mix_ref[...], back, preferred_element_type=F32, precision=lax.Precision.HIGHEST)
    out_ref[...] = (hidden_ref[...].astype(F32) + routed).astype(BF)


def combine(back, mix, hidden):
    return pl.pallas_call(
        combine_kernel,
        out_shape=jax.ShapeDtypeStruct(hidden.shape, BF),
        in_specs=[whole()] * 3,
        out_specs=whole(),
        compiler_params=params(),
        name="combine",
    )(back, mix, hidden)


def exchange(x, axes):
    return lax.all_to_all(x, axes, split_axis=0, concat_axis=0, tiled=True)


def gather_over_head(x):
    near = ring_gather(x, HEAD[0], 1)
    layout = [len(p) if isinstance(p, tuple) else 1 for p in near]
    near = flat(near)
    far = [shifted(p, HEAD[1], 1) for p in near]
    return tuple(layout * 2), near + far


def per_device(
    queries,
    resident_cache,
    resident_len,
    new_cache,
    new_len,
    new_owner,
    value_up,
    w_output,
    residual,
    expert_ids,
    expert_gates,
    norm_gain,
    w_gate,
    w_up,
    w_down,
):
    n_expert = lax.axis_size(EXPERT)
    n_head = lax.axis_size(HEAD)
    n_z, n_y = lax.axis_size(EXPERT[0]), lax.axis_size(COLUMN)
    z, y = lax.axis_index(EXPERT[0]), lax.axis_index(COLUMN)
    me = lax.axis_index(EXPERT)
    head = lax.axis_index(HEAD)
    req_count = resident_cache.shape[0]
    new_count = new_cache.shape[0]
    rows_dev = req_count + new_count
    rows_all = rows_dev * n_expert
    block_rows = rows_all // n_head
    columns = residual.shape[1]
    news = new_owner.shape[0]

    x, core = lax.axis_index(HEAD[0]), lax.axis_index(HEAD[1])
    ring = lax.axis_size(HEAD[0])
    number = jnp.arange(news, dtype=I32)
    equal = (new_owner[:, None] == new_owner[None, :]) & (number[None, :] < number[:, None])
    place = jnp.sum(equal.astype(I32), axis=1)
    mine = jnp.arange(new_count, dtype=I32)
    taken = (new_owner == me)[None, :] & (place[None, :] == mine[:, None])
    sources = jnp.sum(jnp.where(taken, (number // new_count)[None, :], 0), axis=1)[::MOST]
    lens = jnp.sum(jnp.where(taken, new_len[None, :], 0), axis=1)
    at = jnp.stack([x, core, y % 2]).astype(I32)

    packed = pack_cache(new_owner, new_cache, new_cache.shape[1] // ring, n_expert)
    resident = attend(queries[:req_count], jnp.swapaxes(resident_cache, 1, 2), resident_len, value_up)

    packed, w_t, w_d = lax.optimization_barrier((packed, w_output.T, w_down.reshape(w_down.shape[1:])))
    width, part = w_t.shape[1] // 2, w_d.shape[1] // ring
    group = lambda d: lax.dynamic_slice_in_dim(w_t, ((y + d) % 2) * width, width, 1)
    weights = [group(0), across(group(1), COLUMN, 1)]
    downs = [lax.dynamic_slice_in_dim(w_d, ((x + d) % ring) * part, part, 1) for d in range(ring)]
    for d in (1, 3):
        downs[d] = shifted(downs[d], HEAD[0], d)
    arrived, resident, weights, downs = lax.optimization_barrier(
        (exchange(packed, EXPERT), resident, weights, downs)
    )
    ours = select_arrived(sources, arrived)
    near = layers([ours] + [shifted(ours, HEAD[0], d) for d in range(1, ring)])
    attention = new_attention(lens, at, queries, value_up, resident, near, shifted(near, HEAD[1], 1), 2)
    along_y = list(attention[:1]) + [across(attention[d % 2], COLUMN, d) for d in range(1, n_y)]
    rows_here = flat(ring_gather(stacked(along_y), EXPERT[0], 0))
    downs[2] = shifted(downs[2], HEAD[0], 2)
    block = lambda a: lax.dynamic_slice_in_dim(a, head * block_rows, block_rows)
    planned = plan(block(expert_ids), block(expert_gates), rows_dev, n_expert)
    downs, rows_here, (sel, mix), kept = lax.optimization_barrier((downs, rows_here, planned, block(residual)))
    away = jnp.arange(n_expert, dtype=I32)
    maker_z = (z + n_z - away // n_y) % n_z
    maker_y = y ^ (away % n_y)
    per_head = n_expert // n_head
    maker_head = (maker_z * n_y + maker_y) // per_head
    places = jnp.stack([maker_head * 2 + y % 2, maker_head * 2 + (y + 1) % 2, (maker_z * n_y + maker_y) % per_head])
    mixed = project(places, rows_here, weights, (2 * n_head, per_head, rows_dev, columns))
    parts = exchange(mixed.reshape(2 * n_head, block_rows, columns), HEAD + COLUMN[1:])

    hidden, outgoing = dispatch(parts, kept, sel, n_expert)
    received = exchange(outgoing, EXPERT)
    normed = normed_rows(received, norm_gain.reshape(1, -1))
    layout, pieces = gather_over_head(normed)
    act = run_units(layout, pieces, w_gate.reshape(w_gate.shape[1:]), w_up.reshape(w_up.shape[1:]))
    acts = [act] + [shifted(act, HEAD[0], d) for d in range(1, ring)]
    kept, sent = run_down(acts, downs)
    made = pair_sum(kept, shifted(sent, HEAD[1], 1))
    made = list(made[:1]) + [shifted(made[t], HEAD[0], -t) for t in range(1, ring)]
    back = exchange(by_columns(at, made, n_expert), EXPERT)
    return combine(back, mix, hidden)


def solution(mesh):
    finer = Mesh(mesh.devices.reshape(4, 2, 8, 2, 2), HEAD + EXPERT)
    in_specs = (
        P(EXPERT, HEAD, None),
        P(EXPERT, None, None),
        P(EXPERT),
        P(EXPERT, None, None),
        P(),
        P(),
        P(HEAD, None, None),
        P(HEAD, EXPERT),
        P(None, EXPERT),
        P(),
        P(),
        P(),
        P(EXPERT, None, HEAD),
        P(EXPERT, None, HEAD),
        P(EXPERT, HEAD, None),
    )
    out_specs = P(HEAD, EXPERT)
    return jax.shard_map(
        per_device, mesh=finer, in_specs=in_specs, out_specs=out_specs, check_vma=False
    )
```

```python
import functools

import jax
import jax.numpy as jnp
from jax import lax
from jax.experimental import pallas as pl
from jax.experimental.pallas import tpu as pltpu
from jax.sharding import Mesh
from jax.sharding import PartitionSpec as P

ROPE = 64
NOPE = 128
EXPERT = ("expert_0", "expert_1", "expert_2")
COLUMN = EXPERT[1:]
HEAD = ("head_0", "head_1")
MOST = 2
CAP = 6
BF = jnp.bfloat16
F32 = jnp.float32
I32 = jnp.int32
VMEM_BYTES = 24 * 1024 * 1024


def params():
    return pltpu.CompilerParams(vmem_limit_bytes=VMEM_BYTES)


def whole(memory=pltpu.VMEM):
    return pl.BlockSpec(memory_space=memory)


def shifted(x, axis, step):
    n = lax.axis_size(axis)
    return lax.ppermute(x, axis, [(i, (i + step) % n) for i in range(n)])


def across(x, axis, mask):
    return lax.ppermute(x, axis, [(i, i ^ mask) for i in range(lax.axis_size(axis))])


def ring_gather(x, axis, dim):
    n = lax.axis_size(axis)
    far = n // 2
    cut = x.shape[dim] // 2
    found = {0: x}
    right, left = x, x
    for step in range(1, far):
        right, left = shifted(right, axis, 1), shifted(left, axis, -1)
        found[step], found[n - step] = right, left
    low = lax.slice_in_dim(right, 0, cut, axis=dim)
    high = lax.slice_in_dim(left, cut, x.shape[dim], axis=dim)
    found[far] = (shifted(low, axis, 1), shifted(high, axis, -1))
    return [found[d] for d in range(n)]


def flat(pieces):
    out = []
    for piece in pieces:
        out.extend(piece if isinstance(piece, tuple) else (piece,))
    return out


def attend(queries, caches_t, length, value_up):
    inverse_root = (NOPE + ROPE) ** (-0.5)
    latent_width = value_up.shape[1]
    scores = jnp.einsum("rhc,rct->rht", queries, caches_t, preferred_element_type=F32) * inverse_root
    inside = lax.broadcasted_iota(I32, scores.shape, 2) < length[:, None, None]
    scores = jnp.where(inside, scores, -jnp.inf)
    highest = jnp.max(scores, axis=2, keepdims=True)
    raised = jnp.exp(scores - highest)
    weights = (raised / jnp.sum(raised, axis=2, keepdims=True)).astype(BF)
    latent = jnp.einsum("rht,rct->rhc", weights, caches_t[:, :latent_width], preferred_element_type=F32).astype(BF)
    return jnp.einsum("rhc,hcv->hrv", latent, value_up, preferred_element_type=F32).astype(BF)


def pack_kernel(owners, cache_ref, out_ref, sems):
    count, span = cache_ref.shape[0], out_ref.shape[1]
    place, core = lax.axis_index(HEAD[0]), lax.axis_index(HEAD[1])
    base = lax.axis_index(EXPERT) * count
    first = pl.multiple_of(place * span, span)
    owner = [owners[base + i] for i in range(count)]
    turn = []
    for i in range(count):
        earlier = jnp.int32(0)
        for j in range(i):
            earlier = earlier + (owner[j] == owner[i]).astype(I32)
        turn.append(earlier)

    def copy(i):
        return pltpu.make_async_copy(
            cache_ref.at[i, pl.ds(first, span)], out_ref.at[owner[i]], sems.at[i]
        )

    for i in range(count):

        @pl.when(turn[i] == core)
        def _():
            copy(i).start()

    for i in range(count):

        @pl.when(turn[i] == core)
        def _():
            copy(i).wait()


def pack_cache(owners, cache, span, n_expert):
    return pl.pallas_call(
        pack_kernel,
        out_shape=jax.ShapeDtypeStruct((n_expert, span, cache.shape[2]), cache.dtype),
        in_specs=[whole(pltpu.SMEM), whole(pl.ANY)],
        out_specs=whole(pl.ANY),
        scratch_shapes=[pltpu.SemaphoreType.DMA((cache.shape[0],))],
        compiler_params=params(),
        name="pack_cache",
    )(owners, cache)


def select_kernel(sources, arrived_ref, out_ref, sems):
    copies = [
        pltpu.make_async_copy(arrived_ref.at[sources[k]], out_ref.at[k], sems.at[k])
        for k in range(out_ref.shape[0])
    ]
    for copy in copies:
        copy.start()
    for copy in copies:
        copy.wait()


def select_arrived(sources, arrived):
    count = sources.shape[0]
    return pl.pallas_call(
        select_kernel,
        out_shape=jax.ShapeDtypeStruct((count,) + arrived.shape[1:], arrived.dtype),
        in_specs=[whole(pltpu.SMEM), whole(pl.ANY)],
        out_specs=whole(pl.ANY),
        scratch_shapes=[pltpu.SemaphoreType.DMA((count,))],
        compiler_params=params(),
        name="select_arrived",
    )(sources, arrived)


def new_attention_kernel(groups, lens, at, q_ref, up_ref, res_ref, *refs):
    pieces, out_refs, latents = refs[: -groups - 1], refs[-groups - 1 : -1], refs[-1]
    ring = len(pieces) // 2
    pairs, span = pieces[0].shape[0], pieces[0].shape[1]
    old = res_ref.shape[1]
    count = pairs * MOST
    heads, latent_width, value_width = up_ref.shape
    inverse_root = (NOPE + ROPE) ** (-0.5)
    place, core, row = at[0], at[1], at[2]
    column = lax.broadcasted_iota(I32, (heads, ring * span), 1)
    position = ((place + ring - column // span) % ring) * span + column % span
    for i in range(count):
        k, turn = i // MOST, i % MOST
        ours = core == turn
        cache = jnp.concatenate(
            [jnp.where(ours, pieces[d][k], pieces[ring + d][k]) for d in range(ring)], axis=0
        )
        scores = (
            lax.dot_general(q_ref[old + i], cache, (((1,), (1,)), ((), ())), preferred_element_type=F32)
            * inverse_root
        )
        scores = jnp.where(position < lens[i], scores, -jnp.inf)
        raised = jnp.exp(scores - jnp.max(scores, axis=1, keepdims=True))
        weights = (raised / jnp.sum(raised, axis=1, keepdims=True)).astype(BF)
        latents[:, i, :] = jnp.dot(weights, cache[:, :latent_width], preferred_element_type=F32)
    each = heads // groups
    for d, out_ref in enumerate(out_refs):
        for k in range(each):
            h = k if groups == 1 else lax.rem(row + d, groups) * each + k
            values = jnp.dot(latents[h].astype(BF), up_ref[h], preferred_element_type=F32)
            rows = jnp.concatenate([res_ref[h].astype(F32), values[:count]], axis=0).astype(BF)
            out_ref[:, k * value_width : (k + 1) * value_width] = rows


def new_attention(lens, at, queries, value_up, resident, pieces, groups):
    heads, latent_width, value_width = value_up.shape
    rows = queries.shape[0]
    out = jax.ShapeDtypeStruct((rows, heads // groups * value_width), BF)
    return pl.pallas_call(
        functools.partial(new_attention_kernel, groups),
        out_shape=(out,) * groups,
        in_specs=[whole(pltpu.SMEM)] * 2 + [whole()] * (3 + len(pieces)),
        out_specs=(whole(),) * groups,
        scratch_shapes=[pltpu.VMEM((heads, rows, latent_width), F32)],
        compiler_params=params(),
        name="new_attention",
    )(lens, at, queries, value_up, resident, *pieces)


def stack_kernel(*refs):
    rows = refs[0].shape[0]
    for k, ref in enumerate(refs[:-1]):
        refs[-1][k * rows : (k + 1) * rows, :] = ref[...]


def stacked(pieces):
    rows, width = pieces[0].shape
    return pl.pallas_call(
        stack_kernel,
        out_shape=jax.ShapeDtypeStruct((rows * len(pieces), width), pieces[0].dtype),
        in_specs=[whole()] * len(pieces),
        out_specs=whole(),
        compiler_params=params(),
        name="stack",
    )(*pieces)


def project_kernel(makers, w_ref, *refs):
    pieces, out_ref = refs[:-1], refs[-1]
    rows = out_ref.shape[1]
    attention = jnp.concatenate([piece[...] for piece in pieces], axis=0)
    mixed = lax.dot_general(attention, w_ref[...], (((1,), (1,)), ((), ())), preferred_element_type=F32).astype(BF)
    for k in range(out_ref.shape[0]):
        out_ref[makers[k]] = mixed[k * rows : (k + 1) * rows]


def project(makers, w_output_t, pieces, rows):
    return pl.pallas_call(
        project_kernel,
        out_shape=jax.ShapeDtypeStruct((makers.shape[0], rows, w_output_t.shape[0]), BF),
        in_specs=[whole(pltpu.SMEM)] + [whole()] * (1 + len(pieces)),
        out_specs=whole(),
        compiler_params=params(),
        name="project",
    )(makers, w_output_t, *pieces)


def pair_kernel(a_ref, b_ref, *outs):
    for d, out in enumerate(outs):
        out[...] = (a_ref[d].astype(F32) + b_ref[d].astype(F32)).astype(out.dtype)


def pair_sum(a, b):
    out = jax.ShapeDtypeStruct(a.shape[1:], BF)
    return pl.pallas_call(
        pair_kernel,
        out_shape=(out,) * a.shape[0],
        in_specs=[whole()] * 2,
        out_specs=(whole(),) * a.shape[0],
        compiler_params=params(),
        name="pair_sum",
    )(a, b)


def plan_kernel(rows_dev, ids_ref, gates_ref, sel_ref, mix_ref):
    rows, choose = ids_ref.shape
    slots_all = sel_ref.shape[1]
    slots = rows // rows_dev * CAP
    experts = slots_all // slots
    expert = lax.broadcasted_iota(I32, (rows, experts), 1)
    member = jnp.zeros((rows, experts), F32)
    gate = jnp.zeros((rows, experts), F32)
    for k in range(choose):
        same = ids_ref[:, k : k + 1] == expert
        member = jnp.where(same, 1.0, member)
        gate = jnp.where(same, gates_ref[:, k : k + 1], gate)
    to_row = lax.broadcasted_iota(I32, (rows, rows), 0)
    from_row = lax.broadcasted_iota(I32, (rows, rows), 1)
    before = (from_row < to_row) & (from_row // rows_dev == to_row // rows_dev)
    rank = jnp.dot(before.astype(F32).astype(BF), member.astype(BF), preferred_element_type=F32)
    block = lax.broadcasted_iota(I32, (rows, experts), 0) // rows_dev
    slot = jnp.where(member > 0, rank + (block * CAP).astype(F32), -1.0)
    spread = (
        lax.broadcasted_iota(I32, (experts, slots_all), 0)
        == lax.broadcasted_iota(I32, (experts, slots_all), 1) // slots
    ).astype(F32)
    slot_wide = jnp.dot(slot.astype(BF), spread.astype(BF), preferred_element_type=F32)
    gate_wide = jnp.dot(gate, spread, preferred_element_type=F32, precision=lax.Precision.HIGHEST)
    wanted = (lax.broadcasted_iota(I32, (rows, slots_all), 1) % slots).astype(F32)
    hit = slot_wide == wanted
    sel_ref[...] = jnp.where(hit, 1.0, 0.0).astype(BF)
    mix_ref[...] = jnp.where(hit, gate_wide, 0.0)


def plan(ids, gates, rows_dev, experts):
    rows = ids.shape[0]
    slots_all = experts * (rows // rows_dev) * CAP
    return pl.pallas_call(
        functools.partial(plan_kernel, rows_dev),
        out_shape=(
            jax.ShapeDtypeStruct((rows, slots_all), BF),
            jax.ShapeDtypeStruct((rows, slots_all), F32),
        ),
        in_specs=[whole()] * 2,
        out_specs=(whole(), whole()),
        compiler_params=params(),
        name="plan",
    )(ids, gates)


def dispatch_kernel(parts_ref, residual_ref, sel_ref, hidden_ref, out_ref):
    total = parts_ref[0].astype(F32)
    for k in range(1, parts_ref.shape[0]):
        total = total + parts_ref[k].astype(F32)
    hidden = (residual_ref[...].astype(F32) + total).astype(BF)
    hidden_ref[...] = hidden
    picked = lax.dot_general(sel_ref[...], hidden, (((0,), (0,)), ((), ())), preferred_element_type=F32)
    out_ref[...] = picked.reshape(out_ref.shape).astype(BF)


def dispatch(parts, residual, sel, experts):
    rows, columns = residual.shape
    return pl.pallas_call(
        dispatch_kernel,
        out_shape=(
            jax.ShapeDtypeStruct((rows, columns), BF),
            jax.ShapeDtypeStruct((experts, sel.shape[1] // experts, columns), BF),
        ),
        in_specs=[whole()] * 3,
        out_specs=(whole(), whole()),
        compiler_params=params(),
        name="dispatch",
    )(parts, residual, sel)


def norm_kernel(x_ref, gain_ref, out_ref):
    count = x_ref.shape[0]
    squares = 0.0
    for j in range(count):
        x = x_ref[j].astype(F32)
        squares = squares + x * x
    mean = jnp.sum(squares, axis=1, keepdims=True) / out_ref.shape[1]
    inverse = lax.rsqrt(mean + 1e-06)
    x = jnp.concatenate([x_ref[j].astype(F32) for j in range(count)], axis=1)
    out_ref[...] = (x * inverse * gain_ref[...].astype(F32)).astype(BF)


def normed_rows(x, gain):
    return pl.pallas_call(
        norm_kernel,
        out_shape=jax.ShapeDtypeStruct((x.shape[1], x.shape[0] * x.shape[2]), BF),
        in_specs=[whole()] * 2,
        out_specs=whole(),
        compiler_params=params(),
        name="norm",
    )(x, gain)


def units_kernel(layout, *refs):
    count = sum(layout)
    x_refs, (gate_ref, up_ref, act_ref) = refs[:count], refs[count:]
    blocks, at = [], 0
    for parts in layout:
        blocks.append(jnp.concatenate([x_refs[at + p][...] for p in range(parts)], axis=1))
        at += parts
    x = jnp.concatenate(blocks, axis=0)
    gate = jnp.dot(x, gate_ref[...], preferred_element_type=F32)
    up = jnp.dot(x, up_ref[...], preferred_element_type=F32)
    act_ref[...] = (gate * jax.nn.sigmoid(gate) * up).astype(BF)


def run_units(layout, pieces, w_gate, w_up):
    slots = pieces[0].shape[0] * len(layout)
    return pl.pallas_call(
        functools.partial(units_kernel, layout),
        out_shape=jax.ShapeDtypeStruct((slots, w_gate.shape[1]), BF),
        in_specs=[whole()] * (len(pieces) + 2),
        out_specs=whole(),
        compiler_params=params(),
        name="units",
    )(*pieces, w_gate, w_up)


def down_kernel(*refs):
    ring = len(refs) // 2 - 1
    acts, downs, outs = refs[:ring], refs[ring : 2 * ring], refs[2 * ring :]
    slots = acts[0].shape[0] // (2 * ring)
    turned = []
    for d in range(ring):
        act = acts[d][...].astype(F32)
        order = [core * ring + (t + ring - d) % ring for core in range(2) for t in range(ring)]
        turned.append(jnp.concatenate([act[k * slots : (k + 1) * slots] for k in order], axis=0).astype(BF))
    units = jnp.concatenate(turned, axis=1)
    down = jnp.concatenate([w[...] for w in downs], axis=0)
    y = jnp.dot(units, down, preferred_element_type=F32).astype(BF)
    half = ring * slots
    for k, out in enumerate(outs):
        for t in range(ring):
            at = k * half + t * slots
            out[t] = y[at : at + slots]


def run_down(acts, downs):
    ring = len(acts)
    out = jax.ShapeDtypeStruct((ring, acts[0].shape[0] // (2 * ring), downs[0].shape[1]), BF)
    return pl.pallas_call(
        down_kernel,
        out_shape=(out, out),
        in_specs=[whole()] * (2 * ring),
        out_specs=(whole(), whole()),
        compiler_params=params(),
        name="down",
    )(*acts, *downs)


def columns_kernel(at, *refs):
    pieces, out_ref = refs[:-1], refs[-1]
    ring = len(pieces)
    each, width = out_ref.shape[0] // ring, out_ref.shape[2]
    for t, piece in enumerate(pieces):
        first = lax.rem(at[0] + t, ring) * each
        values = piece[...].astype(F32)
        for j in range(each):
            out_ref[first + j] = values[:, j * width : (j + 1) * width].astype(BF)


def by_columns(at, pieces, parts):
    slots, width = pieces[0].shape
    return pl.pallas_call(
        columns_kernel,
        out_shape=jax.ShapeDtypeStruct((parts, slots, width * len(pieces) // parts), BF),
        in_specs=[whole(pltpu.SMEM)] + [whole()] * len(pieces),
        out_specs=whole(),
        compiler_params=params(),
        name="by_columns",
    )(at, *pieces)


def combine_kernel(back_ref, mix_ref, hidden_ref, out_ref):
    back = back_ref[...].astype(F32).reshape(-1, back_ref.shape[2])
    routed = jnp.dot(mix_ref[...], back, preferred_element_type=F32, precision=lax.Precision.HIGHEST)
    out_ref[...] = (hidden_ref[...].astype(F32) + routed).astype(BF)


def combine(back, mix, hidden):
    return pl.pallas_call(
        combine_kernel,
        out_shape=jax.ShapeDtypeStruct(hidden.shape, BF),
        in_specs=[whole()] * 3,
        out_specs=whole(),
        compiler_params=params(),
        name="combine",
    )(back, mix, hidden)


def exchange(x, axes):
    return lax.all_to_all(x, axes, split_axis=0, concat_axis=0, tiled=True)


def gather_over_head(x):
    near = ring_gather(x, HEAD[0], 1)
    layout = [len(p) if isinstance(p, tuple) else 1 for p in near]
    near = flat(near)
    far = [shifted(p, HEAD[1], 1) for p in near]
    return tuple(layout * 2), near + far


def per_device(
    queries,
    resident_cache,
    resident_len,
    new_cache,
    new_len,
    new_owner,
    value_up,
    w_output,
    residual,
    expert_ids,
    expert_gates,
    norm_gain,
    w_gate,
    w_up,
    w_down,
):
    n_expert = lax.axis_size(EXPERT)
    n_head = lax.axis_size(HEAD)
    n_z, n_y = lax.axis_size(EXPERT[0]), lax.axis_size(COLUMN)
    z, y = lax.axis_index(EXPERT[0]), lax.axis_index(COLUMN)
    me = lax.axis_index(EXPERT)
    head = lax.axis_index(HEAD)
    req_count = resident_cache.shape[0]
    new_count = new_cache.shape[0]
    rows_dev = req_count + new_count
    rows_all = rows_dev * n_expert
    block_rows = rows_all // n_head
    columns = residual.shape[1]
    news = new_owner.shape[0]

    x, core = lax.axis_index(HEAD[0]), lax.axis_index(HEAD[1])
    ring = lax.axis_size(HEAD[0])
    number = jnp.arange(news, dtype=I32)
    equal = (new_owner[:, None] == new_owner[None, :]) & (number[None, :] < number[:, None])
    place = jnp.sum(equal.astype(I32), axis=1)
    mine = jnp.arange(new_count, dtype=I32)
    taken = (new_owner == me)[None, :] & (place[None, :] == mine[:, None])
    sources = jnp.sum(jnp.where(taken, (number // new_count)[None, :], 0), axis=1)[::MOST]
    lens = jnp.sum(jnp.where(taken, new_len[None, :], 0), axis=1)
    at = jnp.stack([x, core, y % 2]).astype(I32)

    packed = pack_cache(new_owner, new_cache, new_cache.shape[1] // ring, n_expert)
    resident = attend(queries[:req_count], jnp.swapaxes(resident_cache, 1, 2), resident_len, value_up)

    packed, w_d = lax.optimization_barrier((packed, w_down.reshape(w_down.shape[1:])))
    part = w_d.shape[1] // ring
    downs = [lax.dynamic_slice_in_dim(w_d, ((x + d) % ring) * part, part, 1) for d in range(ring)]
    for d in (1, 3):
        downs[d] = shifted(downs[d], HEAD[0], d)
    arrived, resident, downs = lax.optimization_barrier((exchange(packed, EXPERT), resident, downs))
    ours = select_arrived(sources, arrived)
    near = [ours] + [shifted(ours, HEAD[0], d) for d in range(1, ring)]
    pieces = near + [shifted(p, HEAD[1], 1) for p in near]
    (attention,) = new_attention(lens, at, queries, value_up, resident, pieces, 1)

    along_y = [attention] + [across(attention, COLUMN, d) for d in range(1, n_y)]
    rows_here = flat(ring_gather(stacked(along_y), EXPERT[0], 0))
    downs[2] = shifted(downs[2], HEAD[0], 2)
    block = lambda a: lax.dynamic_slice_in_dim(a, head * block_rows, block_rows)
    planned = plan(block(expert_ids), block(expert_gates), rows_dev, n_expert)
    downs, rows_here, (sel, mix), kept = lax.optimization_barrier((downs, rows_here, planned, block(residual)))
    away = jnp.arange(n_expert, dtype=I32)
    maker_z = (z + n_z - away // n_y) % n_z
    maker_y = y ^ (away % n_y)
    mixed = project(maker_z * n_y + maker_y, w_output.T, rows_here, rows_dev)
    parts = exchange(mixed.reshape(n_head, block_rows, columns), HEAD)
    hidden, outgoing = dispatch(parts, kept, sel, n_expert)
    received = exchange(outgoing, EXPERT)
    normed = normed_rows(received, norm_gain.reshape(1, -1))
    layout, pieces = gather_over_head(normed)
    act = run_units(layout, pieces, w_gate.reshape(w_gate.shape[1:]), w_up.reshape(w_up.shape[1:]))
    acts = [act] + [shifted(act, HEAD[0], d) for d in range(1, ring)]
    kept, sent = run_down(acts, downs)
    made = pair_sum(kept, shifted(sent, HEAD[1], 1))
    made = list(made[:1]) + [shifted(made[t], HEAD[0], -t) for t in range(1, ring)]
    back = exchange(by_columns(at, made, n_expert), EXPERT)
    return combine(back, mix, hidden)


def solution(mesh):
    finer = Mesh(mesh.devices.reshape(4, 2, 8, 2, 2), HEAD + EXPERT)
    in_specs = (
        P(EXPERT, HEAD, None),
        P(EXPERT, None, None),
        P(EXPERT),
        P(EXPERT, None, None),
        P(),
        P(),
        P(HEAD, None, None),
        P(HEAD, EXPERT),
        P(None, EXPERT),
        P(),
        P(),
        P(),
        P(EXPERT, None, HEAD),
        P(EXPERT, None, HEAD),
        P(EXPERT, HEAD, None),
    )
    out_specs = P(HEAD, EXPERT)
    return jax.shard_map(
        per_device, mesh=finer, in_specs=in_specs, out_specs=out_specs, check_vma=False
    )
```

```python
import functools

import jax
import jax.numpy as jnp
from jax import lax
from jax.experimental import pallas as pl
from jax.experimental.pallas import tpu as pltpu
from jax.sharding import Mesh
from jax.sharding import PartitionSpec as P

ROPE = 64
NOPE = 128
EXPERT = ("expert_0", "expert_1", "expert_2")
COLUMN = EXPERT[1:]
HEAD = ("head_0", "head_1")
MOST = 2
CAP = 6
BF = jnp.bfloat16
F32 = jnp.float32
I32 = jnp.int32
VMEM_BYTES = 24 * 1024 * 1024


def params():
    return pltpu.CompilerParams(vmem_limit_bytes=VMEM_BYTES)


def whole(memory=pltpu.VMEM):
    return pl.BlockSpec(memory_space=memory)


def shifted(x, axis, step):
    n = lax.axis_size(axis)
    return lax.ppermute(x, axis, [(i, (i + step) % n) for i in range(n)])


def across(x, axis, mask):
    return lax.ppermute(x, axis, [(i, i ^ mask) for i in range(lax.axis_size(axis))])


def ring_gather(x, axis, dim, beside=None):
    n = lax.axis_size(axis)
    far = n // 2
    cut = x.shape[dim] // 2
    found = {0: x}
    right, left = x, x
    for step in range(1, far):
        right, left = shifted(right, axis, 1), shifted(left, axis, -1)
        if step == 2:
            left, beside = lax.optimization_barrier((left, beside))
        found[step], found[n - step] = right, left
    low = lax.slice_in_dim(right, 0, cut, axis=dim)
    high = lax.slice_in_dim(left, cut, x.shape[dim], axis=dim)
    found[far] = (shifted(low, axis, 1), shifted(high, axis, -1))
    pieces = [found[d] for d in range(n)]
    return pieces if beside is None else (pieces, beside)


def flat(pieces):
    out = []
    for piece in pieces:
        out.extend(piece if isinstance(piece, tuple) else (piece,))
    return out


def attend(queries, caches_t, length, value_up):
    inverse_root = (NOPE + ROPE) ** (-0.5)
    latent_width = value_up.shape[1]
    scores = jnp.einsum("rhc,rct->rht", queries, caches_t, preferred_element_type=F32) * inverse_root
    inside = lax.broadcasted_iota(I32, scores.shape, 2) < length[:, None, None]
    scores = jnp.where(inside, scores, -jnp.inf)
    highest = jnp.max(scores, axis=2, keepdims=True)
    raised = jnp.exp(scores - highest)
    weights = (raised / jnp.sum(raised, axis=2, keepdims=True)).astype(BF)
    latent = jnp.einsum("rht,rct->rhc", weights, caches_t[:, :latent_width], preferred_element_type=F32).astype(BF)
    return jnp.einsum("rhc,hcv->hrv", latent, value_up, preferred_element_type=F32).astype(BF)


def pack_kernel(owners, cache_ref, out_ref, sems):
    count, span = cache_ref.shape[0], out_ref.shape[1]
    place, core = lax.axis_index(HEAD[0]), lax.axis_index(HEAD[1])
    base = lax.axis_index(EXPERT) * count
    first = pl.multiple_of(place * span, span)
    owner = [owners[base + i] for i in range(count)]
    turn = []
    for i in range(count):
        earlier = jnp.int32(0)
        for j in range(i):
            earlier = earlier + (owner[j] == owner[i]).astype(I32)
        turn.append(earlier)

    def copy(i):
        return pltpu.make_async_copy(
            cache_ref.at[i, pl.ds(first, span)], out_ref.at[owner[i]], sems.at[i]
        )

    for i in range(count):

        @pl.when(turn[i] == core)
        def _():
            copy(i).start()

    for i in range(count):

        @pl.when(turn[i] == core)
        def _():
            copy(i).wait()


def pack_cache(owners, cache, span, n_expert):
    return pl.pallas_call(
        pack_kernel,
        out_shape=jax.ShapeDtypeStruct((n_expert, span, cache.shape[2]), cache.dtype),
        in_specs=[whole(pltpu.SMEM), whole(pl.ANY)],
        out_specs=whole(pl.ANY),
        scratch_shapes=[pltpu.SemaphoreType.DMA((cache.shape[0],))],
        compiler_params=params(),
        name="pack_cache",
    )(owners, cache)


def select_kernel(sources, arrived_ref, out_ref, sems):
    copies = [
        pltpu.make_async_copy(arrived_ref.at[sources[k]], out_ref.at[k], sems.at[k])
        for k in range(out_ref.shape[0])
    ]
    for copy in copies:
        copy.start()
    for copy in copies:
        copy.wait()


def select_arrived(sources, arrived):
    count = sources.shape[0]
    return pl.pallas_call(
        select_kernel,
        out_shape=jax.ShapeDtypeStruct((count,) + arrived.shape[1:], arrived.dtype),
        in_specs=[whole(pltpu.SMEM), whole(pl.ANY)],
        out_specs=whole(pl.ANY),
        scratch_shapes=[pltpu.SemaphoreType.DMA((count,))],
        compiler_params=params(),
        name="select_arrived",
    )(sources, arrived)


def new_attention_kernel(groups, lens, at, q_ref, up_ref, res_ref, *refs):
    pieces, out_refs, latents = refs[: -groups - 1], refs[-groups - 1 : -1], refs[-1]
    ring = len(pieces) // 2
    pairs, span = pieces[0].shape[0], pieces[0].shape[1]
    old = res_ref.shape[1]
    count = pairs * MOST
    heads, latent_width, value_width = up_ref.shape
    inverse_root = (NOPE + ROPE) ** (-0.5)
    place, core, row = at[0], at[1], at[2]
    column = lax.broadcasted_iota(I32, (heads, ring * span), 1)
    position = ((place + ring - column // span) % ring) * span + column % span
    for i in range(count):
        k, turn = i // MOST, i % MOST
        ours = core == turn
        cache = jnp.concatenate(
            [jnp.where(ours, pieces[d][k], pieces[ring + d][k]) for d in range(ring)], axis=0
        )
        scores = (
            lax.dot_general(q_ref[old + i], cache, (((1,), (1,)), ((), ())), preferred_element_type=F32)
            * inverse_root
        )
        scores = jnp.where(position < lens[i], scores, -jnp.inf)
        raised = jnp.exp(scores - jnp.max(scores, axis=1, keepdims=True))
        weights = (raised / jnp.sum(raised, axis=1, keepdims=True)).astype(BF)
        latents[:, i, :] = jnp.dot(weights, cache[:, :latent_width], preferred_element_type=F32)
    each = heads // groups
    for d, out_ref in enumerate(out_refs):
        for k in range(each):
            h = k if groups == 1 else lax.rem(row + d, groups) * each + k
            values = jnp.dot(latents[h].astype(BF), up_ref[h], preferred_element_type=F32)
            rows = jnp.concatenate([res_ref[h].astype(F32), values[:count]], axis=0).astype(BF)
            out_ref[:, k * value_width : (k + 1) * value_width] = rows


def new_attention(lens, at, queries, value_up, resident, pieces, groups):
    heads, latent_width, value_width = value_up.shape
    rows = queries.shape[0]
    out = jax.ShapeDtypeStruct((rows, heads // groups * value_width), BF)
    return pl.pallas_call(
        functools.partial(new_attention_kernel, groups),
        out_shape=(out,) * groups,
        in_specs=[whole(pltpu.SMEM)] * 2 + [whole()] * (3 + len(pieces)),
        out_specs=(whole(),) * groups,
        scratch_shapes=[pltpu.VMEM((heads, rows, latent_width), F32)],
        compiler_params=params(),
        name="new_attention",
    )(lens, at, queries, value_up, resident, *pieces)


def stack_kernel(*refs):
    rows = refs[0].shape[0]
    for k, ref in enumerate(refs[:-1]):
        refs[-1][k * rows : (k + 1) * rows, :] = ref[...]


def stacked(pieces):
    rows, width = pieces[0].shape
    return pl.pallas_call(
        stack_kernel,
        out_shape=jax.ShapeDtypeStruct((rows * len(pieces), width), pieces[0].dtype),
        in_specs=[whole()] * len(pieces),
        out_specs=whole(),
        compiler_params=params(),
        name="stack",
    )(*pieces)


def project_kernel(makers, w_ref, *refs):
    pieces, out_ref = refs[:-1], refs[-1]
    rows = out_ref.shape[1]
    attention = jnp.concatenate([piece[...] for piece in pieces], axis=0)
    mixed = lax.dot_general(attention, w_ref[...], (((1,), (1,)), ((), ())), preferred_element_type=F32).astype(BF)
    for k in range(out_ref.shape[0]):
        out_ref[makers[k]] = mixed[k * rows : (k + 1) * rows]


def project(makers, w_output_t, pieces, rows):
    return pl.pallas_call(
        project_kernel,
        out_shape=jax.ShapeDtypeStruct((makers.shape[0], rows, w_output_t.shape[0]), BF),
        in_specs=[whole(pltpu.SMEM)] + [whole()] * (1 + len(pieces)),
        out_specs=whole(),
        compiler_params=params(),
        name="project",
    )(makers, w_output_t, *pieces)


def pair_kernel(a_ref, b_ref, *outs):
    for d, out in enumerate(outs):
        out[...] = (a_ref[d].astype(F32) + b_ref[d].astype(F32)).astype(out.dtype)


def pair_sum(a, b):
    out = jax.ShapeDtypeStruct(a.shape[1:], BF)
    return pl.pallas_call(
        pair_kernel,
        out_shape=(out,) * a.shape[0],
        in_specs=[whole()] * 2,
        out_specs=(whole(),) * a.shape[0],
        compiler_params=params(),
        name="pair_sum",
    )(a, b)


def plan_kernel(rows_dev, ids_ref, gates_ref, sel_ref, mix_ref):
    rows, choose = ids_ref.shape
    slots_all = sel_ref.shape[1]
    slots = rows // rows_dev * CAP
    experts = slots_all // slots
    expert = lax.broadcasted_iota(I32, (rows, experts), 1)
    member = jnp.zeros((rows, experts), F32)
    gate = jnp.zeros((rows, experts), F32)
    for k in range(choose):
        same = ids_ref[:, k : k + 1] == expert
        member = jnp.where(same, 1.0, member)
        gate = jnp.where(same, gates_ref[:, k : k + 1], gate)
    to_row = lax.broadcasted_iota(I32, (rows, rows), 0)
    from_row = lax.broadcasted_iota(I32, (rows, rows), 1)
    before = (from_row < to_row) & (from_row // rows_dev == to_row // rows_dev)
    rank = jnp.dot(before.astype(F32).astype(BF), member.astype(BF), preferred_element_type=F32)
    block = lax.broadcasted_iota(I32, (rows, experts), 0) // rows_dev
    slot = jnp.where(member > 0, rank + (block * CAP).astype(F32), -1.0)
    spread = (
        lax.broadcasted_iota(I32, (experts, slots_all), 0)
        == lax.broadcasted_iota(I32, (experts, slots_all), 1) // slots
    ).astype(F32)
    slot_wide = jnp.dot(slot.astype(BF), spread.astype(BF), preferred_element_type=F32)
    gate_wide = jnp.dot(gate, spread, preferred_element_type=F32, precision=lax.Precision.HIGHEST)
    wanted = (lax.broadcasted_iota(I32, (rows, slots_all), 1) % slots).astype(F32)
    hit = slot_wide == wanted
    sel_ref[...] = jnp.where(hit, 1.0, 0.0).astype(BF)
    mix_ref[...] = jnp.where(hit, gate_wide, 0.0)


def plan(ids, gates, rows_dev, experts):
    rows = ids.shape[0]
    slots_all = experts * (rows // rows_dev) * CAP
    return pl.pallas_call(
        functools.partial(plan_kernel, rows_dev),
        out_shape=(
            jax.ShapeDtypeStruct((rows, slots_all), BF),
            jax.ShapeDtypeStruct((rows, slots_all), F32),
        ),
        in_specs=[whole()] * 2,
        out_specs=(whole(), whole()),
        compiler_params=params(),
        name="plan",
    )(ids, gates)


def dispatch_kernel(parts_ref, residual_ref, sel_ref, hidden_ref, out_ref):
    total = parts_ref[0].astype(F32)
    for k in range(1, parts_ref.shape[0]):
        total = total + parts_ref[k].astype(F32)
    hidden = (residual_ref[...].astype(F32) + total).astype(BF)
    hidden_ref[...] = hidden
    picked = lax.dot_general(sel_ref[...], hidden, (((0,), (0,)), ((), ())), preferred_element_type=F32)
    out_ref[...] = picked.reshape(out_ref.shape).astype(BF)


def dispatch(parts, residual, sel, experts):
    rows, columns = residual.shape
    return pl.pallas_call(
        dispatch_kernel,
        out_shape=(
            jax.ShapeDtypeStruct((rows, columns), BF),
            jax.ShapeDtypeStruct((experts, sel.shape[1] // experts, columns), BF),
        ),
        in_specs=[whole()] * 3,
        out_specs=(whole(), whole()),
        compiler_params=params(),
        name="dispatch",
    )(parts, residual, sel)


def norm_kernel(x_ref, gain_ref, out_ref):
    count = x_ref.shape[0]
    squares = 0.0
    for j in range(count):
        x = x_ref[j].astype(F32)
        squares = squares + x * x
    mean = jnp.sum(squares, axis=1, keepdims=True) / out_ref.shape[1]
    inverse = lax.rsqrt(mean + 1e-06)
    x = jnp.concatenate([x_ref[j].astype(F32) for j in range(count)], axis=1)
    out_ref[...] = (x * inverse * gain_ref[...].astype(F32)).astype(BF)


def normed_rows(x, gain):
    return pl.pallas_call(
        norm_kernel,
        out_shape=jax.ShapeDtypeStruct((x.shape[1], x.shape[0] * x.shape[2]), BF),
        in_specs=[whole()] * 2,
        out_specs=whole(),
        compiler_params=params(),
        name="norm",
    )(x, gain)


def units_kernel(layout, *refs):
    count = sum(layout)
    x_refs, (gate_ref, up_ref, act_ref) = refs[:count], refs[count:]
    blocks, at = [], 0
    for parts in layout:
        blocks.append(jnp.concatenate([x_refs[at + p][...] for p in range(parts)], axis=1))
        at += parts
    x = jnp.concatenate(blocks, axis=0)
    gate = jnp.dot(x, gate_ref[...], preferred_element_type=F32)
    up = jnp.dot(x, up_ref[...], preferred_element_type=F32)
    act_ref[...] = (gate * jax.nn.sigmoid(gate) * up).astype(BF)


def run_units(layout, pieces, w_gate, w_up):
    slots = pieces[0].shape[0] * len(layout)
    return pl.pallas_call(
        functools.partial(units_kernel, layout),
        out_shape=jax.ShapeDtypeStruct((slots, w_gate.shape[1]), BF),
        in_specs=[whole()] * (len(pieces) + 2),
        out_specs=whole(),
        compiler_params=params(),
        name="units",
    )(*pieces, w_gate, w_up)


def down_kernel(*refs):
    ring = len(refs) // 2 - 1
    acts, downs, outs = refs[:ring], refs[ring : 2 * ring], refs[2 * ring :]
    slots = acts[0].shape[0] // (2 * ring)
    turned = []
    for d in range(ring):
        act = acts[d][...].astype(F32)
        order = [core * ring + (t + ring - d) % ring for core in range(2) for t in range(ring)]
        turned.append(jnp.concatenate([act[k * slots : (k + 1) * slots] for k in order], axis=0).astype(BF))
    units = jnp.concatenate(turned, axis=1)
    down = jnp.concatenate([w[...] for w in downs], axis=0)
    y = jnp.dot(units, down, preferred_element_type=F32).astype(BF)
    half = ring * slots
    for k, out in enumerate(outs):
        for t in range(ring):
            at = k * half + t * slots
            out[t] = y[at : at + slots]


def run_down(acts, downs):
    ring = len(acts)
    out = jax.ShapeDtypeStruct((ring, acts[0].shape[0] // (2 * ring), downs[0].shape[1]), BF)
    return pl.pallas_call(
        down_kernel,
        out_shape=(out, out),
        in_specs=[whole()] * (2 * ring),
        out_specs=(whole(), whole()),
        compiler_params=params(),
        name="down",
    )(*acts, *downs)


def columns_kernel(at, *refs):
    pieces, out_ref = refs[:-1], refs[-1]
    ring = len(pieces)
    each, width = out_ref.shape[0] // ring, out_ref.shape[2]
    for t, piece in enumerate(pieces):
        first = lax.rem(at[0] + t, ring) * each
        values = piece[...].astype(F32)
        for j in range(each):
            out_ref[first + j] = values[:, j * width : (j + 1) * width].astype(BF)


def by_columns(at, pieces, parts):
    slots, width = pieces[0].shape
    return pl.pallas_call(
        columns_kernel,
        out_shape=jax.ShapeDtypeStruct((parts, slots, width * len(pieces) // parts), BF),
        in_specs=[whole(pltpu.SMEM)] + [whole()] * len(pieces),
        out_specs=whole(),
        compiler_params=params(),
        name="by_columns",
    )(at, *pieces)


def combine_kernel(back_ref, mix_ref, hidden_ref, out_ref):
    back = back_ref[...].astype(F32).reshape(-1, back_ref.shape[2])
    routed = jnp.dot(mix_ref[...], back, preferred_element_type=F32, precision=lax.Precision.HIGHEST)
    out_ref[...] = (hidden_ref[...].astype(F32) + routed).astype(BF)


def combine(back, mix, hidden):
    return pl.pallas_call(
        combine_kernel,
        out_shape=jax.ShapeDtypeStruct(hidden.shape, BF),
        in_specs=[whole()] * 3,
        out_specs=whole(),
        compiler_params=params(),
        name="combine",
    )(back, mix, hidden)


def exchange(x, axes):
    return lax.all_to_all(x, axes, split_axis=0, concat_axis=0, tiled=True)


def gather_over_head(x):
    near = ring_gather(x, HEAD[0], 1)
    layout = [len(p) if isinstance(p, tuple) else 1 for p in near]
    near = flat(near)
    far = [shifted(p, HEAD[1], 1) for p in near]
    return tuple(layout * 2), near + far


def per_device(
    queries,
    resident_cache,
    resident_len,
    new_cache,
    new_len,
    new_owner,
    value_up,
    w_output,
    residual,
    expert_ids,
    expert_gates,
    norm_gain,
    w_gate,
    w_up,
    w_down,
):
    n_expert = lax.axis_size(EXPERT)
    n_head = lax.axis_size(HEAD)
    n_z, n_y = lax.axis_size(EXPERT[0]), lax.axis_size(COLUMN)
    z, y = lax.axis_index(EXPERT[0]), lax.axis_index(COLUMN)
    me = lax.axis_index(EXPERT)
    head = lax.axis_index(HEAD)
    req_count = resident_cache.shape[0]
    new_count = new_cache.shape[0]
    rows_dev = req_count + new_count
    rows_all = rows_dev * n_expert
    block_rows = rows_all // n_head
    columns = residual.shape[1]
    news = new_owner.shape[0]

    x, core = lax.axis_index(HEAD[0]), lax.axis_index(HEAD[1])
    ring = lax.axis_size(HEAD[0])
    number = jnp.arange(news, dtype=I32)
    equal = (new_owner[:, None] == new_owner[None, :]) & (number[None, :] < number[:, None])
    place = jnp.sum(equal.astype(I32), axis=1)
    mine = jnp.arange(new_count, dtype=I32)
    taken = (new_owner == me)[None, :] & (place[None, :] == mine[:, None])
    sources = jnp.sum(jnp.where(taken, (number // new_count)[None, :], 0), axis=1)[::MOST]
    lens = jnp.sum(jnp.where(taken, new_len[None, :], 0), axis=1)
    at = jnp.stack([x, core, y % 2]).astype(I32)

    packed = pack_cache(new_owner, new_cache, new_cache.shape[1] // ring, n_expert)
    resident = attend(queries[:req_count], jnp.swapaxes(resident_cache, 1, 2), resident_len, value_up)

    packed, w_d = lax.optimization_barrier((packed, w_down.reshape(w_down.shape[1:])))
    part = w_d.shape[1] // ring
    downs = [lax.dynamic_slice_in_dim(w_d, ((x + d) % ring) * part, part, 1) for d in range(ring)]
    for d in (1, 3):
        downs[d] = shifted(downs[d], HEAD[0], d)
    arrived, resident, downs = lax.optimization_barrier((exchange(packed, EXPERT), resident, downs))
    ours = select_arrived(sources, arrived)
    near = [ours] + [shifted(ours, HEAD[0], d) for d in range(1, ring)]
    pieces = near + [shifted(p, HEAD[1], 1) for p in near]
    (attention,) = new_attention(lens, at, queries, value_up, resident, pieces, 1)

    along_y = [attention] + [across(attention, COLUMN, d) for d in range(1, n_y)]
    block = lambda a: lax.dynamic_slice_in_dim(a, head * block_rows, block_rows)
    planned = plan(block(expert_ids), block(expert_gates), rows_dev, n_expert)
    rows_here, ((sel, mix), kept) = ring_gather(stacked(along_y), EXPERT[0], 0, (planned, block(residual)))
    rows_here = flat(rows_here)
    downs[2] = shifted(downs[2], HEAD[0], 2)
    downs, rows_here = lax.optimization_barrier((downs, rows_here))
    away = jnp.arange(n_expert, dtype=I32)
    maker_z = (z + n_z - away // n_y) % n_z
    maker_y = y ^ (away % n_y)
    mixed = project(maker_z * n_y + maker_y, w_output.T, rows_here, rows_dev)
    parts = exchange(mixed.reshape(n_head, block_rows, columns), HEAD)
    hidden, outgoing = dispatch(parts, kept, sel, n_expert)
    received = exchange(outgoing, EXPERT)
    normed = normed_rows(received, norm_gain.reshape(1, -1))
    layout, pieces = gather_over_head(normed)
    act = run_units(layout, pieces, w_gate.reshape(w_gate.shape[1:]), w_up.reshape(w_up.shape[1:]))
    acts = [act] + [shifted(act, HEAD[0], d) for d in range(1, ring)]
    kept, sent = run_down(acts, downs)
    made = pair_sum(kept, shifted(sent, HEAD[1], 1))
    made = list(made[:1]) + [shifted(made[t], HEAD[0], -t) for t in range(1, ring)]
    back = exchange(by_columns(at, made, n_expert), EXPERT)
    return combine(back, mix, hidden)


def solution(mesh):
    finer = Mesh(mesh.devices.reshape(4, 2, 8, 2, 2), HEAD + EXPERT)
    in_specs = (
        P(EXPERT, HEAD, None),
        P(EXPERT, None, None),
        P(EXPERT),
        P(EXPERT, None, None),
        P(),
        P(),
        P(HEAD, None, None),
        P(HEAD, EXPERT),
        P(None, EXPERT),
        P(),
        P(),
        P(),
        P(EXPERT, None, HEAD),
        P(EXPERT, None, HEAD),
        P(EXPERT, HEAD, None),
    )
    out_specs = P(HEAD, EXPERT)
    return jax.shard_map(
        per_device, mesh=finer, in_specs=in_specs, out_specs=out_specs, check_vma=False
    )
```

```python
import functools

import jax
import jax.numpy as jnp
from jax import lax
from jax.experimental import pallas as pl
from jax.experimental.pallas import tpu as pltpu
from jax.sharding import Mesh
from jax.sharding import PartitionSpec as P

ROPE = 64
NOPE = 128
EXPERT = ("expert_0", "expert_1", "expert_2")
COLUMN = EXPERT[1:]
HEAD = ("head_0", "head_1")
MOST = 2
CAP = 6
BF = jnp.bfloat16
F32 = jnp.float32
I32 = jnp.int32
VMEM_BYTES = 24 * 1024 * 1024


def params():
    return pltpu.CompilerParams(vmem_limit_bytes=VMEM_BYTES)


def whole(memory=pltpu.VMEM):
    return pl.BlockSpec(memory_space=memory)


def shifted(x, axis, step):
    n = lax.axis_size(axis)
    return lax.ppermute(x, axis, [(i, (i + step) % n) for i in range(n)])


def across(x, axis, mask):
    return lax.ppermute(x, axis, [(i, i ^ mask) for i in range(lax.axis_size(axis))])


def ring_gather(x, axis, dim, beside=None):
    n = lax.axis_size(axis)
    far = n // 2
    cut = x.shape[dim] // 2
    found = {0: x}
    right, left = x, x
    for step in range(1, far):
        right, left = shifted(right, axis, 1), shifted(left, axis, -1)
        if step == 2:
            left, beside = lax.optimization_barrier((left, beside))
        found[step], found[n - step] = right, left
    low = lax.slice_in_dim(right, 0, cut, axis=dim)
    high = lax.slice_in_dim(left, cut, x.shape[dim], axis=dim)
    found[far] = (shifted(low, axis, 1), shifted(high, axis, -1))
    pieces = [found[d] for d in range(n)]
    return pieces if beside is None else (pieces, beside)


def flat(pieces):
    out = []
    for piece in pieces:
        out.extend(piece if isinstance(piece, tuple) else (piece,))
    return out


def attend(queries, caches_t, length, value_up):
    inverse_root = (NOPE + ROPE) ** (-0.5)
    latent_width = value_up.shape[1]
    scores = jnp.einsum("rhc,rct->rht", queries, caches_t, preferred_element_type=F32) * inverse_root
    inside = lax.broadcasted_iota(I32, scores.shape, 2) < length[:, None, None]
    scores = jnp.where(inside, scores, -jnp.inf)
    highest = jnp.max(scores, axis=2, keepdims=True)
    raised = jnp.exp(scores - highest)
    weights = (raised / jnp.sum(raised, axis=2, keepdims=True)).astype(BF)
    latent = jnp.einsum("rht,rct->rhc", weights, caches_t[:, :latent_width], preferred_element_type=F32).astype(BF)
    return jnp.einsum("rhc,hcv->hrv", latent, value_up, preferred_element_type=F32).astype(BF)


def pack_kernel(owners, cache_ref, out_ref, sems):
    count, span = cache_ref.shape[0], out_ref.shape[1]
    place, core = lax.axis_index(HEAD[0]), lax.axis_index(HEAD[1])
    base = lax.axis_index(EXPERT) * count
    first = pl.multiple_of(place * span, span)
    owner = [owners[base + i] for i in range(count)]
    turn = []
    for i in range(count):
        earlier = jnp.int32(0)
        for j in range(i):
            earlier = earlier + (owner[j] == owner[i]).astype(I32)
        turn.append(earlier)

    def copy(i):
        return pltpu.make_async_copy(
            cache_ref.at[i, pl.ds(first, span)], out_ref.at[owner[i]], sems.at[i]
        )

    for i in range(count):

        @pl.when(turn[i] == core)
        def _():
            copy(i).start()

    for i in range(count):

        @pl.when(turn[i] == core)
        def _():
            copy(i).wait()


def pack_cache(owners, cache, span, n_expert):
    return pl.pallas_call(
        pack_kernel,
        out_shape=jax.ShapeDtypeStruct((n_expert, span, cache.shape[2]), cache.dtype),
        in_specs=[whole(pltpu.SMEM), whole(pl.ANY)],
        out_specs=whole(pl.ANY),
        scratch_shapes=[pltpu.SemaphoreType.DMA((cache.shape[0],))],
        compiler_params=params(),
        name="pack_cache",
    )(owners, cache)


def select_kernel(sources, arrived_ref, out_ref, sems):
    copies = [
        pltpu.make_async_copy(arrived_ref.at[sources[k]], out_ref.at[k], sems.at[k])
        for k in range(out_ref.shape[0])
    ]
    for copy in copies:
        copy.start()
    for copy in copies:
        copy.wait()


def select_arrived(sources, arrived):
    count = sources.shape[0]
    return pl.pallas_call(
        select_kernel,
        out_shape=jax.ShapeDtypeStruct((count,) + arrived.shape[1:], arrived.dtype),
        in_specs=[whole(pltpu.SMEM), whole(pl.ANY)],
        out_specs=whole(pl.ANY),
        scratch_shapes=[pltpu.SemaphoreType.DMA((count,))],
        compiler_params=params(),
        name="select_arrived",
    )(sources, arrived)


def new_attention_kernel(groups, lens, at, q_ref, up_ref, res_ref, *refs):
    pieces, out_refs, latents = refs[: -groups - 1], refs[-groups - 1 : -1], refs[-1]
    ring = len(pieces) // 2
    pairs, span = pieces[0].shape[0], pieces[0].shape[1]
    old = res_ref.shape[1]
    count = pairs * MOST
    heads, latent_width, value_width = up_ref.shape
    inverse_root = (NOPE + ROPE) ** (-0.5)
    place, core, row = at[0], at[1], at[2]
    column = lax.broadcasted_iota(I32, (heads, ring * span), 1)
    position = ((place + ring - column // span) % ring) * span + column % span

    def cache(i):
        k, ours = i // MOST, core == i % MOST
        return jnp.concatenate([jnp.where(ours, pieces[d][k], pieces[ring + d][k]) for d in range(ring)], axis=0)

    rows = []
    for i in range(count):
        scores = lax.dot_general(
            q_ref[old + i], cache(i), (((1,), (1,)), ((), ())), preferred_element_type=F32
        )
        rows.append(jnp.where(position < lens[i], scores * inverse_root, -jnp.inf))
    scores = jnp.concatenate(rows, axis=0)
    raised = jnp.exp(scores - jnp.max(scores, axis=1, keepdims=True))
    weights = (raised / jnp.sum(raised, axis=1, keepdims=True)).astype(BF)
    for i in range(count):
        latents[:, i, :] = jnp.dot(
            weights[i * heads : (i + 1) * heads], cache(i)[:, :latent_width], preferred_element_type=F32
        )
    each = heads // groups
    for d, out_ref in enumerate(out_refs):
        for k in range(each):
            h = k if groups == 1 else lax.rem(row + d, groups) * each + k
            values = jnp.dot(latents[h].astype(BF), up_ref[h], preferred_element_type=F32)
            rows = jnp.concatenate([res_ref[h].astype(F32), values[:count]], axis=0).astype(BF)
            out_ref[:, k * value_width : (k + 1) * value_width] = rows


def new_attention(lens, at, queries, value_up, resident, pieces, groups):
    heads, latent_width, value_width = value_up.shape
    rows = queries.shape[0]
    out = jax.ShapeDtypeStruct((rows, heads // groups * value_width), BF)
    return pl.pallas_call(
        functools.partial(new_attention_kernel, groups),
        out_shape=(out,) * groups,
        in_specs=[whole(pltpu.SMEM)] * 2 + [whole()] * (3 + len(pieces)),
        out_specs=(whole(),) * groups,
        scratch_shapes=[pltpu.VMEM((heads, rows, latent_width), F32)],
        compiler_params=params(),
        name="new_attention",
    )(lens, at, queries, value_up, resident, *pieces)


def stack_kernel(*refs):
    rows = refs[0].shape[0]
    for k, ref in enumerate(refs[:-1]):
        refs[-1][k * rows : (k + 1) * rows, :] = ref[...]


def stacked(pieces):
    rows, width = pieces[0].shape
    return pl.pallas_call(
        stack_kernel,
        out_shape=jax.ShapeDtypeStruct((rows * len(pieces), width), pieces[0].dtype),
        in_specs=[whole()] * len(pieces),
        out_specs=whole(),
        compiler_params=params(),
        name="stack",
    )(*pieces)


def project_kernel(makers, w_ref, *refs):
    pieces, out_ref = refs[:-1], refs[-1]
    rows = out_ref.shape[1]
    attention = jnp.concatenate([piece[...] for piece in pieces], axis=0)
    mixed = lax.dot_general(attention, w_ref[...], (((1,), (1,)), ((), ())), preferred_element_type=F32).astype(BF)
    for k in range(out_ref.shape[0]):
        out_ref[makers[k]] = mixed[k * rows : (k + 1) * rows]


def project(makers, w_output_t, pieces, rows):
    return pl.pallas_call(
        project_kernel,
        out_shape=jax.ShapeDtypeStruct((makers.shape[0], rows, w_output_t.shape[0]), BF),
        in_specs=[whole(pltpu.SMEM)] + [whole()] * (1 + len(pieces)),
        out_specs=whole(),
        compiler_params=params(),
        name="project",
    )(makers, w_output_t, *pieces)


def pair_kernel(a_ref, b_ref, *outs):
    for d, out in enumerate(outs):
        out[...] = (a_ref[d].astype(F32) + b_ref[d].astype(F32)).astype(out.dtype)


def pair_sum(a, b):
    out = jax.ShapeDtypeStruct(a.shape[1:], BF)
    return pl.pallas_call(
        pair_kernel,
        out_shape=(out,) * a.shape[0],
        in_specs=[whole()] * 2,
        out_specs=(whole(),) * a.shape[0],
        compiler_params=params(),
        name="pair_sum",
    )(a, b)


def plan_kernel(rows_dev, ids_ref, gates_ref, sel_ref, mix_ref):
    rows, choose = ids_ref.shape
    slots_all = sel_ref.shape[1]
    slots = rows // rows_dev * CAP
    experts = slots_all // slots
    expert = lax.broadcasted_iota(I32, (rows, experts), 1)
    member = jnp.zeros((rows, experts), F32)
    gate = jnp.zeros((rows, experts), F32)
    for k in range(choose):
        same = ids_ref[:, k : k + 1] == expert
        member = jnp.where(same, 1.0, member)
        gate = jnp.where(same, gates_ref[:, k : k + 1], gate)
    to_row = lax.broadcasted_iota(I32, (rows, rows), 0)
    from_row = lax.broadcasted_iota(I32, (rows, rows), 1)
    before = (from_row < to_row) & (from_row // rows_dev == to_row // rows_dev)
    rank = jnp.dot(before.astype(F32).astype(BF), member.astype(BF), preferred_element_type=F32)
    block = lax.broadcasted_iota(I32, (rows, experts), 0) // rows_dev
    slot = jnp.where(member > 0, rank + (block * CAP).astype(F32), -1.0)
    spread = (
        lax.broadcasted_iota(I32, (experts, slots_all), 0)
        == lax.broadcasted_iota(I32, (experts, slots_all), 1) // slots
    ).astype(F32)
    slot_wide = jnp.dot(slot.astype(BF), spread.astype(BF), preferred_element_type=F32)
    gate_wide = jnp.dot(gate, spread, preferred_element_type=F32, precision=lax.Precision.HIGHEST)
    wanted = (lax.broadcasted_iota(I32, (rows, slots_all), 1) % slots).astype(F32)
    hit = slot_wide == wanted
    sel_ref[...] = jnp.where(hit, 1.0, 0.0).astype(BF)
    mix_ref[...] = jnp.where(hit, gate_wide, 0.0)


def plan(ids, gates, rows_dev, experts):
    rows = ids.shape[0]
    slots_all = experts * (rows // rows_dev) * CAP
    return pl.pallas_call(
        functools.partial(plan_kernel, rows_dev),
        out_shape=(
            jax.ShapeDtypeStruct((rows, slots_all), BF),
            jax.ShapeDtypeStruct((rows, slots_all), F32),
        ),
        in_specs=[whole()] * 2,
        out_specs=(whole(), whole()),
        compiler_params=params(),
        name="plan",
    )(ids, gates)


def dispatch_kernel(parts_ref, residual_ref, sel_ref, hidden_ref, out_ref):
    total = parts_ref[0].astype(F32)
    for k in range(1, parts_ref.shape[0]):
        total = total + parts_ref[k].astype(F32)
    hidden = (residual_ref[...].astype(F32) + total).astype(BF)
    hidden_ref[...] = hidden
    picked = lax.dot_general(sel_ref[...], hidden, (((0,), (0,)), ((), ())), preferred_element_type=F32)
    out_ref[...] = picked.reshape(out_ref.shape).astype(BF)


def dispatch(parts, residual, sel, experts):
    rows, columns = residual.shape
    return pl.pallas_call(
        dispatch_kernel,
        out_shape=(
            jax.ShapeDtypeStruct((rows, columns), BF),
            jax.ShapeDtypeStruct((experts, sel.shape[1] // experts, columns), BF),
        ),
        in_specs=[whole()] * 3,
        out_specs=(whole(), whole()),
        compiler_params=params(),
        name="dispatch",
    )(parts, residual, sel)


def norm_kernel(x_ref, gain_ref, out_ref):
    count = x_ref.shape[0]
    squares = 0.0
    for j in range(count):
        x = x_ref[j].astype(F32)
        squares = squares + x * x
    mean = jnp.sum(squares, axis=1, keepdims=True) / out_ref.shape[1]
    inverse = lax.rsqrt(mean + 1e-06)
    x = jnp.concatenate([x_ref[j].astype(F32) for j in range(count)], axis=1)
    out_ref[...] = (x * inverse * gain_ref[...].astype(F32)).astype(BF)


def normed_rows(x, gain):
    return pl.pallas_call(
        norm_kernel,
        out_shape=jax.ShapeDtypeStruct((x.shape[1], x.shape[0] * x.shape[2]), BF),
        in_specs=[whole()] * 2,
        out_specs=whole(),
        compiler_params=params(),
        name="norm",
    )(x, gain)


def units_kernel(layout, *refs):
    count = sum(layout)
    x_refs, (gate_ref, up_ref, act_ref) = refs[:count], refs[count:]
    blocks, at = [], 0
    for parts in layout:
        blocks.append(jnp.concatenate([x_refs[at + p][...] for p in range(parts)], axis=1))
        at += parts
    x = jnp.concatenate(blocks, axis=0)
    gate = jnp.dot(x, gate_ref[...], preferred_element_type=F32)
    up = jnp.dot(x, up_ref[...], preferred_element_type=F32)
    act_ref[...] = (gate * jax.nn.sigmoid(gate) * up).astype(BF)


def run_units(layout, pieces, w_gate, w_up):
    slots = pieces[0].shape[0] * len(layout)
    return pl.pallas_call(
        functools.partial(units_kernel, layout),
        out_shape=jax.ShapeDtypeStruct((slots, w_gate.shape[1]), BF),
        in_specs=[whole()] * (len(pieces) + 2),
        out_specs=whole(),
        compiler_params=params(),
        name="units",
    )(*pieces, w_gate, w_up)


def down_kernel(*refs):
    ring = len(refs) // 2 - 1
    acts, downs, outs = refs[:ring], refs[ring : 2 * ring], refs[2 * ring :]
    slots = acts[0].shape[0] // (2 * ring)
    turned = []
    for d in range(ring):
        act = acts[d][...].astype(F32)
        order = [core * ring + (t + ring - d) % ring for core in range(2) for t in range(ring)]
        turned.append(jnp.concatenate([act[k * slots : (k + 1) * slots] for k in order], axis=0).astype(BF))
    units = jnp.concatenate(turned, axis=1)
    down = jnp.concatenate([w[...] for w in downs], axis=0)
    y = jnp.dot(units, down, preferred_element_type=F32).astype(BF)
    half = ring * slots
    for k, out in enumerate(outs):
        for t in range(ring):
            at = k * half + t * slots
            out[t] = y[at : at + slots]


def run_down(acts, downs):
    ring = len(acts)
    out = jax.ShapeDtypeStruct((ring, acts[0].shape[0] // (2 * ring), downs[0].shape[1]), BF)
    return pl.pallas_call(
        down_kernel,
        out_shape=(out, out),
        in_specs=[whole()] * (2 * ring),
        out_specs=(whole(), whole()),
        compiler_params=params(),
        name="down",
    )(*acts, *downs)


def columns_kernel(at, *refs):
    pieces, out_ref = refs[:-1], refs[-1]
    ring = len(pieces)
    each, width = out_ref.shape[0] // ring, out_ref.shape[2]
    for t, piece in enumerate(pieces):
        first = lax.rem(at[0] + t, ring) * each
        values = piece[...].astype(F32)
        for j in range(each):
            out_ref[first + j] = values[:, j * width : (j + 1) * width].astype(BF)


def by_columns(at, pieces, parts):
    slots, width = pieces[0].shape
    return pl.pallas_call(
        columns_kernel,
        out_shape=jax.ShapeDtypeStruct((parts, slots, width * len(pieces) // parts), BF),
        in_specs=[whole(pltpu.SMEM)] + [whole()] * len(pieces),
        out_specs=whole(),
        compiler_params=params(),
        name="by_columns",
    )(at, *pieces)


def combine_kernel(back_ref, mix_ref, hidden_ref, out_ref):
    back = back_ref[...].astype(F32).reshape(-1, back_ref.shape[2])
    routed = jnp.dot(mix_ref[...], back, preferred_element_type=F32, precision=lax.Precision.HIGHEST)
    out_ref[...] = (hidden_ref[...].astype(F32) + routed).astype(BF)


def combine(back, mix, hidden):
    return pl.pallas_call(
        combine_kernel,
        out_shape=jax.ShapeDtypeStruct(hidden.shape, BF),
        in_specs=[whole()] * 3,
        out_specs=whole(),
        compiler_params=params(),
        name="combine",
    )(back, mix, hidden)


def exchange(x, axes):
    return lax.all_to_all(x, axes, split_axis=0, concat_axis=0, tiled=True)


def gather_over_head(x):
    near = ring_gather(x, HEAD[0], 1)
    layout = [len(p) if isinstance(p, tuple) else 1 for p in near]
    near = flat(near)
    far = [shifted(p, HEAD[1], 1) for p in near]
    return tuple(layout * 2), near + far


def per_device(
    queries,
    resident_cache,
    resident_len,
    new_cache,
    new_len,
    new_owner,
    value_up,
    w_output,
    residual,
    expert_ids,
    expert_gates,
    norm_gain,
    w_gate,
    w_up,
    w_down,
):
    n_expert = lax.axis_size(EXPERT)
    n_head = lax.axis_size(HEAD)
    n_z, n_y = lax.axis_size(EXPERT[0]), lax.axis_size(COLUMN)
    z, y = lax.axis_index(EXPERT[0]), lax.axis_index(COLUMN)
    me = lax.axis_index(EXPERT)
    head = lax.axis_index(HEAD)
    req_count = resident_cache.shape[0]
    new_count = new_cache.shape[0]
    rows_dev = req_count + new_count
    rows_all = rows_dev * n_expert
    block_rows = rows_all // n_head
    columns = residual.shape[1]
    news = new_owner.shape[0]

    x, core = lax.axis_index(HEAD[0]), lax.axis_index(HEAD[1])
    ring = lax.axis_size(HEAD[0])
    number = jnp.arange(news, dtype=I32)
    equal = (new_owner[:, None] == new_owner[None, :]) & (number[None, :] < number[:, None])
    place = jnp.sum(equal.astype(I32), axis=1)
    mine = jnp.arange(new_count, dtype=I32)
    taken = (new_owner == me)[None, :] & (place[None, :] == mine[:, None])
    sources = jnp.sum(jnp.where(taken, (number // new_count)[None, :], 0), axis=1)[::MOST]
    lens = jnp.sum(jnp.where(taken, new_len[None, :], 0), axis=1)
    at = jnp.stack([x, core, y % 2]).astype(I32)

    packed = pack_cache(new_owner, new_cache, new_cache.shape[1] // ring, n_expert)
    resident = attend(queries[:req_count], jnp.swapaxes(resident_cache, 1, 2), resident_len, value_up)

    packed, w_d = lax.optimization_barrier((packed, w_down.reshape(w_down.shape[1:])))
    part = w_d.shape[1] // ring
    downs = [lax.dynamic_slice_in_dim(w_d, ((x + d) % ring) * part, part, 1) for d in range(ring)]
    for d in (1, 3):
        downs[d] = shifted(downs[d], HEAD[0], d)
    arrived, resident, downs = lax.optimization_barrier((exchange(packed, EXPERT), resident, downs))
    ours = select_arrived(sources, arrived)
    near = [ours] + [shifted(ours, HEAD[0], d) for d in range(1, ring)]
    pieces = near + [shifted(p, HEAD[1], 1) for p in near]
    (attention,) = new_attention(lens, at, queries, value_up, resident, pieces, 1)

    along_y = [attention] + [across(attention, COLUMN, d) for d in range(1, n_y)]
    block = lambda a: lax.dynamic_slice_in_dim(a, head * block_rows, block_rows)
    planned = plan(block(expert_ids), block(expert_gates), rows_dev, n_expert)
    rows_here, ((sel, mix), kept) = ring_gather(stacked(along_y), EXPERT[0], 0, (planned, block(residual)))
    rows_here = flat(rows_here)
    downs[2] = shifted(downs[2], HEAD[0], 2)
    downs, rows_here = lax.optimization_barrier((downs, rows_here))
    away = jnp.arange(n_expert, dtype=I32)
    maker_z = (z + n_z - away // n_y) % n_z
    maker_y = y ^ (away % n_y)
    mixed = project(maker_z * n_y + maker_y, w_output.T, rows_here, rows_dev)
    parts = exchange(mixed.reshape(n_head, block_rows, columns), HEAD)
    hidden, outgoing = dispatch(parts, kept, sel, n_expert)
    received = exchange(outgoing, EXPERT)
    normed = normed_rows(received, norm_gain.reshape(1, -1))
    layout, pieces = gather_over_head(normed)
    act = run_units(layout, pieces, w_gate.reshape(w_gate.shape[1:]), w_up.reshape(w_up.shape[1:]))
    acts = [act] + [shifted(act, HEAD[0], d) for d in range(1, ring)]
    kept, sent = run_down(acts, downs)
    made = pair_sum(kept, shifted(sent, HEAD[1], 1))
    made = list(made[:1]) + [shifted(made[t], HEAD[0], -t) for t in range(1, ring)]
    back = exchange(by_columns(at, made, n_expert), EXPERT)
    return combine(back, mix, hidden)


def solution(mesh):
    finer = Mesh(mesh.devices.reshape(4, 2, 8, 2, 2), HEAD + EXPERT)
    in_specs = (
        P(EXPERT, HEAD, None),
        P(EXPERT, None, None),
        P(EXPERT),
        P(EXPERT, None, None),
        P(),
        P(),
        P(HEAD, None, None),
        P(HEAD, EXPERT),
        P(None, EXPERT),
        P(),
        P(),
        P(),
        P(EXPERT, None, HEAD),
        P(EXPERT, None, HEAD),
        P(EXPERT, HEAD, None),
    )
    out_specs = P(HEAD, EXPERT)
    return jax.shard_map(
        per_device, mesh=finer, in_specs=in_specs, out_specs=out_specs, check_vma=False
    )
```
